32 devices in a mesh: gx: 4 (over z), gy: 8 (over y, x, core).
Axes of the slice: x: 2, y: 2, z: 4, core: 2. Of those that a mesh axis runs over, the one named last changes fastest.
Arguments:
- tokens: bfloat16 [8, 512, 1536], P('gy', 'gx'), may hold values from -6 to 6
- first_gain: float32 [1536], replicated, may hold values from 0.5 to 1.5
- query_weight: bfloat16 [1536, 1536], P('gy', 'gx'), may hold values from -0.4375 to 0.4375
- key_matrix: bfloat16 [1536, 512], P('gy', 'gx'), may hold values from -0.4375 to 0.4375
- value_matrix: bfloat16 [1536, 512], P('gy', 'gx'), may hold values from -0.15625 to 0.15625
- out_weight: bfloat16 [1536, 1536], P('gx', 'gy'), may hold values from -2.5 to 2.5
- second_gain: float32 [1536], replicated, may hold values from 0.5 to 1.5
- gate_weight: bfloat16 [40, 1536, 512], P('gx', 'gy'), may hold values from -0.15625 to 0.15625
- up_weight: bfloat16 [40, 1536, 512], P('gx', 'gy'), may hold values from -0.15625 to 0.15625
- down_weight: bfloat16 [40, 512, 1536], P('gx', None, 'gy'), may hold values from -3 to 3
- routes: int32 [8, 512, 8], P('gy', 'gx'), may hold values from 0 to 39, all different within a row; in each aligned block of 128 rows (0 to 127, 128 to 255, ..., all dimensions but the last counted through in order) at most 48 rows name the same one
- route_logits: float32 [8, 512, 8], P('gy', 'gx'), may hold values from -1.25 to 1.25
- cotangent: bfloat16 [8, 512, 1536], P('gy', 'gx'), may hold values from -6 to 6
Outputs:
- output: bfloat16 [8, 512, 1536], P('gy', 'gx')
- tokens_grad: float32 [8, 512, 1536], P('gy', 'gx')
- first_gain_grad: float32 [1536], replicated
- query_grad: float32 [1536, 1536], P('gy', 'gx')
- key_grad: float32 [1536, 512], P('gy', 'gx')
- value_grad: float32 [1536, 512], P('gy', 'gx')
- out_weight_grad: float32 [1536, 1536], P('gx', 'gy')
- second_gain_grad: float32 [1536], replicated
- gate_grad: float32 [40, 1536, 512], P('gx', 'gy')
- up_grad: float32 [40, 1536, 512], P('gx', 'gy')
- down_grad: float32 [40, 512, 1536], P('gx', None, 'gy')
- logit_grad: float32 [8, 512, 8], P('gy', 'gx')
The draws below stay inside these ranges and needn't reach their ends.
Inputs may be any that keep to these rules, and one draw needn't show every extreme that they name: `routes`: each token names 8 different experts. In the 128 tokens of one device no expert is named by more than 48 of them, and in every draw some expert is named by exactly 48 tokens of some device.
All inputs are finite; a program needn't handle non-finite values.
Results may differ from the reference program's by a relative error of at most 0.015.
Values may be sent and summed in bfloat16 or wider, within the bound.
No kernel may reach another device: no remote copies, remote signals or barrier semaphores. Data moves between devices by JAX's collectives and lax.ppermute only.
A program may use at most 256 MiB of HBM per device.

```python
import math
import jax
import jax.numpy as jnp
import numpy as np
from jax import lax

MODEL_WIDTH = 1536
QUERY_HEAD_COUNT = 24
KEY_VALUE_HEADS = 8
HEAD_SIZE = 64
FF = 512
EXPERTS = 40
TOPK = 8
TOK_DEV = 128
SEQ = 512
SEQS = 8
CAP = 48


def level_of(own_key, dims, pieces, least, largest):
    loudness, own = 1.0, jax.random.fold_in(own_key, 6)
    for position, blocks in pieces:
        heights = jnp.exp(jax.random.uniform(jax.random.fold_in(own, position), (blocks,), jnp.float32, least / len(pieces), largest / len(pieces)))
        loudness = loudness * jnp.repeat(heights, dims[position] // blocks).reshape([-1 if axis == position else 1 for axis in range(len(dims))])
    return loudness


def assign_block(rng, own, number, rows, amount, top, most, slope):
    sequence = jax.random.permutation(rng, amount)
    crowded, common = portions_of(amount, rows * top, most, slope, True), portions_of(amount, rows * top, most, slope, False)
    places = jnp.arange(amount)

    def named(tallies, offset_by):
        used = int((tallies > 0).sum())
        fixed = max(1, used // 4)
        moved = fixed + (places - fixed + offset_by * (used - fixed)) % max(1, amount - fixed)
        return jnp.zeros((amount,), jnp.int32).at[sequence[jnp.where(places < fixed, places, moved)]].set(jnp.asarray(tallies, jnp.int32))

    tallies = jnp.where(number % 4 == 0, named(crowded, number // 4), named(common, number - number // 4 - 1))
    mixed = jax.random.permutation(jax.random.fold_in(own, 3), amount)
    donor, receiver = mixed[0:amount // 2 * 2:2], mixed[1:amount // 2 * 2:2]
    margin = jnp.minimum(tallies[donor] - 1, most - tallies[receiver]) // 2
    margin = jnp.where((donor == sequence[0]) | (receiver == sequence[0]) | (tallies[receiver] == 0), 0, jnp.maximum(margin, 0))
    moved = jax.random.randint(jax.random.fold_in(own, 4), (amount // 2,), 0, 1 << 20) % (margin + 1)
    tallies = tallies.at[donor].add(-moved).at[receiver].add(moved)
    items = jnp.searchsorted(jnp.cumsum(tallies), jnp.arange(rows * top), side="right").astype(jnp.int32)
    table = items.reshape(top, rows).T
    table = table[jax.random.permutation(jax.random.fold_in(own, 1), rows)]
    offset_by = jax.random.randint(jax.random.fold_in(own, 2), (rows, 1), 0, top)
    return jnp.take_along_axis(table, (jnp.arange(top)[None, :] + offset_by) % top, axis=1)


def portions_of(number_of, total, bound, lean, full):
    weights = [(1 << 20) // math.isqrt(standing ** lean) + 1 for standing in range(1, number_of + 1)]
    largest = bound if full else min(bound, max(-(-total // number_of), total * weights[0] // sum(weights)))
    least = 1 if total - largest >= number_of - 1 else 0
    holding, rest = [largest] + [least] * (number_of - 1), total - largest - least * (number_of - 1)
    while rest > 0:
        movable = [i for i in range(1, number_of) if holding[i] < largest] or [i for i in range(1, number_of) if holding[i] < bound]
        whole, budget = sum([weights[i] for i in movable]), rest
        for i in movable:
            extra = min(bound - holding[i], max(1, budget * weights[i] // whole), rest)
            holding[i] = holding[i] + extra
            rest = rest - extra
    return np.array(holding)


def bell_draw(own_key, extent, deviation, most, cuts=(), kind=jnp.bfloat16):
    entries = jax.random.normal(own_key, extent, jnp.float32) * deviation
    if len(cuts) > 0:
        entries = level_of(own_key, extent, cuts, -0.22, 0.18) * entries
    return jnp.clip(entries, min=-most, max=most).astype(kind)


def setup_inputs(seed: int = 0) -> dict:
    keys = jax.random.split(jax.random.key(seed), 14)
    tokens = bell_draw(keys[0], (SEQS, SEQ, MODEL_WIDTH), 1.0, 6.0, ((0, 8), (1, 4)))
    first_gain = jnp.clip(1.0 + 0.1 * jax.random.normal(keys[1], (MODEL_WIDTH,), jnp.float32), 0.5, 1.5)
    query_weight = bell_draw(keys[2], (MODEL_WIDTH, QUERY_HEAD_COUNT * HEAD_SIZE), (MODEL_WIDTH // 8) ** -0.5, 0.4375, ((0, 8), (1, 4)))
    key_matrix = bell_draw(keys[3], (MODEL_WIDTH, KEY_VALUE_HEADS * HEAD_SIZE), (MODEL_WIDTH // 8) ** -0.5, 0.4375, ((0, 8), (1, 4)))
    value_matrix = bell_draw(keys[4], (MODEL_WIDTH, KEY_VALUE_HEADS * HEAD_SIZE), MODEL_WIDTH ** -0.5, 0.15625, ((0, 8), (1, 4)))
    out_weight = bell_draw(keys[5], (QUERY_HEAD_COUNT * HEAD_SIZE, MODEL_WIDTH), (max(QUERY_HEAD_COUNT * HEAD_SIZE // 256, 1)) ** -0.5, 2.5, ((0, 4), (1, 8)))
    second_gain = jnp.clip(1.0 + 0.1 * jax.random.normal(keys[6], (MODEL_WIDTH,), jnp.float32), 0.5, 1.5)
    gate_weight = bell_draw(keys[7], (EXPERTS, MODEL_WIDTH, FF), MODEL_WIDTH ** -0.5, 0.15625, ((0, 4), (1, 8)))
    up_weight = bell_draw(keys[8], (EXPERTS, MODEL_WIDTH, FF), MODEL_WIDTH ** -0.5, 0.15625, ((0, 4), (1, 8)))
    down_weight = bell_draw(keys[9], (EXPERTS, FF, MODEL_WIDTH), (max(FF // 128, 1)) ** -0.5, 3.0, ((0, 4), (2, 8)))
    routes_keys = jax.random.split(jax.random.fold_in(keys[10], 1), SEQS * SEQ // TOK_DEV)
    routes_turns = jax.random.permutation(jax.random.fold_in(keys[10], 3), SEQS * SEQ // TOK_DEV)
    routes = jax.vmap(lambda own, number: assign_block(jax.random.fold_in(keys[10], 2), own, number, TOK_DEV, EXPERTS, TOPK, CAP, 1))(routes_keys, routes_turns).reshape((SEQS, SEQ, TOPK))
    route_logits = bell_draw(keys[11], (SEQS, SEQ, TOPK), 0.5, 1.25, ((0, 8), (1, 4)), jnp.float32)
    cotangent = bell_draw(keys[12], (SEQS, SEQ, MODEL_WIDTH), 1.0, 6.0, ((0, 8), (1, 4)))
    return dict(tokens=tokens, first_gain=first_gain, query_weight=query_weight, key_matrix=key_matrix, value_matrix=value_matrix, out_weight=out_weight, second_gain=second_gain, gate_weight=gate_weight, up_weight=up_weight, down_weight=down_weight, routes=routes, route_logits=route_logits, cotangent=cotangent)


@jax.custom_vjp
def low(v):
    return lax.optimization_barrier(v.astype(jnp.bfloat16)).astype(jnp.float32)

@jax.custom_vjp
def low_back(v):
    return v

def low_keep(v):
    return (low(v), None)

def low_pass(kept, grad):
    return (grad,)

def back_keep(v):
    return (v, None)

def back_low(kept, grad):
    return (low(grad),)
low.defvjp(low_keep, low_pass)
low_back.defvjp(back_keep, back_low)
epsilon = 1e-06
rope_base = 10000.0
residual_factor = 0.22
score_factor = 0.015625
masked_value = -1e+30
highest_value = lax.Precision.HIGHEST

def rms_norm(rows, gain):
    return rows * lax.rsqrt(lax.optimization_barrier(jnp.mean(rows * rows, axis=-1, keepdims=True)) + epsilon) * gain

def rotary_embedding(rows, sign):
    width = rows.shape[-1]
    half = width // 2
    length_total = rows.shape[0]
    freq = rope_base ** (-(jnp.arange(half).astype(jnp.float32) * 2.0 / width))
    angle = jnp.arange(length_total).astype(jnp.float32)[:, None] * freq[None, :]
    cosine = jnp.cos(angle)[:, None, :]
    sine = sign * jnp.sin(angle)[:, None, :]
    first = rows[..., :half]
    second = rows[..., half:]
    return jnp.concatenate([first * cosine - second * sine, first * sine + second * cosine], axis=-1)

def attend_block(query_block, key_rows, value_rows, offset):
    raw = jnp.einsum('qhgd,khd->hgqk', query_block, key_rows, precision=highest_value)
    scores = low_back(raw * score_factor)
    positions = offset + jnp.arange(query_block.shape[0]).astype(jnp.int32)
    columns = jnp.arange(key_rows.shape[0]).astype(jnp.int32)
    scores = jnp.where(columns[None, :] <= positions[:, None], scores, masked_value)
    top = lax.optimization_barrier(jnp.max(scores, axis=-1, keepdims=True))
    weights = jnp.exp(scores - top)
    probs = weights / lax.optimization_barrier(jnp.sum(weights, axis=-1, keepdims=True))
    mixed = jnp.einsum('hgqk,khd->qhgd', low(probs), value_rows, precision=highest_value)
    return low(low_back(mixed))

def attend_sequence(normed_rows, query_weight, key_matrix, value_matrix, out_weight):
    length_total = normed_rows.shape[0]
    ratio_factor = QUERY_HEAD_COUNT // KEY_VALUE_HEADS
    query_rows = low_back(jnp.dot(normed_rows, query_weight, precision=highest_value)).reshape(length_total, QUERY_HEAD_COUNT, HEAD_SIZE)
    query_rows = low(rotary_embedding(query_rows, 1.0)).reshape(length_total, KEY_VALUE_HEADS, ratio_factor, HEAD_SIZE)
    key_rows = low_back(jnp.dot(normed_rows, key_matrix, precision=highest_value)).reshape(length_total, KEY_VALUE_HEADS, HEAD_SIZE)
    key_rows = low(rotary_embedding(key_rows, 1.0))
    value_rows = low(low_back(jnp.dot(normed_rows, value_matrix, precision=highest_value))).reshape(length_total, KEY_VALUE_HEADS, HEAD_SIZE)
    block_slice = min(512, length_total)
    count_total = length_total // block_slice
    block_list = query_rows.reshape(count_total, block_slice, KEY_VALUE_HEADS, ratio_factor, HEAD_SIZE)
    offsets = (jnp.arange(count_total) * block_slice).astype(jnp.int32)
    stepper = jax.checkpoint(attend_block)
    mixed = lax.map(lambda pair: stepper(pair[0], key_rows, value_rows, pair[1]), (block_list, offsets))
    return low_back(jnp.dot(mixed.reshape(length_total, QUERY_HEAD_COUNT * HEAD_SIZE), out_weight, precision=highest_value))

def route_slots(route_rows):
    flat = route_rows.reshape(-1).astype(jnp.int32)
    total = flat.shape[0]
    hits = (flat[:, None] == jnp.arange(EXPERTS).astype(jnp.int32)[None, :]).astype(jnp.int32)
    before = (jnp.cumsum(hits, axis=0) - hits).astype(jnp.int32)
    place = lax.optimization_barrier(jnp.sum(before * hits, axis=1)).astype(jnp.int32)
    target = (flat * CAP + place).astype(jnp.int32)
    owner = jnp.zeros((EXPERTS * CAP,), jnp.int32).at[target].set(jnp.arange(total).astype(jnp.int32))
    filled = jnp.zeros((EXPERTS * CAP,), jnp.int32).at[target].set(jnp.ones((total,), jnp.int32))
    return (target, owner, filled)

def expert_block(normed_rows, route_rows, logit_rows, gate_weight, up_weight, down_weight):
    target, owner, filled = route_slots(route_rows)
    source = normed_rows[owner // TOPK] * filled[:, None].astype(normed_rows.dtype)
    rows = low_back(source).reshape(EXPERTS, CAP, MODEL_WIDTH)
    gate = low_back(jnp.einsum('ecd,edf->ecf', rows, gate_weight, precision=highest_value))
    upper = low_back(jnp.einsum('ecd,edf->ecf', rows, up_weight, precision=highest_value))
    active = low(jax.nn.silu(gate) * upper)
    produced = low(low_back(jnp.einsum('ecf,efd->ecd', active, down_weight, precision=highest_value)))
    picked = produced.reshape(EXPERTS * CAP, MODEL_WIDTH)[target].reshape(-1, TOPK, MODEL_WIDTH)
    weights = jnp.exp(logit_rows - lax.optimization_barrier(jnp.max(logit_rows, axis=-1, keepdims=True)))
    chance = weights / lax.optimization_barrier(jnp.sum(weights, axis=-1, keepdims=True))
    return jnp.einsum('tk,tkd->td', chance, picked, precision=highest_value)

def layer(routes, packed):
    tokens, first_gain, query_weight, key_matrix, value_matrix, out_weight, second_gain, gate_weight, up_weight, down_weight, route_logits = packed
    normed_rows = low(rms_norm(tokens, first_gain))
    attend = jax.checkpoint(attend_sequence)
    branch = lax.map(lambda rows: attend(rows, query_weight, key_matrix, value_matrix, out_weight), normed_rows)
    middle = tokens + residual_factor * branch
    normed_two = low(rms_norm(middle, second_gain))
    mixer = jax.checkpoint(expert_block)
    block_list = normed_two.shape[0] * normed_two.shape[1] // TOK_DEV
    mixed = lax.map(lambda trio: mixer(trio[0], trio[1], trio[2], gate_weight, up_weight, down_weight), (normed_two.reshape(block_list, TOK_DEV, MODEL_WIDTH), routes.reshape(block_list, TOK_DEV, TOPK), route_logits.reshape(block_list, TOK_DEV, TOPK)))
    return middle + residual_factor * mixed.reshape(middle.shape)

def reference(tokens, first_gain, query_weight, key_matrix, value_matrix, out_weight, second_gain, gate_weight, up_weight, down_weight, routes, route_logits, cotangent):
    floats = (tokens.astype(jnp.float32), first_gain.astype(jnp.float32), query_weight.astype(jnp.float32), key_matrix.astype(jnp.float32), value_matrix.astype(jnp.float32), out_weight.astype(jnp.float32), second_gain.astype(jnp.float32), gate_weight.astype(jnp.float32), up_weight.astype(jnp.float32), down_weight.astype(jnp.float32), route_logits.astype(jnp.float32))
    result, pullback = jax.vjp(lambda packed: layer(routes, packed), floats)
    grads = pullback(cotangent.astype(jnp.float32))[0]
    return (result.astype(jnp.bfloat16), grads[0], grads[1], grads[2], grads[3], grads[4], grads[5], grads[6], grads[7], grads[8], grads[9], grads[10])
```

```python
import jax
import jax.numpy as jnp
import numpy as np
from jax import lax
from jax.sharding import Mesh, PartitionSpec as P

HEAD_SIZE = 64
EXPERTS = 40
TOPK = 8

epsilon = 1e-06
rope_base = 10000.0
residual_factor = 0.22
score_factor = 0.015625
masked_value = -1e30

f32 = jnp.float32
bf16 = jnp.bfloat16


def swap(value, axis, step):
    count = lax.axis_size(axis)
    return lax.ppermute(value, axis, [(i, i ^ step) for i in range(count)])


def after(value, *others):
    return lax.optimization_barrier((value,) + others)[0]


def pick(array, index, dim):
    return lax.dynamic_index_in_dim(array, index, dim, keepdims=False)


def rms_factor(rows):
    return lax.rsqrt(jnp.mean(rows * rows, axis=-1, keepdims=True) + epsilon)


def norm_back(rows, factor, gain, upstream):
    scaled = upstream * gain
    inner = jnp.mean(scaled * rows, axis=-1, keepdims=True)
    return factor * scaled - rows * factor * factor * factor * inner


def rotary(rows, cosine, sine):
    half = rows.shape[-1] // 2
    first = rows[..., :half]
    second = rows[..., half:]
    return jnp.concatenate(
        [first * cosine - second * sine, first * sine + second * cosine], axis=-1
    )


def contract_rows(left, right):
    return lax.dot_general(left, right, (((0,), (0,)), ((), ())), preferred_element_type=f32)


def contract_cols(left, right):
    return lax.dot_general(left, right, (((1,), (1,)), ((), ())), preferred_element_type=f32)


def gather_gx(block):
    return [block] + [swap(block, "gx", s) for s in range(1, lax.axis_size("gx"))]


def scatter_gx(blocks):
    total = blocks[0].astype(f32)
    for s in range(1, len(blocks)):
        total = total + swap(blocks[s].astype(bf16), "gx", s).astype(f32)
    return total


def gather_gy(block):
    parts = [block, swap(block, "gw", 1)]
    for s in range(1, lax.axis_size("gt")):
        parts = parts + [swap(p, "gt", s) for p in parts[:2]]
    parts = [q for p in parts for q in (p, swap(p, "co", 1))]
    me = (lax.axis_index("gt") * 2 + lax.axis_index("gw")) * 2 + lax.axis_index("co")
    stacked = jnp.stack(parts)
    return jnp.concatenate([lax.dynamic_index_in_dim(stacked, j ^ me, 0) for j in range(len(parts))])


def gather_halves(weight):
    side = lax.axis_index("gw")
    half = weight.shape[2] // 2
    keep = lax.dynamic_slice_in_dim(weight, side * half, half, 2)
    give = lax.dynamic_slice_in_dim(weight, (1 - side) * half, half, 2)
    parts = [keep, swap(give, "gw", 1)]
    for s in range(1, lax.axis_size("gt")):
        parts = parts + [swap(p, "gt", s) for p in parts[:2]]
    parts = [q for p in parts for q in (p, swap(p, "co", 1))]
    me = (lax.axis_index("gt") * 2 + side) * 2 + lax.axis_index("co")
    stacked = jnp.stack(parts, axis=1)
    ordered = jnp.concatenate(
        [lax.dynamic_index_in_dim(stacked, j ^ me, 1) for j in range(len(parts))], axis=1
    )
    return ordered.reshape(weight.shape[0], -1, half)


def scatter_halves(grad):
    many = lax.axis_size("gt")
    t, w, k = lax.axis_index("gt"), lax.axis_index("gw"), lax.axis_index("co")
    experts, _, half = grad.shape
    grad = grad.reshape(experts, many * 2, 2, -1, half)
    total = pick(grad, k, 2).astype(f32) + swap(pick(grad, 1 - k, 2), "co", 1).astype(f32)
    total = total.astype(bf16).reshape(experts, many, 2, -1, half)
    own = pick(total, t, 1).astype(f32)
    for s in range(1, many):
        own = own + swap(pick(total, t ^ s, 1), "gt", s).astype(f32)
    mine = pick(own, w, 1)
    other = swap(pick(own, 1 - w, 1).astype(bf16), "gw", 1).astype(f32)
    low = jnp.where(w == 0, mine, other)
    high = jnp.where(w == 0, other, mine)
    return jnp.concatenate([low, high], axis=2)


def scatter_gy(grad):
    many = lax.axis_size("gt")
    t, w, k = lax.axis_index("gt"), lax.axis_index("gw"), lax.axis_index("co")
    cols = grad.shape[1]
    grad = grad.reshape(many * 2, 2, -1, cols)
    total = pick(grad, k, 1).astype(f32) + swap(pick(grad, 1 - k, 1), "co", 1).astype(f32)
    total = total.astype(bf16).reshape(many, 2, -1, cols)
    own = pick(total, t, 0).astype(f32)
    for s in range(1, many):
        own = own + swap(pick(total, t ^ s, 0), "gt", s).astype(f32)
    own = own.astype(bf16)
    return pick(own, w, 0).astype(f32) + swap(pick(own, 1 - w, 0), "gw", 1).astype(f32)


def block_scores(query_rows, key_rows, positions):
    raw = jnp.einsum("qhgd,khd->hgqk", query_rows, key_rows, preferred_element_type=f32)
    return jnp.where(positions[None, :] <= positions[:, None], raw * score_factor, masked_value)


def attend_forward(query_rows, key_rows, value_rows, positions):
    scores = block_scores(query_rows, key_rows, positions)
    top = jnp.max(scores, axis=-1, keepdims=True)
    weights = jnp.exp(scores - top)
    total = jnp.sum(weights, axis=-1, keepdims=True)
    probs = (weights / total).astype(bf16)
    mixed = jnp.einsum("hgqk,khd->qhgd", probs, value_rows, preferred_element_type=f32)
    return (mixed.astype(bf16).reshape(query_rows.shape[0], -1), top + jnp.log(total))


def attend_backward(query_rows, key_rows, value_rows, heads_back, spread, positions):
    scores = block_scores(query_rows, key_rows, positions)
    probs = jnp.exp(scores - spread)
    prob_back = jnp.einsum("qhgd,khd->hgqk", heads_back, value_rows, preferred_element_type=f32)
    inner = jnp.sum(probs * prob_back, axis=-1, keepdims=True)
    score_back = (probs * (prob_back - inner)).astype(bf16)
    query_back = jnp.einsum("hgqk,khd->qhgd", score_back, key_rows, preferred_element_type=f32)
    key_back = jnp.einsum("hgqk,qhgd->khd", score_back, query_rows, preferred_element_type=f32)
    value_back = jnp.einsum(
        "hgqk,qhgd->khd", probs.astype(bf16), heads_back, preferred_element_type=f32
    )
    return (query_back * score_factor, key_back * score_factor, value_back)


def local(
    tokens,
    first_gain,
    query_weight,
    key_matrix,
    value_matrix,
    out_weight,
    second_gain,
    gate_weight,
    up_weight,
    down_weight,
    routes,
    route_logits,
    cotangent,
):
    groups = lax.axis_size("gx")
    me_x = lax.axis_index("gx")
    own_tokens = tokens[0]
    rows, width = own_tokens.shape
    query_cols = query_weight.shape[1]
    key_cols = key_matrix.shape[1]
    query_heads = query_cols // HEAD_SIZE
    pair_heads = key_cols // HEAD_SIZE
    ratio = query_heads // pair_heads

    token_blocks = gather_gx(own_tokens)
    attention = jnp.concatenate(
        [query_weight, key_matrix, value_matrix, out_weight.T], axis=1
    )
    attention_full = gather_gy(attention).reshape(width, -1)
    joined = attention_full[:, : query_cols + 2 * key_cols]
    out_full = attention_full[:, query_cols + 2 * key_cols :]

    gate_full = gather_halves(after(gate_weight, attention_full))
    up_full = gather_halves(after(up_weight, attention_full))
    down_full = gather_halves(jnp.swapaxes(after(down_weight, attention_full), 1, 2))

    logits = route_logits[0]
    weights = jnp.exp(logits - jnp.max(logits, axis=-1, keepdims=True))
    chance = weights / jnp.sum(weights, axis=-1, keepdims=True)
    routing = jnp.concatenate([routes[0].astype(f32), chance], axis=1)

    def gather_tokens(block):
        parts = gather_gx(block)
        return jnp.concatenate(parts + [swap(p, "gw", 1) for p in parts], axis=0)

    cotangent_rows = gather_tokens(after(cotangent[0], token_blocks[groups - 1]))
    routing_rows = gather_tokens(after(routing, token_blocks[groups - 1]))

    sequence = jnp.concatenate(token_blocks, axis=0).astype(f32)
    length = sequence.shape[0]
    factor_all = rms_factor(sequence)
    sequence_rows = (sequence * factor_all * first_gain).astype(bf16)
    projected = jnp.dot(sequence_rows, joined, preferred_element_type=f32)
    positions = jnp.concatenate(
        [(me_x ^ s) * rows + jnp.arange(rows, dtype=jnp.int32) for s in range(groups)]
    )
    half = HEAD_SIZE // 2
    freq = rope_base ** (-(jnp.arange(half, dtype=f32) * 2.0 / HEAD_SIZE))
    angle = positions.astype(f32)[:, None] * freq[None, :]
    cosine = jnp.cos(angle)[:, None, :]
    sine = jnp.sin(angle)[:, None, :]
    query_rows = rotary(projected[:, :query_cols].reshape(length, query_heads, HEAD_SIZE), cosine, sine)
    query_rows = query_rows.astype(bf16).reshape(length, pair_heads, ratio, HEAD_SIZE)
    key_rows = rotary(
        projected[:, query_cols : query_cols + key_cols].reshape(length, pair_heads, HEAD_SIZE),
        cosine,
        sine,
    ).astype(bf16)
    value_rows = (
        projected[:, query_cols + key_cols :].reshape(length, pair_heads, HEAD_SIZE).astype(bf16)
    )
    heads, spread = attend_forward(query_rows, key_rows, value_rows, positions)
    branch_parts = contract_cols(heads, out_full).astype(bf16)
    branch = scatter_gx([branch_parts[s * rows : (s + 1) * rows] for s in range(groups)])

    hidden = own_tokens.astype(f32)
    middle = hidden + residual_factor * branch
    factor_two = rms_factor(middle)
    normed_two = (middle * factor_two * second_gain).astype(bf16)
    normed_rows = gather_tokens(normed_two)

    experts = gate_weight.shape[0]
    first_expert = me_x * experts
    ids = (first_expert + jnp.arange(experts, dtype=jnp.int32)).astype(f32)
    same = routing_rows[None, :, :TOPK] == ids[:, None, None]
    chosen = jnp.sum(jnp.where(same, routing_rows[None, :, TOPK:], 0.0), axis=2)[:, :, None]
    back = jnp.einsum("td,edf->etf", cotangent_rows, down_full, preferred_element_type=f32)
    gate = jnp.einsum("td,edf->etf", normed_rows, gate_full, preferred_element_type=f32)
    upper = jnp.einsum("td,edf->etf", normed_rows, up_full, preferred_element_type=f32)
    sigma = jax.nn.sigmoid(gate)
    active = gate * sigma * upper
    back = back * residual_factor
    chance_part = jnp.sum(active * back, axis=2)
    scaled = (active * chosen).astype(bf16)
    active_back = back * chosen
    gate_back = (active_back * upper * sigma * (1.0 + gate * (1.0 - sigma))).astype(bf16)
    upper_back = (active_back * gate * sigma).astype(bf16)

    rows_back = jnp.einsum("etf,edf->td", gate_back, gate_full, preferred_element_type=f32)
    rows_back = rows_back + jnp.einsum("etf,edf->td", upper_back, up_full, preferred_element_type=f32)
    rows_back = rows_back.astype(bf16)

    def scatter_tokens(parts, kind):
        cut = [parts[s * rows : (s + 1) * rows] for s in range(2 * groups)]
        own = [
            cut[s].astype(f32) + swap(cut[groups + s], "gw", 1).astype(f32) for s in range(groups)
        ]
        total = own[0]
        for s in range(1, groups):
            total = total + swap(own[s].astype(kind), "gx", s).astype(f32)
        return total

    normed_two_back = scatter_tokens(rows_back, bf16)

    mixed_parts = jnp.einsum("etf,edf->td", scaled, down_full, preferred_element_type=f32)
    mixed = scatter_tokens(mixed_parts.astype(bf16), bf16)
    output = (middle + residual_factor * mixed).astype(bf16)
    chance_rows = jnp.sum(jnp.where(same, chance_part[:, :, None], 0.0), axis=0)
    chance_back = scatter_tokens(chance_rows, f32)
    logit_back = chance * (chance_back - jnp.sum(chance * chance_back, axis=-1, keepdims=True))

    gate_grad = jnp.einsum("td,etf->edf", normed_rows, gate_back, preferred_element_type=f32)
    up_grad = jnp.einsum("td,etf->edf", normed_rows, upper_back, preferred_element_type=f32)
    down_grad = jnp.einsum("td,etf->edf", cotangent_rows, scaled, preferred_element_type=f32)
    gate_sum = scatter_halves(gate_grad.astype(bf16))
    up_sum = scatter_halves(up_grad.astype(bf16))
    down_sum = scatter_halves((residual_factor * down_grad).astype(bf16))

    upstream = cotangent[0].astype(f32)
    middle_back = upstream + norm_back(middle, factor_two, second_gain, normed_two_back)
    second_part = jnp.sum(normed_two_back * middle * factor_two, axis=0)
    branch_back = (residual_factor * middle_back).astype(bf16)
    piece = jnp.concatenate(gather_gx(branch_back), axis=0)
    heads_back = jnp.dot(piece, out_full, preferred_element_type=f32)
    out_grad = contract_rows(piece, heads)
    heads_back = heads_back.astype(bf16).reshape(length, pair_heads, ratio, HEAD_SIZE)
    query_back, key_back, value_back = attend_backward(
        query_rows, key_rows, value_rows, heads_back, spread, positions
    )
    query_back = rotary(query_back.reshape(length, query_heads, HEAD_SIZE), cosine, -sine)
    key_back = rotary(key_back, cosine, -sine)
    projected_back = jnp.concatenate(
        [
            query_back.reshape(length, query_cols),
            key_back.reshape(length, key_cols),
            value_back.reshape(length, key_cols),
        ],
        axis=1,
    ).astype(bf16)
    normed_one_parts = contract_cols(projected_back, joined)
    first_part = jnp.sum(normed_one_parts * (sequence * factor_all), axis=0)
    normed_one_back = scatter_gx(
        [normed_one_parts[s * rows : (s + 1) * rows] for s in range(groups)]
    )
    tokens_back = middle_back + norm_back(hidden, factor_all[:rows], first_gain, normed_one_back)
    gains = lax.psum(jnp.stack([first_part, second_part]), ("gx", "gt", "gw", "co"))
    joined_grad = contract_rows(sequence_rows, projected_back)
    attention_sum = scatter_gy(jnp.concatenate([joined_grad, out_grad], axis=1).astype(bf16))
    return (
        output[None],
        tokens_back[None],
        gains[0],
        attention_sum[:, :query_cols],
        attention_sum[:, query_cols : query_cols + key_cols],
        attention_sum[:, query_cols + key_cols : query_cols + 2 * key_cols],
        attention_sum[:, query_cols + 2 * key_cols :].T,
        gains[1],
        gate_sum,
        up_sum,
        jnp.swapaxes(down_sum, 1, 2),
        logit_back[None],
    )


def solution(mesh):
    groups, others = mesh.shape["gx"], mesh.shape["gy"]
    split = Mesh(mesh.devices.reshape(groups, others // 4, 2, 2), ("gx", "gt", "gw", "co"))
    gy = ("gt", "gw", "co")
    in_specs = (
        P(gy, "gx", None),
        P(),
        P(gy, "gx"),
        P(gy, "gx"),
        P(gy, "gx"),
        P("gx", gy),
        P(),
        P("gx", gy, None),
        P("gx", gy, None),
        P("gx", None, gy),
        P(gy, "gx", None),
        P(gy, "gx", None),
        P(gy, "gx", None),
    )
    out_specs = (
        P(gy, "gx", None),
        P(gy, "gx", None),
        P(),
        P(gy, "gx"),
        P(gy, "gx"),
        P(gy, "gx"),
        P("gx", gy),
        P(),
        P("gx", gy, None),
        P("gx", gy, None),
        P("gx", None, gy),
        P(gy, "gx", None),
    )
    return jax.shard_map(local, mesh=split, in_specs=in_specs, out_specs=out_specs, check_vma=False)
```

```python
import functools

import jax
import jax.numpy as jnp
from jax import lax
from jax.experimental import pallas as pl
from jax.experimental.pallas import tpu as pltpu
from jax.sharding import Mesh, PartitionSpec as P

HEAD_SIZE = 64
EXPERTS = 40
TOPK = 8
CAP = 48

epsilon = 1e-06
rope_base = 10000.0
residual_factor = 0.22
score_factor = 0.015625
masked_value = -1e30

f32 = jnp.float32
bf16 = jnp.bfloat16


def swap(value, axis, step):
    count = lax.axis_size(axis)
    return lax.ppermute(value, axis, [(i, i ^ step) for i in range(count)])


def after(value, *others):
    return lax.optimization_barrier((value,) + others)[0]


def pick(array, index, dim):
    return lax.dynamic_index_in_dim(array, index, dim, keepdims=False)


def rms_factor(rows):
    return lax.rsqrt(jnp.mean(rows * rows, axis=-1, keepdims=True) + epsilon)


def norm_back(rows, factor, gain, upstream):
    scaled = upstream * gain
    inner = jnp.mean(scaled * rows, axis=-1, keepdims=True)
    return factor * scaled - rows * factor * factor * factor * inner


def rotary(rows, cosine, sine):
    half = rows.shape[-1] // 2
    first = rows[..., :half]
    second = rows[..., half:]
    return jnp.concatenate(
        [first * cosine - second * sine, first * sine + second * cosine], axis=-1
    )


def contract_rows(left, right):
    return lax.dot_general(left, right, (((0,), (0,)), ((), ())), preferred_element_type=f32)


def contract_cols(left, right):
    return lax.dot_general(left, right, (((1,), (1,)), ((), ())), preferred_element_type=f32)


def gather_gx(block):
    return [block] + [swap(block, "gx", s) for s in range(1, lax.axis_size("gx"))]


def scatter_gx(blocks):
    total = blocks[0].astype(f32)
    for s in range(1, len(blocks)):
        total = total + swap(blocks[s].astype(bf16), "gx", s).astype(f32)
    return total


def gather_gy(block):
    parts = [block, swap(block, "gw", 1)]
    many = lax.axis_size("gt")
    for s in range(1, many):
        parts.append(swap(block, "gt", s))
    for s in range(1, many):
        parts.append(swap(parts[1], "gt", s))
    parts = parts + [swap(p, "co", 1) for p in parts]
    places = [0, 2] + [4 * s for s in range(1, many)] + [4 * s + 2 for s in range(1, many)]
    places = places + [p + 1 for p in places]
    me = (lax.axis_index("gt") * 2 + lax.axis_index("gw")) * 2 + lax.axis_index("co")
    count = len(parts)

    def kernel(me_ref, *refs):
        for place, ref in zip(places, refs[:count]):
            refs[count][me_ref[0] ^ place] = ref[...]

    full = pl.BlockSpec(memory_space=pltpu.VMEM)
    stacked = pl.pallas_call(
        kernel,
        out_shape=jax.ShapeDtypeStruct((count,) + block.shape, block.dtype),
        in_specs=[pl.BlockSpec(memory_space=pltpu.SMEM)] + [full] * count,
        out_specs=full,
        compiler_params=pltpu.CompilerParams(vmem_limit_bytes=40 * 2**20),
        name="place_attention_weights",
    )(jnp.full((1,), me, jnp.int32), *parts)
    return stacked, parts[1], parts[many + 1 if many > 1 else 1]


def halve_weights(gate, up, down):
    experts, rows, full = gate.shape
    half = full // 2

    def kernel(side_ref, gate_ref, up_ref, down_ref, keep_gu, give_gu, keep_d, give_d):
        flipped = down_ref[0].astype(f32).T.astype(bf16)
        pieces = []
        for low in (0, half):
            pieces.append((gate_ref[0, :, low : low + half], up_ref[0, :, low : low + half], flipped[:, low : low + half]))

        def put(piece, gu, d):
            gu[0, :, :half] = piece[0]
            gu[0, :, half:] = piece[1]
            d[0] = piece[2]

        @pl.when(side_ref[0] == 0)
        def _():
            put(pieces[0], keep_gu, keep_d)
            put(pieces[1], give_gu, give_d)

        @pl.when(side_ref[0] != 0)
        def _():
            put(pieces[1], keep_gu, keep_d)
            put(pieces[0], give_gu, give_d)

    def block(shape):
        return pl.BlockSpec((1,) + shape, lambda e, *_: (e, 0, 0))

    wide = jax.ShapeDtypeStruct((experts, rows, full), bf16)
    thin = jax.ShapeDtypeStruct((experts, rows, half), bf16)
    return pl.pallas_call(
        kernel,
        grid_spec=pltpu.PrefetchScalarGridSpec(
            num_scalar_prefetch=1,
            grid=(experts,),
            in_specs=[block((rows, full)), block((rows, full)), block((full, rows))],
            out_specs=[block((rows, full)), block((rows, full)), block((rows, half)), block((rows, half))],
        ),
        out_shape=[wide, wide, thin, thin],
        name="halve_weights",
    )(jnp.full((1,), lax.axis_index("gw"), jnp.int32), gate, up, down)


def gather_weights(gate, up, down, first_x, first_y):
    many = lax.axis_size("gt")
    keep_gu, give_gu, keep_d, give_d = halve_weights(gate, up, down)
    got_gu = swap(after(give_gu, first_x), "gw", 1)
    got_d = swap(after(give_d, got_gu), "gw", 1)
    wide, thin = [keep_gu, got_gu], [keep_d, got_d]
    places = [0, 2]
    last = first_y
    for bulk, many_parts in ((wide, True), (thin, False)):
        for w in range(2):
            for s in range(1, many):
                last = swap(after(bulk[w], last), "gt", s)
                bulk.append(last)
    for w in range(2):
        for s in range(1, many):
            places.append(4 * s + 2 * w)
    wide = wide + [swap(p, "co", 1) for p in wide]
    thin = thin + [swap(p, "co", 1) for p in thin]
    return wide, thin, places + [p + 1 for p in places]


def scatter_gradients(parts, rows):
    many = lax.axis_size("gt")
    total = {}
    order = [(t, w) for t in range(many - 1, -1, -1) for w in (1, 0)]
    for t, w in order:
        got = swap(parts[t, w, 1], "co", 1)
        total[t, w] = parts[t, w, 0].astype(f32) + got.astype(f32)
    own = {}
    last = None
    for w in (1, 0):
        own[w] = total[0, w]
        for t in range(1, many):
            send = total[t, w].astype(bf16)
            last = swap(send if last is None else after(send, last), "gt", t)
            own[w] = own[w] + last.astype(f32)
    return own[0], swap(own[1].astype(bf16), "gw", 1).astype(f32)


def scatter_gy(grad):
    many = lax.axis_size("gt")
    t, w, k = lax.axis_index("gt"), lax.axis_index("gw"), lax.axis_index("co")
    cols = grad.shape[1]
    grad = grad.reshape(many * 2, 2, -1, cols)
    total = pick(grad, k, 1).astype(f32) + swap(pick(grad, 1 - k, 1), "co", 1).astype(f32)
    total = total.astype(bf16).reshape(many, 2, -1, cols)
    own = pick(total, t, 0).astype(f32)
    for s in range(1, many):
        own = own + swap(pick(total, t ^ s, 0), "gt", s).astype(f32)
    own = own.astype(bf16)
    return pick(own, w, 0).astype(f32) + swap(pick(own, 1 - w, 0), "gw", 1).astype(f32)


def sum_everywhere(value):
    for axis in ("co", "gw", "gt", "gx"):
        step = 1
        while step < lax.axis_size(axis):
            value = value + swap(value, axis, step)
            step = step * 2
    return value


def slot_mask(slot_row):
    wanted = lax.broadcasted_iota(jnp.int32, (CAP, slot_row.shape[1]), 0).astype(f32)
    return slot_row == wanted


def gather_slots(rows_all, slots):
    blocks, experts, tokens = slots.shape
    width = rows_all.shape[1]

    def kernel(slots_ref, rows_ref, out_ref):
        mask = jnp.concatenate([slot_mask(slots_ref[0, e : e + 1, :]) for e in range(experts)], axis=0)
        found = jnp.dot(mask.astype(f32).astype(bf16), rows_ref[...], preferred_element_type=f32)
        out_ref[...] = found.astype(bf16).reshape(experts, 1, CAP, width)

    return pl.pallas_call(
        kernel,
        grid=(blocks,),
        in_specs=[
            pl.BlockSpec((1, experts, tokens), lambda b: (b, 0, 0)),
            pl.BlockSpec((tokens, width), lambda b: (b, 0)),
        ],
        out_specs=pl.BlockSpec((experts, 1, CAP, width), lambda b: (0, b, 0, 0)),
        out_shape=jax.ShapeDtypeStruct((experts, blocks, CAP, width), bf16),
        compiler_params=pltpu.CompilerParams(vmem_limit_bytes=40 * 2**20),
        cost_estimate=pl.CostEstimate(
            flops=2 * blocks * tokens * experts * CAP * width,
            bytes_accessed=2 * blocks * (tokens + experts * CAP) * width,
            transcendentals=0,
        ),
        name="gather_slots",
    )(slots, rows_all)


def sum_slots(slot_rows, slots):
    blocks, experts, tokens = slots.shape
    width = slot_rows.shape[3]

    def kernel(slots_ref, rows_ref, out_ref):
        mask = jnp.concatenate([slot_mask(slots_ref[0, e : e + 1, :]) for e in range(experts)], axis=0)
        total = contract_rows(mask.astype(f32).astype(bf16), rows_ref[...].reshape(experts * CAP, width))
        out_ref[...] = total.astype(bf16)

    return pl.pallas_call(
        kernel,
        grid=(blocks,),
        in_specs=[
            pl.BlockSpec((1, experts, tokens), lambda b: (b, 0, 0)),
            pl.BlockSpec((experts, 1, CAP, width), lambda b: (0, b, 0, 0)),
        ],
        out_specs=pl.BlockSpec((tokens, width), lambda b: (b, 0)),
        out_shape=jax.ShapeDtypeStruct((blocks * tokens, width), bf16),
        compiler_params=pltpu.CompilerParams(vmem_limit_bytes=40 * 2**20),
        cost_estimate=pl.CostEstimate(
            flops=2 * blocks * tokens * experts * CAP * width,
            bytes_accessed=2 * blocks * (tokens + experts * CAP) * width,
            transcendentals=0,
        ),
        name="sum_slots",
    )(slots, slot_rows)


def run_experts(rows_in, back_in, wide, thin, places, slots, chances):
    experts, blocks, _, width = rows_in.shape
    tokens = slots.shape[2]
    cut, half = thin[0].shape[1:]
    count = len(places)
    total_slots = blocks * CAP
    me = (lax.axis_index("gt") * 2 + lax.axis_index("gw")) * 2 + lax.axis_index("co")

    def kernel(me_ref, rows_ref, back_ref, slots_ref, chances_ref, *refs):
        wide_refs, thin_refs = refs[:count], refs[count : 2 * count]
        rows_out, mixed_out, chance_out = refs[2 * count : 2 * count + 3]
        grads = refs[2 * count + 3 : 3 * count + 3]
        gu_full, d_full, gu_total, d_total = refs[3 * count + 3 :]
        spots = [pl.ds(pl.multiple_of((me_ref[0] ^ place) * cut, cut), cut) for place in places]
        for spot, gu, d in zip(spots, wide_refs, thin_refs):
            gu_full[spot, :] = gu[0]
            d_full[spot, :] = d[0]
        rows = rows_ref[0].reshape(total_slots, width)
        back = back_ref[0].reshape(total_slots, width)
        masks = [slot_mask(slots_ref[0, b : b + 1, :]) for b in range(blocks)]
        chance = jnp.concatenate(
            [
                jnp.sum(jnp.where(masks[b], chances_ref[0, b : b + 1, :], 0.0), axis=1, keepdims=True)
                for b in range(blocks)
            ],
            axis=0,
        )
        both = jnp.dot(rows, gu_full[...], preferred_element_type=f32)
        active_back = jnp.dot(back, d_full[...], preferred_element_type=f32) * residual_factor
        gate, upper = both[:, :half], both[:, half:]
        sigma = jax.nn.sigmoid(gate)
        silu = gate * sigma
        active = silu * upper
        chance_back = jnp.sum(active * active_back, axis=1, keepdims=True)
        for b in range(blocks):
            column = chance_back[b * CAP : (b + 1) * CAP]
            chance_out[0, b : b + 1, :] = jnp.sum(jnp.where(masks[b], column, 0.0), axis=0, keepdims=True)
        scaled = (active * chance).astype(bf16)
        active_back = active_back * chance
        gate_back = active_back * upper * (sigma * (1.0 + gate * (1.0 - sigma)))
        upper_back = active_back * silu
        both_back = jnp.concatenate([gate_back.astype(bf16), upper_back.astype(bf16)], axis=1)
        rows_out[0] = contract_cols(both_back, gu_full[...]).astype(bf16).reshape(blocks, CAP, width)
        mixed_out[0] = contract_cols(scaled, d_full[...]).astype(bf16).reshape(blocks, CAP, width)
        gu_total[...] = contract_rows(rows, both_back).astype(bf16)
        d_total[...] = (contract_rows(back, scaled) * residual_factor).astype(bf16)
        for spot, grad in zip(spots, grads):
            grad[0, :, : 2 * half] = gu_total[spot, :]
            grad[0, :, 2 * half :] = d_total[spot, :]

    def block(shape):
        zeros = (0,) * len(shape)
        return pl.BlockSpec((1,) + shape, lambda e, *_: (e,) + zeros)

    flops = 2 * experts * total_slots * width * half * 9
    grad_shape = jax.ShapeDtypeStruct((experts, cut, 3 * half), bf16)
    slot_shape = jax.ShapeDtypeStruct((experts, blocks, CAP, width), bf16)
    out = pl.pallas_call(
        kernel,
        grid_spec=pltpu.PrefetchScalarGridSpec(
            num_scalar_prefetch=1,
            grid=(experts,),
            in_specs=[
                block((blocks, CAP, width)),
                block((blocks, CAP, width)),
                block((blocks, tokens)),
                block((blocks, tokens)),
            ]
            + [block((cut, 2 * half))] * count
            + [block((cut, half))] * count,
            out_specs=[block((blocks, CAP, width)), block((blocks, CAP, width)), block((blocks, tokens))]
            + [block((cut, 3 * half))] * count,
            scratch_shapes=[
                pltpu.VMEM((width, 2 * half), bf16),
                pltpu.VMEM((width, half), bf16),
                pltpu.VMEM((width, 2 * half), bf16),
                pltpu.VMEM((width, half), bf16),
            ],
        ),
        out_shape=[slot_shape, slot_shape, jax.ShapeDtypeStruct((experts, blocks, tokens), f32)]
        + [grad_shape] * count,
        compiler_params=pltpu.CompilerParams(vmem_limit_bytes=60 * 2**20),
        cost_estimate=pl.CostEstimate(
            flops=flops,
            bytes_accessed=2 * experts * (4 * total_slots * width + 6 * half * width),
            transcendentals=experts * total_slots * half,
        ),
        name="run_experts",
    )(jnp.full((1,), me, jnp.int32), rows_in, back_in, slots, chances, *wide, *thin)
    gradients = {(p // 4, (p // 2) % 2, p % 2): g for p, g in zip(places, out[3:])}
    return out[0], out[1], out[2], gradients


def block_scores(query_rows, key_rows, positions):
    raw = jnp.einsum("qhgd,khd->hgqk", query_rows, key_rows, preferred_element_type=f32)
    return jnp.where(positions[None, :] <= positions[:, None], raw * score_factor, masked_value)


def attend_forward(query_rows, key_rows, value_rows, positions):
    scores = block_scores(query_rows, key_rows, positions)
    top = jnp.max(scores, axis=-1, keepdims=True)
    weights = jnp.exp(scores - top)
    total = jnp.sum(weights, axis=-1, keepdims=True)
    probs = (weights / total).astype(bf16)
    mixed = jnp.einsum("hgqk,khd->qhgd", probs, value_rows, preferred_element_type=f32)
    return (mixed.astype(bf16).reshape(query_rows.shape[0], -1), top + jnp.log(total))


def attend_backward(query_rows, key_rows, value_rows, heads_back, spread, positions):
    scores = block_scores(query_rows, key_rows, positions)
    probs = jnp.exp(scores - spread)
    prob_back = jnp.einsum("qhgd,khd->hgqk", heads_back, value_rows, preferred_element_type=f32)
    inner = jnp.sum(probs * prob_back, axis=-1, keepdims=True)
    score_back = (probs * (prob_back - inner)).astype(bf16)
    query_back = jnp.einsum("hgqk,khd->qhgd", score_back, key_rows, preferred_element_type=f32)
    key_back = jnp.einsum("hgqk,qhgd->khd", score_back, query_rows, preferred_element_type=f32)
    value_back = jnp.einsum(
        "hgqk,qhgd->khd", probs.astype(bf16), heads_back, preferred_element_type=f32
    )
    return (query_back * score_factor, key_back * score_factor, value_back)


def local(
    tokens,
    first_gain,
    query_weight,
    key_matrix,
    value_matrix,
    out_weight,
    second_gain,
    gate_weight,
    up_weight,
    down_weight,
    routes,
    route_logits,
    cotangent,
):
    groups = lax.axis_size("gx")
    me_x = lax.axis_index("gx")
    own_tokens = tokens[0]
    rows, width = own_tokens.shape
    query_cols = query_weight.shape[1]
    key_cols = key_matrix.shape[1]
    query_heads = query_cols // HEAD_SIZE
    pair_heads = key_cols // HEAD_SIZE
    ratio = query_heads // pair_heads

    token_blocks = gather_gx(own_tokens)
    attention = jnp.concatenate(
        [query_weight, key_matrix, value_matrix, out_weight.T], axis=1
    )
    attention_full, first_x, first_y = gather_gy(attention)
    attention_full = attention_full.reshape(width, -1)
    joined = attention_full[:, : query_cols + 2 * key_cols]
    out_full = attention_full[:, query_cols + 2 * key_cols :]

    wide, thin, places = gather_weights(gate_weight, up_weight, down_weight, first_x, first_y)

    logits = route_logits[0]
    weights = jnp.exp(logits - jnp.max(logits, axis=-1, keepdims=True))
    chance = weights / jnp.sum(weights, axis=-1, keepdims=True)
    routing = jnp.concatenate([routes[0].astype(f32), chance], axis=1)
    last_token = token_blocks[groups - 1]
    me_w = lax.axis_index("gw")
    turned = [((me_x ^ s) * 2 + (me_w ^ w)) for w in range(2) for s in range(groups)]

    def gather_early(block):
        whole = lax.all_gather(after(block, last_token), ("gx", "gw"), axis=0)
        return jnp.stack([lax.dynamic_index_in_dim(whole, j, 0, keepdims=False) for j in turned])

    cotangent_rows = gather_early(cotangent[0]).reshape(-1, width)
    routing_rows = gather_early(routing)

    sequence = jnp.concatenate(token_blocks, axis=0).astype(f32)
    length = sequence.shape[0]
    factor_all = rms_factor(sequence)
    sequence_rows = (sequence * factor_all * first_gain).astype(bf16)
    projected = jnp.dot(sequence_rows, joined, preferred_element_type=f32)
    positions = jnp.concatenate(
        [(me_x ^ s) * rows + jnp.arange(rows, dtype=jnp.int32) for s in range(groups)]
    )
    freq = rope_base ** (-(jnp.arange(HEAD_SIZE // 2, dtype=f32) * 2.0 / HEAD_SIZE))
    angle = positions.astype(f32)[:, None] * freq[None, :]
    cosine = jnp.cos(angle)[:, None, :]
    sine = jnp.sin(angle)[:, None, :]
    query_rows = rotary(projected[:, :query_cols].reshape(length, query_heads, HEAD_SIZE), cosine, sine)
    query_rows = query_rows.astype(bf16).reshape(length, pair_heads, ratio, HEAD_SIZE)
    key_rows = rotary(
        projected[:, query_cols : query_cols + key_cols].reshape(length, pair_heads, HEAD_SIZE),
        cosine,
        sine,
    ).astype(bf16)
    value_rows = (
        projected[:, query_cols + key_cols :].reshape(length, pair_heads, HEAD_SIZE).astype(bf16)
    )
    heads, spread = attend_forward(query_rows, key_rows, value_rows, positions)
    branch_parts = contract_cols(heads, out_full).astype(bf16)
    branch = scatter_gx([branch_parts[s * rows : (s + 1) * rows] for s in range(groups)])

    hidden = own_tokens.astype(f32)
    middle = hidden + residual_factor * branch
    factor_two = rms_factor(middle)
    normed_two = (middle * factor_two * second_gain).astype(bf16)
    parts = gather_gx(normed_two)
    normed_rows = jnp.concatenate(parts + [swap(p, "gw", 1) for p in parts], axis=0)

    experts = gate_weight.shape[0]
    ids = (me_x * experts + jnp.arange(experts, dtype=jnp.int32)).astype(f32)
    same = routing_rows[:, None, :, :TOPK] == ids[None, :, None, None]
    hits = jnp.sum(same.astype(f32), axis=3)
    before = jnp.triu(jnp.ones((rows, rows), f32), 1)
    slots = jnp.where(hits > 0.0, jnp.einsum("beu,ut->bet", hits, before), -1.0)
    chosen = jnp.sum(jnp.where(same, routing_rows[:, None, :, TOPK:], 0.0), axis=3)
    rows_in = gather_slots(normed_rows, slots)
    back_in = gather_slots(cotangent_rows, slots)
    rows_back, mixed_parts, chance_part, gradients = run_experts(
        rows_in, back_in, wide, thin, places, jnp.swapaxes(slots, 0, 1), jnp.swapaxes(chosen, 0, 1)
    )
    rows_back = sum_slots(rows_back, slots)

    def cut(whole, s):
        return whole[s * rows : (s + 1) * rows]

    order = list(range(1, groups)) + [0]
    crossed = {s: swap(cut(rows_back, groups + s), "gw", 1) for s in order}
    normed_two_back = scatter_gx(
        [cut(rows_back, s).astype(f32) + crossed[s].astype(f32) for s in range(groups)]
    )

    mixed_rows = sum_slots(mixed_parts, slots).reshape(2 * groups, rows, width)
    mixed_rows = jnp.concatenate(
        [
            lax.dynamic_index_in_dim(mixed_rows, (w ^ me_w) * groups + (x ^ me_x), 0)
            for x in range(groups)
            for w in range(2)
        ]
    )
    mixed = lax.psum_scatter(mixed_rows, ("gx", "gw"), scatter_dimension=0).astype(f32)
    output = (middle + residual_factor * mixed).astype(bf16)
    chance_rows = jnp.sum(jnp.where(same, jnp.swapaxes(chance_part, 0, 1)[:, :, :, None], 0.0), axis=1)
    chance_rows = jnp.stack(
        [
            lax.dynamic_index_in_dim(chance_rows, (w ^ me_w) * groups + (x ^ me_x), 0, keepdims=False)
            for x in range(groups)
            for w in range(2)
        ]
    )
    chance_back = lax.psum_scatter(chance_rows, ("gx", "gw"), scatter_dimension=0)
    logit_back = chance * (chance_back - jnp.sum(chance * chance_back, axis=-1, keepdims=True))

    mine, other = scatter_gradients(gradients, rows)
    half = mine.shape[2] // 3
    gate_sum, up_sum, down_sum = [
        jnp.concatenate(
            [
                jnp.where(me_w == 0, mine[:, :, c : c + half], other[:, :, c : c + half]),
                jnp.where(me_w == 0, other[:, :, c : c + half], mine[:, :, c : c + half]),
            ],
            axis=2,
        )
        for c in (0, half, 2 * half)
    ]

    upstream = cotangent[0].astype(f32)
    middle_back = upstream + norm_back(middle, factor_two, second_gain, normed_two_back)
    second_part = jnp.sum(normed_two_back * middle * factor_two, axis=0)
    branch_back = (residual_factor * middle_back).astype(bf16)
    piece = jnp.concatenate(gather_gx(branch_back), axis=0)
    heads_back = jnp.dot(piece, out_full, preferred_element_type=f32)
    out_grad = contract_rows(piece, heads)
    heads_back = heads_back.astype(bf16).reshape(length, pair_heads, ratio, HEAD_SIZE)
    query_back, key_back, value_back = attend_backward(
        query_rows, key_rows, value_rows, heads_back, spread, positions
    )
    query_back = rotary(query_back.reshape(length, query_heads, HEAD_SIZE), cosine, -sine)
    key_back = rotary(key_back, cosine, -sine)
    projected_back = jnp.concatenate(
        [
            query_back.reshape(length, query_cols),
            key_back.reshape(length, key_cols),
            value_back.reshape(length, key_cols),
        ],
        axis=1,
    ).astype(bf16)
    normed_one_parts = contract_cols(projected_back, joined)
    first_part = jnp.sum(normed_one_parts * (sequence * factor_all), axis=0)
    normed_one_back = scatter_gx(
        [normed_one_parts[s * rows : (s + 1) * rows] for s in range(groups)]
    )
    tokens_back = middle_back + norm_back(hidden, factor_all[:rows], first_gain, normed_one_back)
    gains = sum_everywhere(jnp.stack([first_part, second_part]))
    joined_grad = contract_rows(sequence_rows, projected_back)
    attention_sum = scatter_gy(jnp.concatenate([joined_grad, out_grad], axis=1).astype(bf16))
    return (
        output[None],
        tokens_back[None],
        gains[0],
        attention_sum[:, :query_cols],
        attention_sum[:, query_cols : query_cols + key_cols],
        attention_sum[:, query_cols + key_cols : query_cols + 2 * key_cols],
        attention_sum[:, query_cols + 2 * key_cols :].T,
        gains[1],
        gate_sum,
        up_sum,
        jnp.swapaxes(down_sum, 1, 2),
        logit_back[None],
    )


def solution(mesh):
    groups, others = mesh.shape["gx"], mesh.shape["gy"]
    split = Mesh(mesh.devices.reshape(groups, others // 4, 2, 2), ("gx", "gt", "gw", "co"))
    gy = ("gt", "gw", "co")
    in_specs = (
        P(gy, "gx", None),
        P(),
        P(gy, "gx"),
        P(gy, "gx"),
        P(gy, "gx"),
        P("gx", gy),
        P(),
        P("gx", gy, None),
        P("gx", gy, None),
        P("gx", None, gy),
        P(gy, "gx", None),
        P(gy, "gx", None),
        P(gy, "gx", None),
    )
    out_specs = (
        P(gy, "gx", None),
        P(gy, "gx", None),
        P(),
        P(gy, "gx"),
        P(gy, "gx"),
        P(gy, "gx"),
        P("gx", gy),
        P(),
        P("gx", gy, None),
        P("gx", gy, None),
        P("gx", None, gy),
        P(gy, "gx", None),
    )
    return jax.shard_map(local, mesh=split, in_specs=in_specs, out_specs=out_specs, check_vma=False)
```

```python
import functools

import jax
import jax.numpy as jnp
from jax import lax
from jax.experimental import pallas as pl
from jax.experimental.pallas import tpu as pltpu
from jax.sharding import Mesh, PartitionSpec as P

HEAD_SIZE = 64
EXPERTS = 40
TOPK = 8
CAP = 48

epsilon = 1e-06
rope_base = 10000.0
residual_factor = 0.22
score_factor = 0.015625
masked_value = -1e30

f32 = jnp.float32
bf16 = jnp.bfloat16


def swap(value, axis, step):
    count = lax.axis_size(axis)
    return lax.ppermute(value, axis, [(i, i ^ step) for i in range(count)])


def tie(*values):
    return lax.optimization_barrier(values)


def pick(array, index, dim):
    return lax.dynamic_index_in_dim(array, index, dim, keepdims=False)


def rms_factor(rows):
    return lax.rsqrt(jnp.mean(rows * rows, axis=-1, keepdims=True) + epsilon)


def norm_back(rows, factor, gain, upstream):
    scaled = upstream * gain
    inner = jnp.mean(scaled * rows, axis=-1, keepdims=True)
    return factor * scaled - rows * factor * factor * factor * inner


def rotary(rows, cosine, sine):
    half = rows.shape[-1] // 2
    first = rows[..., :half]
    second = rows[..., half:]
    return jnp.concatenate(
        [first * cosine - second * sine, first * sine + second * cosine], axis=-1
    )


def contract_rows(left, right):
    return lax.dot_general(left, right, (((0,), (0,)), ((), ())), preferred_element_type=f32)


def contract_cols(left, right):
    return lax.dot_general(left, right, (((1,), (1,)), ((), ())), preferred_element_type=f32)


def gather_gx(block):
    return [block] + [swap(block, "gx", s) for s in range(1, lax.axis_size("gx"))]


def over_y(value):
    return [swap(value, "gt", s) for s in range(1, lax.axis_size("gt"))]


def spread_y(values):
    return [swap(value, "gt", s) for s, value in enumerate(values, 1)]


def part_places():
    many = lax.axis_size("gt")
    places = [0, 2] + [4 * s for s in range(1, many)] + [4 * s + 2 for s in range(1, many)]
    return places + [p + 1 for p in places]


def own_place():
    me = (lax.axis_index("gt") * 2 + lax.axis_index("gw")) * 2 + lax.axis_index("co")
    return jnp.full((1,), me, jnp.int32)


def own_side():
    return jnp.full((1,), lax.axis_index("gw"), jnp.int32)


def place_parts(parts):
    places = part_places()
    count = len(parts)

    def kernel(me_ref, *refs):
        for place, ref in zip(places, refs[:count]):
            refs[count][me_ref[0] ^ place] = ref[...]

    full = pl.BlockSpec(memory_space=pltpu.VMEM)
    return pl.pallas_call(
        kernel,
        out_shape=jax.ShapeDtypeStruct((count,) + parts[0].shape, parts[0].dtype),
        in_specs=[pl.BlockSpec(memory_space=pltpu.SMEM)] + [full] * count,
        out_specs=full,
        compiler_params=pltpu.CompilerParams(vmem_limit_bytes=40 * 2**20),
        name="place_parts",
    )(own_place(), *parts)


def halve_weights(gate, up, down, start, experts):
    rows, full = gate.shape[1:]
    half = full // 2

    def kernel(side_ref, gate_ref, up_ref, down_ref, keep, give):
        def put(low, out):
            for i, ref in enumerate((gate_ref, up_ref, down_ref)):
                out[0, :, i * half : (i + 1) * half] = ref[0, :, low : low + half]

        @pl.when(side_ref[0] == 0)
        def _():
            put(0, keep)
            put(half, give)

        @pl.when(side_ref[0] != 0)
        def _():
            put(half, keep)
            put(0, give)

    def block(columns, first):
        return pl.BlockSpec((1, rows, columns), lambda e, *_: (e + first, 0, 0))

    shape = jax.ShapeDtypeStruct((experts, rows, 3 * half), bf16)
    return pl.pallas_call(
        kernel,
        grid_spec=pltpu.PrefetchScalarGridSpec(
            num_scalar_prefetch=1,
            grid=(experts,),
            in_specs=[block(full, start)] * 3,
            out_specs=[block(3 * half, 0)] * 2,
        ),
        out_shape=[shape, shape],
        name="halve_weights",
    )(own_side(), gate, up, down)


def finish_gradients(summed, crossed, start, before, total_experts):
    experts, rows, columns = crossed.shape
    half = columns // 3
    count = len(summed)
    aliased = 0 if before is None else 3

    def kernel(side_ref, *refs):
        total = refs[0][0].astype(f32)
        for ref in refs[1:count]:
            total = total + ref[0].astype(f32)
        other = refs[count][0].astype(f32)

        def put(low, value):
            for i, out in enumerate(refs[count + 1 + aliased :]):
                out[0, :, low : low + half] = value[:, i * half : (i + 1) * half]

        @pl.when(side_ref[0] == 0)
        def _():
            put(0, total)
            put(half, other)

        @pl.when(side_ref[0] != 0)
        def _():
            put(half, total)
            put(0, other)

    def block(columns, first):
        return pl.BlockSpec((1, rows, columns), lambda e, *_: (e + first, 0, 0))

    shape = jax.ShapeDtypeStruct((total_experts, rows, 2 * half), f32)
    return pl.pallas_call(
        kernel,
        grid_spec=pltpu.PrefetchScalarGridSpec(
            num_scalar_prefetch=1,
            grid=(experts,),
            in_specs=[block(columns, 0)] * (count + 1) + [pl.BlockSpec(memory_space=pl.ANY)] * aliased,
            out_specs=[block(2 * half, start)] * 3,
        ),
        out_shape=[shape] * 3,
        input_output_aliases={count + 2 + i: i for i in range(aliased)},
        name="finish_gradients",
    )(own_side(), *summed, crossed, *(before or ()))


def scatter_gy(grad):
    many = lax.axis_size("gt")
    t, w, k = lax.axis_index("gt"), lax.axis_index("gw"), lax.axis_index("co")
    cols = grad.shape[1]
    grad = grad.reshape(many * 2, 2, -1, cols)
    total = pick(grad, k, 1).astype(f32) + swap(pick(grad, 1 - k, 1), "co", 1).astype(f32)
    total = total.astype(bf16).reshape(many, 2, -1, cols)
    own = pick(total, w, 1).astype(f32) + swap(pick(total, 1 - w, 1), "gw", 1).astype(f32)
    own = own.astype(bf16)
    total = pick(own, t, 0).astype(f32)
    for s in range(1, many):
        total = total + swap(pick(own, t ^ s, 0), "gt", s).astype(f32)
    return total


def sum_everywhere(value):
    for axis in ("co", "gw", "gt", "gx"):
        step = 1
        while step < lax.axis_size(axis):
            value = value + swap(value, axis, step)
            step = step * 2
    return value


def slot_mask(slot_row):
    wanted = lax.broadcasted_iota(jnp.int32, (CAP, slot_row.shape[1]), 0).astype(f32)
    return slot_row == wanted


def gather_slots(sources, order, slots):
    blocks, experts, tokens = slots.shape
    listed = isinstance(sources, list)
    width = sources[0].shape[1] if listed else order[1]

    def find(slots_ref, rows, out_ref):
        mask = jnp.concatenate([slot_mask(slots_ref[0, e : e + 1, :]) for e in range(experts)], axis=0)
        found = jnp.dot(mask.astype(f32).astype(bf16), rows, preferred_element_type=f32)
        out_ref[...] = found.astype(bf16).reshape(experts, 1, CAP, width)

    def kernel_list(order_ref, slots_ref, *refs):
        for i in range(blocks):

            @pl.when(pl.program_id(0) == i)
            def _(i=i):
                refs[blocks + 1][...] = refs[i][...]

        find(slots_ref, refs[blocks + 1][...], refs[blocks])

    def kernel_array(order_ref, slots_ref, rows_ref, out_ref):
        find(slots_ref, rows_ref[0], out_ref)

    if listed:
        specs = [pl.BlockSpec((tokens, width), lambda b, *_: (0, 0))] * blocks
        scratch = [pltpu.VMEM((tokens, width), bf16)]
        prefetch = jnp.zeros((1,), jnp.int32)
    else:
        specs = [pl.BlockSpec((1, tokens, width), lambda b, order_ref: (order_ref[b], 0, 0))]
        scratch = []
        prefetch = order[0]
        sources = [sources]
    return pl.pallas_call(
        kernel_list if listed else kernel_array,
        grid_spec=pltpu.PrefetchScalarGridSpec(
            num_scalar_prefetch=1,
            grid=(blocks,),
            in_specs=[pl.BlockSpec((1, experts, tokens), lambda b, *_: (b, 0, 0))] + specs,
            out_specs=pl.BlockSpec((experts, 1, CAP, width), lambda b, *_: (0, b, 0, 0)),
            scratch_shapes=scratch,
        ),
        out_shape=jax.ShapeDtypeStruct((experts, blocks, CAP, width), bf16),
        compiler_params=pltpu.CompilerParams(vmem_limit_bytes=40 * 2**20),
        cost_estimate=pl.CostEstimate(
            flops=2 * blocks * tokens * experts * CAP * width,
            bytes_accessed=2 * blocks * (tokens + experts * CAP) * width,
            transcendentals=0,
        ),
        name="gather_slots",
    )(prefetch, slots, *sources)


def sum_slots(slot_rows, slots, order):
    blocks, experts, tokens = slots.shape
    width = slot_rows[0].shape[3]

    def kernel(order_ref, slots_ref, *refs):
        total, first = None, 0
        for ref in refs[:-1]:
            mine = ref.shape[0]
            mask = jnp.concatenate(
                [slot_mask(slots_ref[0, e : e + 1, :]) for e in range(first, first + mine)], axis=0
            )
            first = first + mine
            part = contract_rows(mask.astype(f32).astype(bf16), ref[...].reshape(mine * CAP, width))
            total = part if total is None else total + part
        refs[-1][0] = total.astype(bf16)

    return pl.pallas_call(
        kernel,
        grid_spec=pltpu.PrefetchScalarGridSpec(
            num_scalar_prefetch=1,
            grid=(blocks,),
            in_specs=[pl.BlockSpec((1, experts, tokens), lambda b, *_: (b, 0, 0))]
            + [pl.BlockSpec((r.shape[0], 1, CAP, width), lambda b, *_: (0, b, 0, 0)) for r in slot_rows],
            out_specs=pl.BlockSpec((1, tokens, width), lambda b, order_ref: (order_ref[b], 0, 0)),
        ),
        out_shape=jax.ShapeDtypeStruct((blocks, tokens, width), bf16),
        compiler_params=pltpu.CompilerParams(vmem_limit_bytes=40 * 2**20),
        cost_estimate=pl.CostEstimate(
            flops=2 * blocks * tokens * experts * CAP * width,
            bytes_accessed=2 * blocks * (tokens + experts * CAP) * width,
            transcendentals=0,
        ),
        name="sum_slots",
    )(order, slots, *slot_rows)


def run_experts(rows_in, back_in, weights, start, slots, chances):
    blocks, _, width = rows_in.shape[1:]
    experts = weights[0].shape[0]
    places = part_places()
    tokens = slots.shape[2]
    cut, half = weights[0].shape[1], weights[0].shape[2] // 3
    count = len(places)
    total_slots = blocks * CAP

    def kernel(me_ref, rows_ref, back_ref, slots_ref, chances_ref, *refs):
        rows_out, mixed_out, chance_out = refs[count : count + 3]
        grads = refs[count + 3 : 2 * count + 3]
        gu_full, d_full, gu_total, d_total = refs[2 * count + 3 :]
        spots = [pl.ds(pl.multiple_of((me_ref[0] ^ place) * cut, cut), cut) for place in places]
        for spot, part in zip(spots, refs[:count]):
            gu_full[spot, :] = part[0, :, : 2 * half]
            d_full[spot, :] = part[0, :, 2 * half :]
        rows = rows_ref[0].reshape(total_slots, width)
        back = back_ref[0].reshape(total_slots, width)
        masks = [slot_mask(slots_ref[0, b : b + 1, :]) for b in range(blocks)]
        chance = jnp.concatenate(
            [
                jnp.sum(jnp.where(masks[b], chances_ref[0, b : b + 1, :], 0.0), axis=1, keepdims=True)
                for b in range(blocks)
            ],
            axis=0,
        )
        both = jnp.dot(rows, gu_full[...], preferred_element_type=f32)
        active_back = jnp.dot(back, d_full[...], preferred_element_type=f32) * residual_factor
        gate, upper = both[:, :half], both[:, half:]
        sigma = jax.nn.sigmoid(gate)
        silu = gate * sigma
        active = silu * upper
        chance_back = jnp.sum(active * active_back, axis=1, keepdims=True)
        for b in range(blocks):
            column = chance_back[b * CAP : (b + 1) * CAP]
            chance_out[0, b : b + 1, :] = jnp.sum(jnp.where(masks[b], column, 0.0), axis=0, keepdims=True)
        scaled = (active * chance).astype(bf16)
        active_back = active_back * chance
        gate_back = active_back * upper * (sigma * (1.0 + gate * (1.0 - sigma)))
        upper_back = active_back * silu
        both_back = jnp.concatenate([gate_back.astype(bf16), upper_back.astype(bf16)], axis=1)
        rows_out[0] = contract_cols(both_back, gu_full[...]).astype(bf16).reshape(blocks, CAP, width)
        mixed_out[0] = contract_cols(scaled, d_full[...]).astype(bf16).reshape(blocks, CAP, width)
        gu_total[...] = contract_rows(rows, both_back).astype(bf16)
        d_total[...] = (contract_rows(back, scaled) * residual_factor).astype(bf16)
        for spot, grad in zip(spots, grads):
            grad[0, :, : 2 * half] = gu_total[spot, :]
            grad[0, :, 2 * half :] = d_total[spot, :]

    def block(shape, first=0):
        zeros = (0,) * len(shape)
        return pl.BlockSpec((1,) + shape, lambda e, *_: (e + first,) + zeros)

    flops = 2 * experts * total_slots * width * half * 9
    grad_shape = jax.ShapeDtypeStruct((experts, cut, 3 * half), bf16)
    slot_shape = jax.ShapeDtypeStruct((experts, blocks, CAP, width), bf16)
    out = pl.pallas_call(
        kernel,
        grid_spec=pltpu.PrefetchScalarGridSpec(
            num_scalar_prefetch=1,
            grid=(experts,),
            in_specs=[
                block((blocks, CAP, width), start),
                block((blocks, CAP, width), start),
                block((blocks, tokens), start),
                block((blocks, tokens), start),
            ]
            + [block((cut, 3 * half))] * count,
            out_specs=[block((blocks, CAP, width)), block((blocks, CAP, width)), block((blocks, tokens))]
            + [block((cut, 3 * half))] * count,
            scratch_shapes=[
                pltpu.VMEM((width, 2 * half), bf16),
                pltpu.VMEM((width, half), bf16),
                pltpu.VMEM((width, 2 * half), bf16),
                pltpu.VMEM((width, half), bf16),
            ],
        ),
        out_shape=[slot_shape, slot_shape, jax.ShapeDtypeStruct((experts, blocks, tokens), f32)]
        + [grad_shape] * count,
        compiler_params=pltpu.CompilerParams(vmem_limit_bytes=60 * 2**20),
        cost_estimate=pl.CostEstimate(
            flops=flops,
            bytes_accessed=2 * experts * (4 * total_slots * width + 6 * half * width),
            transcendentals=experts * total_slots * half,
        ),
        name="run_experts",
    )(own_place(), rows_in, back_in, slots, chances, *weights)
    gradients = {(p // 4, (p // 2) % 2, p % 2): g for p, g in zip(places, out[3:])}
    return out[0], out[1], out[2], gradients


def block_scores(query_rows, key_rows, positions):
    raw = jnp.einsum("qhgd,khd->hgqk", query_rows, key_rows, preferred_element_type=f32)
    return jnp.where(positions[None, :] <= positions[:, None], raw * score_factor, masked_value)


def attend_forward(query_rows, key_rows, value_rows, positions):
    scores = block_scores(query_rows, key_rows, positions)
    top = jnp.max(scores, axis=-1, keepdims=True)
    weights = jnp.exp(scores - top)
    total = jnp.sum(weights, axis=-1, keepdims=True)
    probs = (weights / total).astype(bf16)
    mixed = jnp.einsum("hgqk,khd->qhgd", probs, value_rows, preferred_element_type=f32)
    return (mixed.astype(bf16).reshape(query_rows.shape[0], -1), top + jnp.log(total))


def attend_backward(query_rows, key_rows, value_rows, heads_back, spread, positions):
    scores = block_scores(query_rows, key_rows, positions)
    probs = jnp.exp(scores - spread)
    prob_back = jnp.einsum("qhgd,khd->hgqk", heads_back, value_rows, preferred_element_type=f32)
    inner = jnp.sum(probs * prob_back, axis=-1, keepdims=True)
    score_back = (probs * (prob_back - inner)).astype(bf16)
    query_back = jnp.einsum("hgqk,khd->qhgd", score_back, key_rows, preferred_element_type=f32)
    key_back = jnp.einsum("hgqk,qhgd->khd", score_back, query_rows, preferred_element_type=f32)
    value_back = jnp.einsum(
        "hgqk,qhgd->khd", probs.astype(bf16), heads_back, preferred_element_type=f32
    )
    return (query_back * score_factor, key_back * score_factor, value_back)


def local(
    tokens,
    first_gain,
    query_weight,
    key_matrix,
    value_matrix,
    out_weight,
    second_gain,
    gate_weight,
    up_weight,
    down_weight,
    routes,
    route_logits,
    cotangent,
):
    groups, many = lax.axis_size("gx"), lax.axis_size("gt")
    me_x, me_w = lax.axis_index("gx"), lax.axis_index("gw")
    own_tokens = tokens[0]
    rows, width = own_tokens.shape
    query_cols = query_weight.shape[1]
    key_cols = key_matrix.shape[1]
    query_heads = query_cols // HEAD_SIZE
    pair_heads = key_cols // HEAD_SIZE
    ratio = query_heads // pair_heads
    experts = gate_weight.shape[0]
    some = (experts + 1) // 2
    spans = ((0, some), (some, experts - some))

    token_blocks = gather_gx(own_tokens)
    attention = jnp.concatenate(
        [query_weight, key_matrix, value_matrix, out_weight.T], axis=1
    )
    down_turned = jnp.swapaxes(down_weight, 1, 2)
    (keep_0, give_0), (keep_1, give_1) = [
        halve_weights(gate_weight, up_weight, down_turned, *span) for span in spans
    ]
    across = swap(attention, "gw", 1)
    along = over_y(attention)
    both = over_y(across)
    across, give_0 = tie(across, give_0)
    both, keep_0, keep_1 = tie(both, keep_0, keep_1)
    attention_parts = [attention, across] + along + both
    attention_full = place_parts(attention_parts + [swap(p, "co", 1) for p in attention_parts])
    attention_full = attention_full.reshape(width, -1)
    joined = attention_full[:, : query_cols + 2 * key_cols]
    out_full = attention_full[:, query_cols + 2 * key_cols :]

    across_0, along_0 = swap(give_0, "gw", 1), over_y(keep_0)
    mirror_keep = [swap(keep_0, "co", 1), swap(keep_1, "co", 1)]

    logits = route_logits[0].T
    weights = jnp.exp(logits - jnp.max(logits, axis=0, keepdims=True))
    chance = weights / jnp.sum(weights, axis=0, keepdims=True)
    chance_high = lax.reduce_precision(chance, 8, 7)
    routing = jnp.concatenate([routes[0].T.astype(f32), chance_high, chance - chance_high], axis=0)
    routing = jnp.pad(routing.astype(bf16).T, ((0, 0), (0, 128 - 3 * TOPK)))
    payload = jnp.concatenate([cotangent[0], routing], axis=1)
    payload, token_blocks = tie(payload, token_blocks)
    turned = jnp.stack([((me_x ^ s) * 2 + (me_w ^ w)) for w in range(2) for s in range(groups)])
    gathered = lax.all_gather(payload, ("gx", "gw"), axis=0)

    sequence = jnp.concatenate(token_blocks, axis=0).astype(f32)
    length = sequence.shape[0]
    factor_all = rms_factor(sequence)
    sequence_rows = (sequence * factor_all * first_gain).astype(bf16)
    projected = jnp.dot(sequence_rows, joined, preferred_element_type=f32)
    positions = jnp.concatenate(
        [(me_x ^ s) * rows + jnp.arange(rows, dtype=jnp.int32) for s in range(groups)]
    )
    freq = rope_base ** (-(jnp.arange(HEAD_SIZE // 2, dtype=f32) * 2.0 / HEAD_SIZE))
    angle = positions.astype(f32)[:, None] * freq[None, :]
    cosine = jnp.cos(angle)[:, None, :]
    sine = jnp.sin(angle)[:, None, :]
    query_rows = rotary(projected[:, :query_cols].reshape(length, query_heads, HEAD_SIZE), cosine, sine)
    query_rows = query_rows.astype(bf16).reshape(length, pair_heads, ratio, HEAD_SIZE)
    key_rows = rotary(
        projected[:, query_cols : query_cols + key_cols].reshape(length, pair_heads, HEAD_SIZE),
        cosine,
        sine,
    ).astype(bf16)
    value_rows = (
        projected[:, query_cols + key_cols :].reshape(length, pair_heads, HEAD_SIZE).astype(bf16)
    )
    heads, spread = attend_forward(query_rows, key_rows, value_rows, positions)
    branch_parts = contract_cols(heads, out_full).astype(bf16)

    branch_parts, across_0, along_0, mirror_keep, keep_1, give_1 = tie(
        branch_parts, across_0, along_0, mirror_keep, keep_1, give_1
    )
    branch_got = [
        swap(branch_parts[s * rows : (s + 1) * rows], "gx", s) for s in range(1, groups)
    ]
    across_1, along_1 = swap(give_1, "gw", 1), over_y(keep_1)
    branch_got[0], branch_got[-1], across_0, along_0 = tie(
        branch_got[0], branch_got[-1], across_0, along_0
    )
    mirror_across = [swap(across_0, "co", 1)]
    mirror_along = [[swap(p, "co", 1) for p in along_0]]
    branch = branch_parts[:rows].astype(f32)
    for value in branch_got:
        branch = branch + value.astype(f32)

    routing_rows = jnp.swapaxes(gathered[:, :, width : width + 3 * TOPK].astype(f32), 1, 2)
    routing_rows = jnp.stack([pick(routing_rows, turned[b], 0) for b in range(2 * groups)])
    ids = (me_x * experts + jnp.arange(experts, dtype=jnp.int32)).astype(f32)
    same = routing_rows[:, None, :TOPK, :] == ids[None, :, None, None]
    chances = routing_rows[:, TOPK : 2 * TOPK] + routing_rows[:, 2 * TOPK :]
    hits = jnp.sum(same.astype(f32), axis=2)
    before = jnp.triu(jnp.ones((rows, rows), f32), 1)
    slots = jnp.where(hits > 0.0, jnp.einsum("beu,ut->bet", hits, before), -1.0)
    chosen = jnp.sum(jnp.where(same, chances[:, None], 0.0), axis=2)
    back_in = gather_slots(gathered, (turned, width), slots)

    hidden = own_tokens.astype(f32)
    middle = hidden + residual_factor * branch
    factor_two = rms_factor(middle)
    normed_two = (middle * factor_two * second_gain).astype(bf16)

    normed_two, back_in, across_0, across_1, along_1, mirror_across, mirror_along = tie(
        normed_two, back_in, across_0, across_1, along_1, mirror_across, mirror_along
    )
    normed_parts = gather_gx(normed_two)
    both_0 = over_y(across_0)
    normed_rows = normed_parts + [swap(p, "gw", 1) for p in normed_parts]

    normed_rows[:groups], both_0, across_1, along_1 = tie(normed_rows[:groups], both_0, across_1, along_1)
    both_1 = over_y(across_1)
    mirror_both = [[swap(p, "co", 1) for p in both_0]]
    mirror_across.append(swap(across_1, "co", 1))
    mirror_along.append([swap(p, "co", 1) for p in along_1])
    mirror_both.append([swap(p, "co", 1) for p in both_1])
    rows_in = gather_slots(normed_rows, None, slots)
    by_expert = (jnp.swapaxes(slots, 0, 1), jnp.swapaxes(chosen, 0, 1))
    rows_back, mixed_parts, chance_parts, gradients = [], [], [], []
    for i, own in enumerate(
        ([keep_0, across_0] + along_0 + both_0, [keep_1, across_1] + along_1 + both_1)
    ):
        mirrors = [mirror_keep[i], mirror_across[i]] + mirror_along[i] + mirror_both[i]
        result = run_experts(rows_in, back_in, own + mirrors, spans[i][0], *by_expert)
        for lot, value in zip((rows_back, mixed_parts, chance_parts, gradients), result):
            lot.append(value)

    got = [{}, {}]

    def joint(i, t, w):
        return gradients[i][t, w, 0].astype(f32) + got[i][t, w].astype(f32)

    others = range(1, many)
    got[0] = {(t, w): swap(gradients[0][t, w, 1], "co", 1) for t in range(many) for w in (0, 1)}
    got[0], rows_back = tie(got[0], rows_back)
    got[1] = {(t, 1): swap(gradients[1][t, 1, 1], "co", 1) for t in others}
    plain = jnp.arange(2 * groups, dtype=jnp.int32)
    summed = sum_slots(rows_back, slots, plain)
    order = [s for s in (2, 3, 1) if s < groups] + list(range(4, groups)) + [0]
    crossed = {s: swap(summed[groups + s], "gw", 1) for s in order}
    far = [joint(0, t, 1).astype(bf16) for t in others]
    crossed[order[0]], far, got[1], mixed_parts = tie(crossed[order[0]], far, got[1], mixed_parts)
    along_one_0 = spread_y(far)
    mixed_rows = sum_slots(mixed_parts, slots, turned)
    chance_part = jnp.swapaxes(jnp.concatenate(chance_parts, axis=0), 0, 1)
    chance_rows = jnp.sum(jnp.where(same, chance_part[:, :, None, :], 0.0), axis=1)
    normed_got = [
        swap((summed[s].astype(f32) + crossed[s].astype(f32)).astype(bf16), "gx", s)
        for s in range(1, groups)
    ]
    near_gradient = gradients[1][0, 1, 1]
    crossed[0], mixed_rows, near_gradient, chance_rows = tie(crossed[0], mixed_rows, near_gradient, chance_rows)
    got[1][0, 1] = swap(near_gradient, "co", 1)
    chance_crossed = swap(chance_rows[groups:], "gw", 1)
    far = [joint(1, t, 1).astype(bf16) for t in others]
    mixed = lax.psum_scatter(mixed_rows, ("gx", "gw"), scatter_dimension=0).astype(f32)
    output = (middle + residual_factor * mixed).astype(bf16)
    normed_two_back = summed[0].astype(f32) + crossed[0].astype(f32)
    for value in normed_got:
        normed_two_back = normed_two_back + value.astype(f32)

    upstream = cotangent[0].astype(f32)
    middle_back = upstream + norm_back(middle, factor_two, second_gain, normed_two_back)
    second_part = jnp.sum(normed_two_back * middle * factor_two, axis=0)
    branch_back = (residual_factor * middle_back).astype(bf16)
    branch_back, along_one_0, got[1], far, chance_crossed = tie(
        branch_back, along_one_0, got[1], far, chance_crossed
    )
    branch_back_blocks = gather_gx(branch_back)
    along_one_1 = spread_y(far)

    def near(i, along):
        total = joint(i, 0, 1)
        for value in along:
            total = total + value.astype(f32)
        return total.astype(bf16)

    crossed_0 = swap(near(0, along_one_0), "gw", 1)
    far = [joint(0, t, 0).astype(bf16) for t in others]
    last = {(t, 0): gradients[1][t, 0, 1] for t in range(many)}
    branch_back_blocks, along_one_1, crossed_0, far, last = tie(
        branch_back_blocks, along_one_1, crossed_0, far, last
    )
    along_zero_0 = spread_y(far)
    crossed_1 = swap(near(1, along_one_1), "gw", 1)
    got[1].update({p: swap(v, "co", 1) for p, v in last.items()})

    piece = jnp.concatenate(branch_back_blocks, axis=0)
    heads_back = jnp.dot(piece, out_full, preferred_element_type=f32)
    out_grad = contract_rows(piece, heads)
    heads_back = heads_back.astype(bf16).reshape(length, pair_heads, ratio, HEAD_SIZE)
    query_back, key_back, value_back = attend_backward(
        query_rows, key_rows, value_rows, heads_back, spread, positions
    )
    query_back = rotary(query_back.reshape(length, query_heads, HEAD_SIZE), cosine, -sine)
    key_back = rotary(key_back, cosine, -sine)
    projected_back = jnp.concatenate(
        [
            query_back.reshape(length, query_cols),
            key_back.reshape(length, key_cols),
            value_back.reshape(length, key_cols),
        ],
        axis=1,
    ).astype(bf16)
    normed_one_parts = contract_cols(projected_back, joined)
    first_part = jnp.sum(normed_one_parts * (sequence * factor_all), axis=0)
    normed_one_parts = normed_one_parts.astype(bf16)
    normed_one_parts, got[1] = tie(normed_one_parts, got[1])
    normed_got = [
        swap(normed_one_parts[s * rows : (s + 1) * rows], "gx", s) for s in range(1, groups)
    ]
    far = [joint(1, t, 0).astype(bf16) for t in others]
    along_zero_0, far = tie(along_zero_0, far)
    along_zero_1 = spread_y(far)
    joined_grad = contract_rows(sequence_rows, projected_back)
    attention_sum = scatter_gy(jnp.concatenate([joined_grad, out_grad], axis=1).astype(bf16))
    gains = jnp.stack([first_part, second_part])
    gains, normed_got, chance_rows = tie(gains, normed_got, chance_rows)
    gains = sum_everywhere(gains)
    normed_one_back = normed_one_parts[:rows].astype(f32)
    for value in normed_got:
        normed_one_back = normed_one_back + value.astype(f32)
    tokens_back = middle_back + norm_back(hidden, factor_all[:rows], first_gain, normed_one_back)
    chance_rows = chance_rows[:groups] + chance_crossed
    chance_back = chance_rows[0]
    for s in range(1, groups):
        chance_back = chance_back + swap(chance_rows[s], "gx", s)
    logit_back = chance * (chance_back - jnp.sum(chance * chance_back, axis=0, keepdims=True))
    sums = finish_gradients(
        [gradients[0][0, 0, 0], got[0][0, 0]] + along_zero_0, crossed_0, 0, None, experts
    )
    gate_sum, up_sum, down_sum = finish_gradients(
        [gradients[1][0, 0, 0], got[1][0, 0]] + along_zero_1, crossed_1, some, sums, experts
    )
    return (
        output[None],
        tokens_back[None],
        gains[0],
        attention_sum[:, :query_cols],
        attention_sum[:, query_cols : query_cols + key_cols],
        attention_sum[:, query_cols + key_cols : query_cols + 2 * key_cols],
        attention_sum[:, query_cols + 2 * key_cols :].T,
        gains[1],
        gate_sum,
        up_sum,
        jnp.swapaxes(down_sum, 1, 2),
        logit_back.T[None],
    )


def solution(mesh):
    groups, others = mesh.shape["gx"], mesh.shape["gy"]
    split = Mesh(mesh.devices.reshape(groups, others // 4, 2, 2), ("gx", "gt", "gw", "co"))
    gy = ("gt", "gw", "co")
    in_specs = (
        P(gy, "gx", None),
        P(),
        P(gy, "gx"),
        P(gy, "gx"),
        P(gy, "gx"),
        P("gx", gy),
        P(),
        P("gx", gy, None),
        P("gx", gy, None),
        P("gx", None, gy),
        P(gy, "gx", None),
        P(gy, "gx", None),
        P(gy, "gx", None),
    )
    out_specs = (
        P(gy, "gx", None),
        P(gy, "gx", None),
        P(),
        P(gy, "gx"),
        P(gy, "gx"),
        P(gy, "gx"),
        P("gx", gy),
        P(),
        P("gx", gy, None),
        P("gx", gy, None),
        P("gx", None, gy),
        P(gy, "gx", None),
    )
    return jax.shard_map(local, mesh=split, in_specs=in_specs, out_specs=out_specs, check_vma=False)
```

```python
import functools

import jax
import jax.numpy as jnp
from jax import lax
from jax.experimental import pallas as pl
from jax.experimental.pallas import tpu as pltpu
from jax.sharding import Mesh, PartitionSpec as P

HEAD_SIZE = 64
EXPERTS = 40
TOPK = 8
CAP = 48

epsilon = 1e-06
rope_base = 10000.0
residual_factor = 0.22
score_factor = 0.015625
masked_value = -1e30

SMALL_COST = pl.CostEstimate(flops=1, bytes_accessed=1, transcendentals=0)
LARGE_COST = pl.CostEstimate(flops=10**10, bytes_accessed=10**8, transcendentals=0)

f32 = jnp.float32
bf16 = jnp.bfloat16


def swap(value, axis, step):
    count = lax.axis_size(axis)
    return lax.ppermute(value, axis, [(i, i ^ step) for i in range(count)])


def tie(*values):
    return lax.optimization_barrier(values)


def pick(array, index, dim):
    return lax.dynamic_index_in_dim(array, index, dim, keepdims=False)


def rms_factor(rows):
    return lax.rsqrt(jnp.mean(rows * rows, axis=-1, keepdims=True) + epsilon)


def norm_back(rows, factor, gain, upstream):
    scaled = upstream * gain
    inner = jnp.mean(scaled * rows, axis=-1, keepdims=True)
    return factor * scaled - rows * factor * factor * factor * inner


def contract_rows(left, right):
    return lax.dot_general(left, right, (((0,), (0,)), ((), ())), preferred_element_type=f32)


def contract_cols(left, right):
    return lax.dot_general(left, right, (((1,), (1,)), ((), ())), preferred_element_type=f32)


def gather_gx(block):
    return [block] + [swap(block, "gx", s) for s in range(1, lax.axis_size("gx"))]


def over_y(value):
    return [swap(value, "gt", s) for s in range(1, lax.axis_size("gt"))]


def spread_y(values):
    return [swap(value, "gt", s) for s, value in enumerate(values, 1)]


def part_places():
    many = lax.axis_size("gt")
    places = [0, 2] + [4 * s for s in range(1, many)] + [4 * s + 2 for s in range(1, many)]
    return places + [p + 1 for p in places]


def own_place():
    me = (lax.axis_index("gt") * 2 + lax.axis_index("gw")) * 2 + lax.axis_index("co")
    return jnp.full((1,), me, jnp.int32)


def own_side():
    return jnp.full((1,), lax.axis_index("gw"), jnp.int32)


def halve_weights(gate, up, down):
    experts, rows, full = gate.shape
    half = full // 2

    def kernel(side_ref, gate_ref, up_ref, down_ref, keep, give):
        def put(low, out):
            for i, ref in enumerate((gate_ref, up_ref, down_ref)):
                out[0, :, i * half : (i + 1) * half] = ref[0, :, low : low + half]

        @pl.when(side_ref[0] == 0)
        def _():
            put(0, keep)
            put(half, give)

        @pl.when(side_ref[0] != 0)
        def _():
            put(half, keep)
            put(0, give)

    def block(columns):
        return pl.BlockSpec((1, rows, columns), lambda e, *_: (e, 0, 0))

    shape = jax.ShapeDtypeStruct((experts, rows, 3 * half), bf16)
    return pl.pallas_call(
        kernel,
        grid_spec=pltpu.PrefetchScalarGridSpec(
            num_scalar_prefetch=1,
            grid=(experts,),
            in_specs=[block(full)] * 3,
            out_specs=[block(3 * half)] * 2,
        ),
        out_shape=[shape, shape],
        cost_estimate=LARGE_COST,
        name="halve_weights",
    )(own_side(), gate, up, down)


def finish_gradients(summed, crossed, start, before, total_experts):
    experts, rows, columns = crossed.shape
    half = columns // 3
    count = len(summed)
    aliased = 0 if before is None else 3

    def kernel(side_ref, *refs):
        total = 0.0
        for ref in refs[:count]:
            total = total + (ref[0, 0] if len(ref.shape) == 4 else ref[0]).astype(f32)
        other = refs[count][0].astype(f32)

        def put(low, value):
            for i, out in enumerate(refs[count + 1 + aliased :]):
                out[0, :, low : low + half] = value[:, i * half : (i + 1) * half]

        @pl.when(side_ref[0] == 0)
        def _():
            put(0, total)
            put(half, other)

        @pl.when(side_ref[0] != 0)
        def _():
            put(half, total)
            put(0, other)

    def block(columns, first):
        return pl.BlockSpec((1, rows, columns), lambda e, *_: (e + first, 0, 0))

    shape = jax.ShapeDtypeStruct((total_experts, rows, 2 * half), f32)
    return pl.pallas_call(
        kernel,
        grid_spec=pltpu.PrefetchScalarGridSpec(
            num_scalar_prefetch=1,
            grid=(experts,),
            in_specs=[
                pl.BlockSpec((1, 1, rows, columns), lambda e, *_: (0, e, 0, 0)) if v.ndim == 4 else block(columns, 0)
                for v in summed
            ]
            + [block(columns, 0)]
            + [pl.BlockSpec(memory_space=pl.ANY)] * aliased,
            out_specs=[block(2 * half, start)] * 3,
        ),
        out_shape=[shape] * 3,
        input_output_aliases={count + 2 + i: i for i in range(aliased)},
        cost_estimate=SMALL_COST,
        name="finish_gradients",
    )(own_side(), *summed, crossed, *(before or ()))


def scatter_gy(keep, got):
    many = lax.axis_size("gt")
    send = (keep[1::2].astype(f32) + got[1::2].astype(f32)).astype(bf16)
    got_w = swap(send, "gw", 1)
    total = keep[0::2].astype(f32) + got[0::2].astype(f32) + got_w.astype(f32)
    own = total[0]
    for value in spread_y([total[t].astype(bf16) for t in range(1, many)]):
        own = own + value.astype(f32)
    return own


def sum_everywhere(value):
    value = value + swap(value, "co", 1)
    for axes in (("gt", "gw"), ("gx",)):
        count = lax.axis_size(axes)
        sent = [lax.ppermute(value, axes, [(i, i ^ s) for i in range(count)]) for s in range(1, count)]
        for got in sent:
            value = value + got
    return value


def slot_mask(slot_row):
    wanted = lax.broadcasted_iota(jnp.int32, (CAP, slot_row.shape[1]), 0).astype(f32)
    return slot_row == wanted


def route_slots(gathered, order, first_expert, experts, width):
    blocks, tokens = gathered.shape[:2]

    def kernel(order_ref, first_ref, routing_ref, routes_out, slots_out, chances_out, slots_by, chances_by):
        earlier = lax.broadcasted_iota(jnp.int32, (tokens, tokens), 0)
        earlier = (earlier < lax.broadcasted_iota(jnp.int32, (tokens, tokens), 1)).astype(f32).astype(bf16)
        for b in range(blocks):
            routing = routing_ref[order_ref[b]].astype(f32).T
            routes = routing[:TOPK]
            chance = routing[TOPK : 2 * TOPK] + routing[2 * TOPK : 3 * TOPK]
            routes_out[b] = routes
            hits, chosen = [], []
            for e in range(experts):
                same = routes == (first_ref[0] + e).astype(f32)
                hits.append(jnp.sum(jnp.where(same, 1.0, 0.0), axis=0, keepdims=True))
                chosen.append(jnp.sum(jnp.where(same, chance, 0.0), axis=0, keepdims=True))
            hits, chosen = jnp.concatenate(hits, axis=0), jnp.concatenate(chosen, axis=0)
            rank = jnp.dot(hits.astype(bf16), earlier, preferred_element_type=f32)
            slots = jnp.where(hits > 0.0, rank, -1.0)
            slots_out[b] = slots
            chances_out[b] = chosen
            for e in range(experts):
                slots_by[e, b : b + 1, :] = slots[e : e + 1]
                chances_by[e, b : b + 1, :] = chosen[e : e + 1]

    def whole(*shape):
        zeros = (0,) * len(shape)
        return pl.BlockSpec(shape, lambda i, *_: zeros)

    shapes = [(blocks, TOPK, tokens)] + [(blocks, experts, tokens)] * 2 + [(experts, blocks, tokens)] * 2
    return pl.pallas_call(
        kernel,
        grid_spec=pltpu.PrefetchScalarGridSpec(
            num_scalar_prefetch=2,
            grid=(1,),
            in_specs=[pl.BlockSpec((blocks, tokens, 128), lambda i, *_: (0, 0, width // 128))],
            out_specs=[whole(*shape) for shape in shapes],
        ),
        out_shape=[jax.ShapeDtypeStruct(shape, f32) for shape in shapes],
        cost_estimate=SMALL_COST,
        name="route_slots",
    )(order, jnp.full((1,), first_expert, jnp.int32), gathered)


def gather_slots(sources, order, slots):
    blocks, experts, tokens = slots.shape
    listed = isinstance(sources, list)
    width = sources[0].shape[1] if listed else order[1]

    def find(slots_ref, rows, out_ref):
        mask = jnp.concatenate([slot_mask(slots_ref[0, e : e + 1, :]) for e in range(experts)], axis=0)
        found = jnp.dot(mask.astype(f32).astype(bf16), rows, preferred_element_type=f32)
        out_ref[...] = found.astype(bf16).reshape(experts, 1, CAP, width)

    def kernel_list(order_ref, slots_ref, *refs):
        for i in range(blocks):

            @pl.when(pl.program_id(0) == i)
            def _(i=i):
                refs[blocks + 1][...] = refs[i][...]

        find(slots_ref, refs[blocks + 1][...], refs[blocks])

    def kernel_array(order_ref, slots_ref, rows_ref, out_ref):
        find(slots_ref, rows_ref[0], out_ref)

    if listed:
        specs = [pl.BlockSpec((tokens, width), lambda b, *_: (0, 0))] * blocks
        scratch = [pltpu.VMEM((tokens, width), bf16)]
        prefetch = jnp.zeros((1,), jnp.int32)
    else:
        specs = [pl.BlockSpec((1, tokens, width), lambda b, order_ref: (order_ref[b], 0, 0))]
        scratch = []
        prefetch = order[0]
        sources = [sources]
    return pl.pallas_call(
        kernel_list if listed else kernel_array,
        grid_spec=pltpu.PrefetchScalarGridSpec(
            num_scalar_prefetch=1,
            grid=(blocks,),
            in_specs=[pl.BlockSpec((1, experts, tokens), lambda b, *_: (b, 0, 0))] + specs,
            out_specs=pl.BlockSpec((experts, 1, CAP, width), lambda b, *_: (0, b, 0, 0)),
            scratch_shapes=scratch,
        ),
        out_shape=jax.ShapeDtypeStruct((experts, blocks, CAP, width), bf16),
        compiler_params=pltpu.CompilerParams(vmem_limit_bytes=40 * 2**20),
        cost_estimate=SMALL_COST,
        name="gather_slots",
    )(prefetch, slots, *sources)


def sum_slots(slot_rows, slots, order):
    blocks, experts, tokens = slots.shape
    width = slot_rows[0].shape[3]

    def kernel(order_ref, slots_ref, *refs):
        total, first = None, 0
        for ref in refs[:-1]:
            mine = ref.shape[0]
            mask = jnp.concatenate(
                [slot_mask(slots_ref[0, e : e + 1, :]) for e in range(first, first + mine)], axis=0
            )
            first = first + mine
            part = contract_rows(mask.astype(f32).astype(bf16), ref[...].reshape(mine * CAP, width))
            total = part if total is None else total + part
        refs[-1][0] = total.astype(bf16)

    return pl.pallas_call(
        kernel,
        grid_spec=pltpu.PrefetchScalarGridSpec(
            num_scalar_prefetch=1,
            grid=(blocks,),
            in_specs=[pl.BlockSpec((1, experts, tokens), lambda b, *_: (b, 0, 0))]
            + [pl.BlockSpec((r.shape[0], 1, CAP, width), lambda b, *_: (0, b, 0, 0)) for r in slot_rows],
            out_specs=pl.BlockSpec((1, tokens, width), lambda b, order_ref: (order_ref[b], 0, 0)),
        ),
        out_shape=jax.ShapeDtypeStruct((blocks, tokens, width), bf16),
        compiler_params=pltpu.CompilerParams(vmem_limit_bytes=40 * 2**20),
        cost_estimate=LARGE_COST,
        name="sum_slots",
    )(order, slots, *slot_rows)


def run_experts(rows_in, back_in, weights, start, experts, slots, chances):
    blocks, _, width = rows_in.shape[1:]
    places = part_places()
    tokens = slots.shape[2]
    cut, half = weights[0][0].shape[1], weights[0][0].shape[2] // 3
    count = len(places)
    total_slots = blocks * CAP

    def kernel(me_ref, rows_ref, back_ref, slots_ref, chances_ref, *refs):
        rows_out, mixed_out, chance_out = refs[count : count + 3]
        grads = refs[count + 3 : count + 5]
        gu_full, d_full, gu_total, d_total = refs[count + 5 :]
        spots = [pl.ds(pl.multiple_of((me_ref[0] ^ place) * cut, cut), cut) for place in places]
        for spot, part in zip(spots, refs[:count]):
            gu_full[spot, :] = part[0, :, : 2 * half]
            d_full[spot, :] = part[0, :, 2 * half :]
        rows = rows_ref[0].reshape(total_slots, width)
        back = back_ref[0].reshape(total_slots, width)
        masks = [slot_mask(slots_ref[0, b : b + 1, :]) for b in range(blocks)]
        chance = jnp.concatenate(
            [
                jnp.sum(jnp.where(masks[b], chances_ref[0, b : b + 1, :], 0.0), axis=1, keepdims=True)
                for b in range(blocks)
            ],
            axis=0,
        )
        both = jnp.dot(rows, gu_full[...], preferred_element_type=f32)
        active_back = jnp.dot(back, d_full[...], preferred_element_type=f32) * residual_factor
        gate, upper = both[:, :half], both[:, half:]
        sigma = jax.nn.sigmoid(gate)
        silu = gate * sigma
        active = silu * upper
        chance_back = jnp.sum(active * active_back, axis=1, keepdims=True)
        for b in range(blocks):
            column = chance_back[b * CAP : (b + 1) * CAP]
            chance_out[0, b : b + 1, :] = jnp.sum(jnp.where(masks[b], column, 0.0), axis=0, keepdims=True)
        scaled = (active * chance).astype(bf16)
        active_back = active_back * chance
        gate_back = active_back * upper * (sigma * (1.0 + gate * (1.0 - sigma)))
        upper_back = active_back * silu
        both_back = jnp.concatenate([gate_back.astype(bf16), upper_back.astype(bf16)], axis=1)
        rows_out[0] = contract_cols(both_back, gu_full[...]).astype(bf16).reshape(blocks, CAP, width)
        mixed_out[0] = contract_cols(scaled, d_full[...]).astype(bf16).reshape(blocks, CAP, width)
        gu_total[...] = contract_rows(rows, both_back).astype(bf16)
        d_total[...] = (contract_rows(back, scaled) * residual_factor).astype(bf16)
        for spot, place in zip(spots, places):
            grads[place % 2][place // 2, 0, :, : 2 * half] = gu_total[spot, :]
            grads[place % 2][place // 2, 0, :, 2 * half :] = d_total[spot, :]

    def block(shape, first=0):
        zeros = (0,) * len(shape)
        return pl.BlockSpec((1,) + shape, lambda e, *_: (e + first,) + zeros)

    grad_shape = jax.ShapeDtypeStruct((count // 2, experts, cut, 3 * half), bf16)
    slot_shape = jax.ShapeDtypeStruct((experts, blocks, CAP, width), bf16)
    out = pl.pallas_call(
        kernel,
        grid_spec=pltpu.PrefetchScalarGridSpec(
            num_scalar_prefetch=1,
            grid=(experts,),
            in_specs=[
                block((blocks, CAP, width), start),
                block((blocks, CAP, width), start),
                block((blocks, tokens), start),
                block((blocks, tokens), start),
            ]
            + [block((cut, 3 * half), first) for _, first in weights],
            out_specs=[block((blocks, CAP, width)), block((blocks, CAP, width)), block((blocks, tokens))]
            + [pl.BlockSpec((count // 2, 1, cut, 3 * half), lambda e, *_: (0, e, 0, 0))] * 2,
            scratch_shapes=[
                pltpu.VMEM((width, 2 * half), bf16),
                pltpu.VMEM((width, half), bf16),
                pltpu.VMEM((width, 2 * half), bf16),
                pltpu.VMEM((width, half), bf16),
            ],
        ),
        out_shape=[slot_shape, slot_shape, jax.ShapeDtypeStruct((experts, blocks, tokens), f32)]
        + [grad_shape] * 2,
        compiler_params=pltpu.CompilerParams(vmem_limit_bytes=60 * 2**20),
        cost_estimate=LARGE_COST,
        name="run_experts",
    )(own_place(), rows_in, back_in, slots, chances, *[w for w, _ in weights])
    return out


ATTENTION_PARAMS = pltpu.CompilerParams(vmem_limit_bytes=60 * 2**20)


def turned_half(x):
    lanes = lax.broadcasted_iota(jnp.int32, x.shape, 1) % HEAD_SIZE
    half = HEAD_SIZE // 2
    return jnp.where(lanes < half, -pltpu.roll(x, 128 - half, 1), pltpu.roll(x, half, 1))


def head(x, h):
    return x[:, h * HEAD_SIZE : (h + 1) * HEAD_SIZE]


def attention_forward(token_blocks, gain, parts, tables, query_cols, key_cols):
    blocks = len(token_blocks)
    rows, width = token_blocks[0].shape
    length = rows * blocks
    count = len(parts)
    places = part_places()
    columns = query_cols + 2 * key_cols
    heads = query_cols // HEAD_SIZE
    ratio = query_cols // key_cols
    step = 256

    def kernel(me_ref, gain_ref, cosine_ref, sine_ref, down_ref, along_ref, *refs):
        token_refs, part_refs = refs[:blocks], refs[blocks : blocks + count]
        full, normed, factors, qkv, heads_out, spread, branch = refs[blocks + count :]
        for place, ref in zip(places, part_refs):
            full[me_ref[0] ^ place] = ref[...]
        for s in range(blocks):
            x = token_refs[s][...].astype(f32)
            factor = rms_factor(x)
            span = slice(s * rows, (s + 1) * rows)
            factors[span, :] = factor
            normed[span, :] = (x * factor * gain_ref[...]).astype(bf16)
        weights = full[...].reshape(width, full.shape[2])
        projected = jnp.dot(normed[...], weights[:, :columns], preferred_element_type=f32)
        for g in range((query_cols + key_cols) // 128):
            span = slice(g * 128, (g + 1) * 128)
            x = projected[:, span]
            qkv[:, span] = (x * cosine_ref[...] + turned_half(x) * sine_ref[...]).astype(bf16)
        qkv[:, query_cols + key_cols :] = projected[:, query_cols + key_cols :].astype(bf16)
        for q in range(0, length, step):
            span = slice(q, q + step)
            mixed = []
            mask = along_ref[...] <= down_ref[span, :]
            query = qkv[span, :query_cols]
            for h in range(heads):
                key = head(qkv[:, query_cols : query_cols + key_cols], h // ratio)
                value = head(qkv[:, query_cols + key_cols :], h // ratio)
                scores = jnp.where(mask, contract_cols(head(query, h), key) * score_factor, masked_value)
                top = jnp.max(scores, axis=1, keepdims=True)
                exps = jnp.exp(scores - top)
                total = jnp.sum(exps, axis=1, keepdims=True)
                probs = (exps * (1.0 / total)).astype(bf16)
                mixed.append(jnp.dot(probs, value, preferred_element_type=f32).astype(bf16))
                spread[span, h : h + 1] = top + jnp.log(total)
            heads_out[span, :] = jnp.concatenate(mixed, axis=1)
        branch[...] = contract_cols(heads_out[...], weights[:, columns:]).astype(bf16)

    vmem = pl.BlockSpec(memory_space=pltpu.VMEM)
    return pl.pallas_call(
        kernel,
        out_shape=[
            jax.ShapeDtypeStruct((count,) + parts[0].shape, bf16),
            jax.ShapeDtypeStruct((length, width), bf16),
            jax.ShapeDtypeStruct((length, 1), f32),
            jax.ShapeDtypeStruct((length, columns), bf16),
            jax.ShapeDtypeStruct((length, query_cols), bf16),
            jax.ShapeDtypeStruct((length, heads), f32),
            jax.ShapeDtypeStruct((length, width), bf16),
        ],
        in_specs=[pl.BlockSpec(memory_space=pltpu.SMEM)] + [vmem] * (5 + blocks + count),
        out_specs=[vmem] * 7,
        compiler_params=ATTENTION_PARAMS,
        cost_estimate=SMALL_COST,
        name="attention_forward",
    )(own_place(), gain[None], *tables, *token_blocks, *parts)


def attention_backward(pieces, token_blocks, tables, full, factors, qkv, spread, query_cols, key_cols):
    blocks = len(pieces)
    rows, width = pieces[0].shape
    length = rows * blocks
    columns = query_cols + 2 * key_cols
    heads = query_cols // HEAD_SIZE
    pairs = key_cols // HEAD_SIZE
    ratio = heads // pairs
    step = 256

    def kernel(cosine_ref, sine_ref, down_ref, along_ref, full_ref, factors_ref, qkv_ref, spread_ref, *refs):
        piece_refs, token_refs = refs[:blocks], refs[blocks : 2 * blocks]
        back, normed_back, gain_back, heads_back, turned = refs[2 * blocks :]
        weights = full_ref[...].reshape(width, full_ref.shape[2])
        for s in range(blocks):
            part = jnp.dot(piece_refs[s][...], weights[:, columns:], preferred_element_type=f32)
            heads_back[s * rows : (s + 1) * rows, :] = part.astype(bf16)
        key_back, value_back = [None] * pairs, [None] * pairs

        def add(total, value):
            return value if total is None else total + value

        for q in range(0, length, step):
            span = slice(q, q + step)
            mask = along_ref[...] <= down_ref[span, :]
            query = qkv_ref[span, :query_cols]
            upper = heads_back[span, :]
            query_back = []
            for h in range(heads):
                g = h // ratio
                key = head(qkv_ref[:, query_cols : query_cols + key_cols], g)
                value = head(qkv_ref[:, query_cols + key_cols :], g)
                query_h, upper_h = head(query, h), head(upper, h)
                scores = jnp.where(mask, contract_cols(query_h, key) * score_factor, masked_value)
                probs = jnp.exp(scores - spread_ref[span, h : h + 1])
                prob_back = contract_cols(upper_h, value)
                inner = jnp.sum(probs * prob_back, axis=1, keepdims=True)
                score_back = (probs * (prob_back - inner)).astype(bf16)
                query_back.append(jnp.dot(score_back, key, preferred_element_type=f32) * score_factor)
                key_back[g] = add(key_back[g], contract_rows(score_back, query_h))
                value_back[g] = add(value_back[g], contract_rows(probs.astype(bf16), upper_h))
            turned[span, :query_cols] = jnp.concatenate(query_back, axis=1)
        turned[:, query_cols:] = jnp.concatenate(
            [k * score_factor for k in key_back] + value_back, axis=1
        )
        for g in range((query_cols + key_cols) // 128):
            span = slice(g * 128, (g + 1) * 128)
            x = turned[:, span]
            back[:, span] = (x * cosine_ref[...] - turned_half(x) * sine_ref[...]).astype(bf16)
        back[:, query_cols + key_cols :] = turned[:, query_cols + key_cols :].astype(bf16)
        total = None
        for s in range(blocks):
            span = slice(s * rows, (s + 1) * rows)
            part = contract_cols(back[span, :], weights[:, :columns])
            normed_back[s] = part.astype(bf16)
            scaled = part * (token_refs[s][...].astype(f32) * factors_ref[span, :])
            total = add(total, jnp.sum(scaled, axis=0, keepdims=True))
        gain_back[...] = total

    vmem = pl.BlockSpec(memory_space=pltpu.VMEM)
    return pl.pallas_call(
        kernel,
        out_shape=[
            jax.ShapeDtypeStruct((length, columns), bf16),
            jax.ShapeDtypeStruct((blocks, rows, width), bf16),
            jax.ShapeDtypeStruct((1, width), f32),
        ],
        in_specs=[vmem] * (8 + 2 * blocks),
        out_specs=[vmem] * 3,
        scratch_shapes=[pltpu.VMEM((length, query_cols), bf16), pltpu.VMEM((length, columns), f32)],
        compiler_params=ATTENTION_PARAMS,
        cost_estimate=LARGE_COST,
        name="attention_backward",
    )(*tables, full, factors, qkv, spread, *pieces, *token_blocks)


def attention_gradients(normed, back, pieces, heads):
    blocks = len(pieces)
    rows, width = pieces[0].shape
    columns = back.shape[1]
    both = columns + heads.shape[1]
    places = part_places()
    count = len(places)
    cut = width // count

    def kernel(me_ref, normed_ref, back_ref, heads_ref, *refs):
        keep, give, total = refs[blocks:]
        total[:, :columns] = contract_rows(normed_ref[...], back_ref[...]).astype(bf16)
        piece = jnp.concatenate([ref[...] for ref in refs[:blocks]], axis=0)
        total[:, columns:] = contract_rows(piece, heads_ref[...]).astype(bf16)
        for place in places:
            spot = pl.ds(pl.multiple_of((me_ref[0] ^ place) * cut, cut), cut)
            (give if place % 2 else keep)[place // 2] = total[spot, :]

    vmem = pl.BlockSpec(memory_space=pltpu.VMEM)
    shape = jax.ShapeDtypeStruct((count // 2, cut, both), bf16)
    return pl.pallas_call(
        kernel,
        out_shape=[shape, shape],
        in_specs=[pl.BlockSpec(memory_space=pltpu.SMEM)] + [vmem] * (3 + blocks),
        out_specs=[vmem] * 2,
        scratch_shapes=[pltpu.VMEM((width, both), bf16)],
        compiler_params=ATTENTION_PARAMS,
        cost_estimate=LARGE_COST,
        name="attention_gradients",
    )(own_place(), normed, back, heads, *pieces)


def local(
    tokens,
    first_gain,
    query_weight,
    key_matrix,
    value_matrix,
    out_weight,
    second_gain,
    gate_weight,
    up_weight,
    down_weight,
    routes,
    route_logits,
    cotangent,
):
    groups, many = lax.axis_size("gx"), lax.axis_size("gt")
    me_x, me_w = lax.axis_index("gx"), lax.axis_index("gw")
    own_tokens = tokens[0]
    rows, width = own_tokens.shape
    query_cols = query_weight.shape[1]
    key_cols = key_matrix.shape[1]
    query_heads = query_cols // HEAD_SIZE
    pair_heads = key_cols // HEAD_SIZE
    ratio = query_heads // pair_heads
    experts = gate_weight.shape[0]
    some = experts * 2 // 5
    spans = ((0, some), (some, experts - some))

    token_blocks = gather_gx(own_tokens)
    attention = jnp.concatenate(
        [query_weight, key_matrix, value_matrix, out_weight.T], axis=1
    )
    across = swap(attention, "gw", 1)
    along = over_y(attention)
    both = over_y(across)
    down_turned = jnp.swapaxes(down_weight, 1, 2)
    keep, give = halve_weights(gate_weight, up_weight, down_turned)
    across, give = tie(across, give)
    attention_parts = [attention, across] + along + both
    attention_parts, keep = tie(attention_parts, keep)
    token_blocks, attention_parts, keep_sent = tie(token_blocks, attention_parts, keep)
    attention_parts = attention_parts + [swap(p, "co", 1) for p in attention_parts]

    given_across, given_along = swap(give, "gw", 1), over_y(keep)
    mirror_keep = swap(keep_sent, "co", 1)

    logits = route_logits[0].T
    weights = jnp.exp(logits - jnp.max(logits, axis=0, keepdims=True))
    chance = weights / jnp.sum(weights, axis=0, keepdims=True)
    chance_high = lax.reduce_precision(chance, 8, 7)
    routing = jnp.concatenate([routes[0].T.astype(f32), chance_high, chance - chance_high], axis=0)
    routing = jnp.pad(routing.astype(bf16).T, ((0, 0), (0, 128 - 3 * TOPK)))
    payload = jnp.concatenate([cotangent[0], routing], axis=1)
    payload, token_blocks = tie(payload, token_blocks)
    turned = jnp.stack([w * groups + (me_x ^ s) for w in range(2) for s in range(groups)])
    gathered = lax.all_gather(payload, "gx", axis=0)

    positions = jnp.concatenate(
        [(me_x ^ s) * rows + jnp.arange(rows, dtype=jnp.int32) for s in range(groups)]
    ).astype(f32)
    half = HEAD_SIZE // 2
    freq = rope_base ** (-(jnp.arange(half, dtype=f32) * 2.0 / HEAD_SIZE))
    angle = positions[:, None] * jnp.tile(freq, 128 // half)[None, :]
    tables = (jnp.cos(angle), jnp.sin(angle), positions[:, None], positions[None, :])
    attention_full, normed_one, factor_all, qkv, heads, spread, branch_parts = attention_forward(
        token_blocks, first_gain, attention_parts, tables, query_cols, key_cols
    )

    branch_parts, mirror_keep = tie(branch_parts, mirror_keep)
    branch_got = [
        swap(branch_parts[s * rows : (s + 1) * rows], "gx", s) for s in range(1, groups)
    ]
    given_across, gathered, branch_got[0] = tie(given_across, gathered, branch_got[0])
    gathered_across = swap(gathered, "gw", 1)
    branch = branch_parts[:rows].astype(f32)
    for value in branch_got:
        branch = branch + value.astype(f32)

    hidden = own_tokens.astype(f32)
    middle = hidden + residual_factor * branch
    factor_two = rms_factor(middle)
    normed_two = (middle * factor_two * second_gain).astype(bf16)

    normed_two, given_across, given_along = tie(normed_two, given_across, given_along)
    normed_parts = gather_gx(normed_two)
    both_0 = over_y(given_across[:some])
    turned_parts = {s: swap(normed_parts[s], "gw", 1) for s in (0, 1)}

    gathered = jnp.concatenate([gathered, gathered_across])
    routes_of, slots, _, slots_by, chances_by = route_slots(gathered, turned, me_x * experts, experts, width)
    back_in = gather_slots(gathered, (turned, width), slots)
    normed_parts, turned_parts[0], turned_parts[1], both_0, given_across, given_along, back_in = tie(
        normed_parts, turned_parts[0], turned_parts[1], both_0, given_across, given_along, back_in
    )

    rest = [s for s in range(groups) if s not in (0, 1)]
    turned_rest = swap(jnp.stack([normed_parts[s] for s in rest]), "gw", 1)
    both_1 = over_y(given_across[some:])
    mirror_given = [swap(v, "co", 1) for v in [given_across] + given_along]
    mirror_both_0 = [swap(v, "co", 1) for v in both_0]
    normed_rows = normed_parts + [turned_parts[0], turned_parts[1]]
    normed_rows = normed_rows + [turned_rest[i] for i in range(len(rest))]
    rows_in = gather_slots(normed_rows, None, slots)
    rows_back, mixed_parts, chance_parts, gradients, given = [], [], [], [], []
    for i, (start, size) in enumerate(spans):
        if i == 0:
            both, mirror_both = both_0, mirror_both_0
        else:
            rows_in, rows_back[0], both_1 = tie(rows_in, rows_back[0], both_1)
            both, mirror_both = both_1, [swap(v, "co", 1) for v in both_1]
        parts = [(v, start) for v in [keep, given_across] + given_along] + [(v, 0) for v in both]
        parts = parts + [(v, start) for v in [mirror_keep] + mirror_given] + [(v, 0) for v in mirror_both]
        result = run_experts(rows_in, back_in, parts, start, size, slots_by, chances_by)
        for lot, value in zip((rows_back, mixed_parts, chance_parts, gradients, given), result):
            lot.append(value)

    got = [None, None]

    def joint(i, t, w):
        return gradients[i][2 * t + w].astype(f32) + got[i][2 * t + w].astype(f32)

    others = range(1, many)
    got[0] = swap(given[0], "co", 1)
    got[0], rows_back = tie(got[0], rows_back)
    got[1] = swap(given[1], "co", 1)
    far = [joint(0, t, 1).astype(bf16) for t in others]
    far, rows_back = tie(far, rows_back)
    along_one_0 = spread_y(far)
    plain = jnp.arange(2 * groups, dtype=jnp.int32)
    summed = sum_slots(rows_back, slots, plain)
    pieces = ((2, groups), (0, 2))
    crossed = [swap(summed[groups + a : groups + b], "gw", 1) for a, b in pieces]
    far = [joint(1, t, 1).astype(bf16) for t in others]
    crossed[1], along_one_0, far, got[1] = tie(crossed[1], along_one_0, far, got[1])
    along_one_1 = spread_y(far)

    def half_sum(s):
        a, b = pieces[0] if s >= 2 else pieces[1]
        value = crossed[0] if s >= 2 else crossed[1]
        return summed[s].astype(f32) + value[s - a].astype(f32)

    normed_got = {s: swap(half_sum(s).astype(bf16), "gx", s) for s in range(2, groups)}
    normed_got[1] = swap(half_sum(1).astype(bf16), "gx", 1)
    normed_got[3], mixed_parts = tie(normed_got[3], mixed_parts)
    mixed_rows = sum_slots(mixed_parts, slots, plain)
    chance_part = jnp.swapaxes(jnp.concatenate(chance_parts, axis=0), 0, 1)
    ids = (me_x * experts + jnp.arange(experts, dtype=jnp.int32)).astype(f32)
    same = routes_of[:, None, :, :] == ids[None, :, None, None]
    chance_rows = jnp.sum(jnp.where(same, chance_part[:, :, None, :], 0.0), axis=1)
    normed_two_back = half_sum(0)
    for value in normed_got.values():
        normed_two_back = normed_two_back + value.astype(f32)

    upstream = cotangent[0].astype(f32)
    middle_back = upstream + norm_back(middle, factor_two, second_gain, normed_two_back)
    second_part = jnp.sum(normed_two_back * middle * factor_two, axis=0)
    branch_back = (residual_factor * middle_back).astype(bf16)
    far = [joint(0, t, 0).astype(bf16) for t in others]
    branch_back, far = tie(branch_back, far)
    branch_back_blocks = gather_gx(branch_back)
    far, along_one_1 = tie(far, along_one_1)
    along_zero_0 = spread_y(far)

    def near(i, along):
        total = joint(i, 0, 1)
        for value in along:
            total = total + value.astype(f32)
        return total.astype(bf16)

    crossed_0 = swap(near(0, along_one_0), "gw", 1)
    crossed_0, mixed_rows = tie(crossed_0, mixed_rows)
    mixed_crossed = swap(mixed_rows[groups:], "gw", 1)
    branch_back_blocks[1], got[1] = tie(branch_back_blocks[1], got[1])
    near_1 = near(1, along_one_1)
    far = [joint(1, t, 0).astype(bf16) for t in others]
    mixed_rows = mixed_rows[:groups].astype(f32) + mixed_crossed.astype(f32)
    mixed_send = mixed_rows.astype(bf16)
    branch_back_blocks, near_1, far, mixed_send, chance_rows = tie(
        branch_back_blocks, near_1, far, mixed_send, chance_rows
    )
    mixed_got = [swap(mixed_send[s], "gx", s) for s in range(1, groups)]
    along_zero_0, far = tie(along_zero_0, far)
    along_zero_1 = spread_y(far)
    crossed_1 = swap(near_1, "gw", 1)

    back, normed_one_parts, first_part = attention_backward(
        branch_back_blocks, token_blocks, tables, attention_full, factor_all, qkv, spread, query_cols, key_cols
    )
    keep_gradient, give_gradient = attention_gradients(normed_one, back, branch_back_blocks, heads)
    got_gradient = swap(give_gradient, "co", 1)
    normed_one_parts, mixed_got, got_gradient = tie(normed_one_parts, mixed_got, got_gradient)
    mixed = mixed_rows[0]
    for value in mixed_got:
        mixed = mixed + value.astype(f32)
    output = (middle + residual_factor * mixed).astype(bf16)
    normed_got = [swap(normed_one_parts[s], "gx", s) for s in range(1, groups)]
    attention_sum = scatter_gy(keep_gradient, got_gradient)
    gains = jnp.stack([first_part[0], second_part])
    gains, along_zero_1, crossed_1, chance_rows = tie(gains, along_zero_1, crossed_1, chance_rows)
    chance_crossed = swap(chance_rows[groups:], "gw", 1)
    normed_got, chance_rows, chance_crossed = tie(normed_got, chance_rows, chance_crossed)
    gains = sum_everywhere(gains)
    normed_one_back = normed_one_parts[0].astype(f32)
    for value in normed_got:
        normed_one_back = normed_one_back + value.astype(f32)
    tokens_back = middle_back + norm_back(hidden, factor_all[:rows], first_gain, normed_one_back)
    chance_rows = chance_rows[:groups] + chance_crossed
    chance_back = chance_rows[0]
    for s in range(1, groups):
        chance_back = chance_back + swap(chance_rows[s], "gx", s)
    logit_back = chance * (chance_back - jnp.sum(chance * chance_back, axis=0, keepdims=True))
    sums = finish_gradients(
        [gradients[0], got[0]] + along_zero_0, crossed_0, 0, None, experts
    )
    gate_sum, up_sum, down_sum = finish_gradients(
        [gradients[1], got[1]] + along_zero_1, crossed_1, some, sums, experts
    )
    return (
        output[None],
        tokens_back[None],
        gains[0],
        attention_sum[:, :query_cols],
        attention_sum[:, query_cols : query_cols + key_cols],
        attention_sum[:, query_cols + key_cols : query_cols + 2 * key_cols],
        attention_sum[:, query_cols + 2 * key_cols :].T,
        gains[1],
        gate_sum,
        up_sum,
        jnp.swapaxes(down_sum, 1, 2),
        logit_back.T[None],
    )


def solution(mesh):
    groups, others = mesh.shape["gx"], mesh.shape["gy"]
    split = Mesh(mesh.devices.reshape(groups, others // 4, 2, 2), ("gx", "gt", "gw", "co"))
    gy = ("gt", "gw", "co")
    in_specs = (
        P(gy, "gx", None),
        P(),
        P(gy, "gx"),
        P(gy, "gx"),
        P(gy, "gx"),
        P("gx", gy),
        P(),
        P("gx", gy, None),
        P("gx", gy, None),
        P("gx", None, gy),
        P(gy, "gx", None),
        P(gy, "gx", None),
        P(gy, "gx", None),
    )
    out_specs = (
        P(gy, "gx", None),
        P(gy, "gx", None),
        P(),
        P(gy, "gx"),
        P(gy, "gx"),
        P(gy, "gx"),
        P("gx", gy),
        P(),
        P("gx", gy, None),
        P("gx", gy, None),
        P("gx", None, gy),
        P(gy, "gx", None),
    )
    return jax.shard_map(local, mesh=split, in_specs=in_specs, out_specs=out_specs, check_vma=False)
```

```python
import functools

import jax
import jax.numpy as jnp
from jax import lax
from jax.experimental import pallas as pl
from jax.experimental.pallas import tpu as pltpu
from jax.sharding import Mesh, PartitionSpec as P

HEAD_SIZE = 64
EXPERTS = 40
TOPK = 8
CAP = 48

epsilon = 1e-06
rope_base = 10000.0
residual_factor = 0.22
score_factor = 0.015625
masked_value = -1e30

SMALL_COST = pl.CostEstimate(flops=1, bytes_accessed=1, transcendentals=0)
LARGE_COST = pl.CostEstimate(flops=10**10, bytes_accessed=10**8, transcendentals=0)

f32 = jnp.float32
bf16 = jnp.bfloat16


def swap(value, axis, step):
    count = lax.axis_size(axis)
    return lax.ppermute(value, axis, [(i, i ^ step) for i in range(count)])


def tie(*values):
    return lax.optimization_barrier(values)


def pick(array, index, dim):
    return lax.dynamic_index_in_dim(array, index, dim, keepdims=False)


def rms_factor(rows):
    return lax.rsqrt(jnp.mean(rows * rows, axis=-1, keepdims=True) + epsilon)


def norm_back(rows, factor, gain, upstream):
    scaled = upstream * gain
    inner = jnp.mean(scaled * rows, axis=-1, keepdims=True)
    return factor * scaled - rows * factor * factor * factor * inner


def contract_rows(left, right):
    return lax.dot_general(left, right, (((0,), (0,)), ((), ())), preferred_element_type=f32)


def contract_cols(left, right):
    return lax.dot_general(left, right, (((1,), (1,)), ((), ())), preferred_element_type=f32)


def gather_gx(block):
    return [block] + [swap(block, "gx", s) for s in range(1, lax.axis_size("gx"))]


def over_y(value):
    return [swap(value, "gt", s) for s in range(1, lax.axis_size("gt"))]


def spread_y(values):
    return [swap(value, "gt", s) for s, value in enumerate(values, 1)]


def part_places():
    many = lax.axis_size("gt")
    places = [0, 2] + [4 * s for s in range(1, many)] + [4 * s + 2 for s in range(1, many)]
    return places + [p + 1 for p in places]


def own_place():
    me = (lax.axis_index("gt") * 2 + lax.axis_index("gw")) * 2 + lax.axis_index("co")
    return jnp.full((1,), me, jnp.int32)


def own_side():
    return jnp.full((1,), lax.axis_index("gw"), jnp.int32)


def halve_weights(gate, up, down):
    experts, rows, full = gate.shape
    half = full // 2

    def kernel(side_ref, gate_ref, up_ref, down_ref, keep, give):
        def put(low, out):
            for i, ref in enumerate((gate_ref, up_ref, down_ref)):
                out[0, :, i * half : (i + 1) * half] = ref[0, :, low : low + half]

        @pl.when(side_ref[0] == 0)
        def _():
            put(0, keep)
            put(half, give)

        @pl.when(side_ref[0] != 0)
        def _():
            put(half, keep)
            put(0, give)

    def block(columns):
        return pl.BlockSpec((1, rows, columns), lambda e, *_: (e, 0, 0))

    shape = jax.ShapeDtypeStruct((experts, rows, 3 * half), bf16)
    return pl.pallas_call(
        kernel,
        grid_spec=pltpu.PrefetchScalarGridSpec(
            num_scalar_prefetch=1,
            grid=(experts,),
            in_specs=[block(full)] * 3,
            out_specs=[block(3 * half)] * 2,
        ),
        out_shape=[shape, shape],
        cost_estimate=LARGE_COST,
        name="halve_weights",
    )(own_side(), gate, up, down)


def finish_gradients(summed, crossed, start, before, total_experts):
    experts, rows, columns = crossed.shape
    half = columns // 3
    count = len(summed)
    aliased = 0 if before is None else 3

    def kernel(side_ref, *refs):
        total = 0.0
        for ref in refs[:count]:
            total = total + (ref[0, 0] if len(ref.shape) == 4 else ref[0]).astype(f32)
        other = refs[count][0].astype(f32)

        def put(low, value):
            for i, out in enumerate(refs[count + 1 + aliased :]):
                out[0, :, low : low + half] = value[:, i * half : (i + 1) * half]

        @pl.when(side_ref[0] == 0)
        def _():
            put(0, total)
            put(half, other)

        @pl.when(side_ref[0] != 0)
        def _():
            put(half, total)
            put(0, other)

    def block(columns, first):
        return pl.BlockSpec((1, rows, columns), lambda e, *_: (e + first, 0, 0))

    shape = jax.ShapeDtypeStruct((total_experts, rows, 2 * half), f32)
    return pl.pallas_call(
        kernel,
        grid_spec=pltpu.PrefetchScalarGridSpec(
            num_scalar_prefetch=1,
            grid=(experts,),
            in_specs=[
                pl.BlockSpec((1, 1, rows, columns), lambda e, *_: (0, e, 0, 0)) if v.ndim == 4 else block(columns, 0)
                for v in summed
            ]
            + [block(columns, 0)]
            + [pl.BlockSpec(memory_space=pl.ANY)] * aliased,
            out_specs=[block(2 * half, start)] * 3,
        ),
        out_shape=[shape] * 3,
        input_output_aliases={count + 2 + i: i for i in range(aliased)},
        cost_estimate=SMALL_COST,
        name="finish_gradients",
    )(own_side(), *summed, crossed, *(before or ()))


def others_of(value, axes):
    count = lax.axis_size(axes)
    return [lax.ppermute(value, axes, [(i, i ^ s) for i in range(count)]) for s in range(1, count)]


def slot_mask(slot_row):
    wanted = lax.broadcasted_iota(jnp.int32, (CAP, slot_row.shape[1]), 0).astype(f32)
    return slot_row == wanted


def route_slots(gathered, order, first_expert, experts, width):
    blocks, tokens = gathered.shape[:2]

    def kernel(order_ref, first_ref, routing_ref, routes_out, slots_out, chances_out, slots_by, chances_by):
        earlier = lax.broadcasted_iota(jnp.int32, (tokens, tokens), 0)
        earlier = (earlier < lax.broadcasted_iota(jnp.int32, (tokens, tokens), 1)).astype(f32).astype(bf16)
        for b in range(blocks):
            routing = routing_ref[order_ref[b]].astype(f32).T
            routes = routing[:TOPK]
            chance = routing[TOPK : 2 * TOPK] + routing[2 * TOPK : 3 * TOPK]
            routes_out[b] = routes
            hits, chosen = [], []
            for e in range(experts):
                same = routes == (first_ref[0] + e).astype(f32)
                hits.append(jnp.sum(jnp.where(same, 1.0, 0.0), axis=0, keepdims=True))
                chosen.append(jnp.sum(jnp.where(same, chance, 0.0), axis=0, keepdims=True))
            hits, chosen = jnp.concatenate(hits, axis=0), jnp.concatenate(chosen, axis=0)
            rank = jnp.dot(hits.astype(bf16), earlier, preferred_element_type=f32)
            slots = jnp.where(hits > 0.0, rank, -1.0)
            slots_out[b] = slots
            chances_out[b] = chosen
            for e in range(experts):
                slots_by[e, b : b + 1, :] = slots[e : e + 1]
                chances_by[e, b : b + 1, :] = chosen[e : e + 1]

    def whole(*shape):
        zeros = (0,) * len(shape)
        return pl.BlockSpec(shape, lambda i, *_: zeros)

    shapes = [(blocks, TOPK, tokens)] + [(blocks, experts, tokens)] * 2 + [(experts, blocks, tokens)] * 2
    return pl.pallas_call(
        kernel,
        grid_spec=pltpu.PrefetchScalarGridSpec(
            num_scalar_prefetch=2,
            grid=(1,),
            in_specs=[pl.BlockSpec((blocks, tokens, 128), lambda i, *_: (0, 0, width // 128))],
            out_specs=[whole(*shape) for shape in shapes],
        ),
        out_shape=[jax.ShapeDtypeStruct(shape, f32) for shape in shapes],
        cost_estimate=SMALL_COST,
        name="route_slots",
    )(order, jnp.full((1,), first_expert, jnp.int32), gathered)


def gather_slots(sources, order, slots):
    blocks, experts, tokens = slots.shape
    listed = isinstance(sources, list)
    width = sources[0].shape[1] if listed else order[1]

    def find(slots_ref, rows, out_ref):
        mask = jnp.concatenate([slot_mask(slots_ref[0, e : e + 1, :]) for e in range(experts)], axis=0)
        found = jnp.dot(mask.astype(f32).astype(bf16), rows, preferred_element_type=f32)
        out_ref[...] = found.astype(bf16).reshape(experts, 1, CAP, width)

    def kernel_list(order_ref, slots_ref, *refs):
        for i in range(blocks):

            @pl.when(pl.program_id(0) == i)
            def _(i=i):
                refs[blocks + 1][...] = refs[i][...]

        find(slots_ref, refs[blocks + 1][...], refs[blocks])

    def kernel_array(order_ref, slots_ref, rows_ref, out_ref):
        find(slots_ref, rows_ref[0], out_ref)

    if listed:
        specs = [pl.BlockSpec((tokens, width), lambda b, *_: (0, 0))] * blocks
        scratch = [pltpu.VMEM((tokens, width), bf16)]
        prefetch = jnp.zeros((1,), jnp.int32)
    else:
        specs = [pl.BlockSpec((1, tokens, width), lambda b, order_ref: (order_ref[b], 0, 0))]
        scratch = []
        prefetch = order[0]
        sources = [sources]
    return pl.pallas_call(
        kernel_list if listed else kernel_array,
        grid_spec=pltpu.PrefetchScalarGridSpec(
            num_scalar_prefetch=1,
            grid=(blocks,),
            in_specs=[pl.BlockSpec((1, experts, tokens), lambda b, *_: (b, 0, 0))] + specs,
            out_specs=pl.BlockSpec((experts, 1, CAP, width), lambda b, *_: (0, b, 0, 0)),
            scratch_shapes=scratch,
        ),
        out_shape=jax.ShapeDtypeStruct((experts, blocks, CAP, width), bf16),
        compiler_params=pltpu.CompilerParams(vmem_limit_bytes=40 * 2**20),
        cost_estimate=LARGE_COST,
        name="gather_slots",
    )(prefetch, slots, *sources)


def sum_slots(slot_rows, slots, order):
    blocks, experts, tokens = slots.shape
    width = slot_rows[0].shape[3]

    def kernel(order_ref, slots_ref, *refs):
        total, first = None, 0
        for ref in refs[:-1]:
            mine = ref.shape[0]
            mask = jnp.concatenate(
                [slot_mask(slots_ref[0, e : e + 1, :]) for e in range(first, first + mine)], axis=0
            )
            first = first + mine
            part = contract_rows(mask.astype(f32).astype(bf16), ref[...].reshape(mine * CAP, width))
            total = part if total is None else total + part
        refs[-1][0] = total.astype(bf16)

    return pl.pallas_call(
        kernel,
        grid_spec=pltpu.PrefetchScalarGridSpec(
            num_scalar_prefetch=1,
            grid=(blocks,),
            in_specs=[pl.BlockSpec((1, experts, tokens), lambda b, *_: (b, 0, 0))]
            + [pl.BlockSpec((r.shape[0], 1, CAP, width), lambda b, *_: (0, b, 0, 0)) for r in slot_rows],
            out_specs=pl.BlockSpec((1, tokens, width), lambda b, order_ref: (order_ref[b], 0, 0)),
        ),
        out_shape=jax.ShapeDtypeStruct((blocks, tokens, width), bf16),
        compiler_params=pltpu.CompilerParams(vmem_limit_bytes=40 * 2**20),
        cost_estimate=LARGE_COST,
        name="sum_slots",
    )(order, slots, *slot_rows)


def run_experts(rows_in, back_in, weights, start, experts, slots, chances):
    blocks, _, width = rows_in.shape[1:]
    places = part_places()
    tokens = slots.shape[2]
    weights = [
        [(w, first) for w, first in part if first < start + experts and first + w.shape[0] > start]
        for part in weights
    ]
    flat = [piece for part in weights for piece in part]
    cut, half = flat[0][0].shape[1], flat[0][0].shape[2] // 3
    count = len(places)
    total_slots = blocks * CAP

    def kernel(me_ref, rows_ref, back_ref, slots_ref, chances_ref, *refs):
        rows_out, mixed_out, chance_out = refs[len(flat) : len(flat) + 3]
        grads = refs[len(flat) + 3 : len(flat) + 5]
        gu_full, d_full, gu_total, d_total = refs[len(flat) + 5 :]
        spots = [pl.ds(pl.multiple_of((me_ref[0] ^ place) * cut, cut), cut) for place in places]
        expert = start + pl.program_id(0)
        part_refs = iter(refs[: len(flat)])
        for spot, part in zip(spots, weights):
            for w, first in part:
                ref = next(part_refs)

                def put(spot=spot, ref=ref):
                    gu_full[spot, :] = ref[0, :, : 2 * half]
                    d_full[spot, :] = ref[0, :, 2 * half :]

                if len(part) == 1:
                    put()
                else:
                    pl.when((expert >= first) & (expert < first + w.shape[0]))(put)
        rows = rows_ref[0].reshape(total_slots, width)
        back = back_ref[0].reshape(total_slots, width)
        masks = [slot_mask(slots_ref[0, b : b + 1, :]) for b in range(blocks)]
        chance = jnp.concatenate(
            [
                jnp.sum(jnp.where(masks[b], chances_ref[0, b : b + 1, :], 0.0), axis=1, keepdims=True)
                for b in range(blocks)
            ],
            axis=0,
        )
        both = jnp.dot(rows, gu_full[...], preferred_element_type=f32)
        active_back = jnp.dot(back, d_full[...], preferred_element_type=f32) * residual_factor
        gate, upper = both[:, :half], both[:, half:]
        sigma = jax.nn.sigmoid(gate)
        silu = gate * sigma
        active = silu * upper
        chance_back = jnp.sum(active * active_back, axis=1, keepdims=True)
        for b in range(blocks):
            column = chance_back[b * CAP : (b + 1) * CAP]
            chance_out[0, b : b + 1, :] = jnp.sum(jnp.where(masks[b], column, 0.0), axis=0, keepdims=True)
        scaled = (active * chance).astype(bf16)
        active_back = active_back * chance
        gate_back = active_back * upper * (sigma * (1.0 + gate * (1.0 - sigma)))
        upper_back = active_back * silu
        both_back = jnp.concatenate([gate_back.astype(bf16), upper_back.astype(bf16)], axis=1)
        rows_out[0] = contract_cols(both_back, gu_full[...]).astype(bf16).reshape(blocks, CAP, width)
        mixed_out[0] = contract_cols(scaled, d_full[...]).astype(bf16).reshape(blocks, CAP, width)
        gu_total[...] = contract_rows(rows, both_back).astype(bf16)
        d_total[...] = (contract_rows(back, scaled) * residual_factor).astype(bf16)
        for spot, place in zip(spots, places):
            grads[place % 2][place // 2, 0, :, : 2 * half] = gu_total[spot, :]
            grads[place % 2][place // 2, 0, :, 2 * half :] = d_total[spot, :]

    def block(shape, first=0):
        zeros = (0,) * len(shape)
        return pl.BlockSpec((1,) + shape, lambda e, *_: (e + first,) + zeros)

    grad_shape = jax.ShapeDtypeStruct((count // 2, experts, cut, 3 * half), bf16)
    def held(size, first):
        return pl.BlockSpec(
            (1, cut, 3 * half), lambda e, *_: (jnp.clip(e + start - first, 0, size - 1), 0, 0)
        )

    slot_shape = jax.ShapeDtypeStruct((experts, blocks, CAP, width), bf16)
    out = pl.pallas_call(
        kernel,
        grid_spec=pltpu.PrefetchScalarGridSpec(
            num_scalar_prefetch=1,
            grid=(experts,),
            in_specs=[
                block((blocks, CAP, width), start),
                block((blocks, CAP, width), start),
                block((blocks, tokens), start),
                block((blocks, tokens), start),
            ]
            + [held(w.shape[0], first) for w, first in flat],
            out_specs=[block((blocks, CAP, width)), block((blocks, CAP, width)), block((blocks, tokens))]
            + [pl.BlockSpec((count // 2, 1, cut, 3 * half), lambda e, *_: (0, e, 0, 0))] * 2,
            scratch_shapes=[
                pltpu.VMEM((width, 2 * half), bf16),
                pltpu.VMEM((width, half), bf16),
                pltpu.VMEM((width, 2 * half), bf16),
                pltpu.VMEM((width, half), bf16),
            ],
        ),
        out_shape=[slot_shape, slot_shape, jax.ShapeDtypeStruct((experts, blocks, tokens), f32)]
        + [grad_shape] * 2,
        compiler_params=pltpu.CompilerParams(vmem_limit_bytes=60 * 2**20),
        cost_estimate=LARGE_COST,
        name="run_experts",
    )(own_place(), rows_in, back_in, slots, chances, *[w for w, _ in flat])
    return out


ATTENTION_PARAMS = pltpu.CompilerParams(vmem_limit_bytes=60 * 2**20)


def turned_half(x):
    lanes = lax.broadcasted_iota(jnp.int32, x.shape, 1) % HEAD_SIZE
    half = HEAD_SIZE // 2
    return jnp.where(lanes < half, -pltpu.roll(x, 128 - half, 1), pltpu.roll(x, half, 1))


def head(x, h):
    return x[:, h * HEAD_SIZE : (h + 1) * HEAD_SIZE]


def attention_forward(token_blocks, gain, parts, mirrors, tables, query_cols, key_cols):
    blocks = len(token_blocks)
    rows, width = token_blocks[0].shape
    length = rows * blocks
    count = len(parts)
    places = part_places()
    columns = query_cols + 2 * key_cols
    heads = query_cols // HEAD_SIZE
    ratio = query_cols // key_cols
    step = 256

    def kernel(me_ref, gain_ref, cosine_ref, sine_ref, down_ref, along_ref, *refs):
        token_refs, part_refs = refs[:blocks], refs[blocks : blocks + count + 1]
        full, normed, factors, qkv, heads_out, spread = refs[blocks + count + 1 : blocks + count + 7]
        branch = refs[blocks + count + 7 :]
        for i, ref in enumerate(part_refs[:count]):
            full[me_ref[0] ^ places[i]] = ref[...]
            full[me_ref[0] ^ places[count + i]] = part_refs[count][i]
        for s in range(blocks):
            x = token_refs[s][...].astype(f32)
            factor = rms_factor(x)
            span = slice(s * rows, (s + 1) * rows)
            factors[span, :] = factor
            normed[span, :] = (x * factor * gain_ref[...]).astype(bf16)
        weights = full[...].reshape(width, full.shape[2])
        projected = jnp.dot(normed[...], weights[:, :columns], preferred_element_type=f32)
        for g in range((query_cols + key_cols) // 128):
            span = slice(g * 128, (g + 1) * 128)
            x = projected[:, span]
            qkv[:, span] = (x * cosine_ref[...] + turned_half(x) * sine_ref[...]).astype(bf16)
        qkv[:, query_cols + key_cols :] = projected[:, query_cols + key_cols :].astype(bf16)
        for q in range(0, length, step):
            span = slice(q, q + step)
            mixed = []
            mask = along_ref[...] <= down_ref[span, :]
            query = qkv[span, :query_cols]
            for h in range(heads):
                key = head(qkv[:, query_cols : query_cols + key_cols], h // ratio)
                value = head(qkv[:, query_cols + key_cols :], h // ratio)
                scores = jnp.where(mask, contract_cols(head(query, h), key) * score_factor, masked_value)
                top = jnp.max(scores, axis=1, keepdims=True)
                exps = jnp.exp(scores - top)
                total = jnp.sum(exps, axis=1, keepdims=True)
                probs = (exps * (1.0 / total)).astype(bf16)
                mixed.append(jnp.dot(probs, value, preferred_element_type=f32).astype(bf16))
                spread[span, h : h + 1] = top + jnp.log(total)
            heads_out[span, :] = jnp.concatenate(mixed, axis=1)
        for s in range(blocks):
            part = contract_cols(heads_out[s * rows : (s + 1) * rows, :], weights[:, columns:])
            branch[s][...] = part.astype(bf16)

    vmem = pl.BlockSpec(memory_space=pltpu.VMEM)
    return pl.pallas_call(
        kernel,
        out_shape=[
            jax.ShapeDtypeStruct((2 * count,) + parts[0].shape, bf16),
            jax.ShapeDtypeStruct((length, width), bf16),
            jax.ShapeDtypeStruct((length, 1), f32),
            jax.ShapeDtypeStruct((length, columns), bf16),
            jax.ShapeDtypeStruct((length, query_cols), bf16),
            jax.ShapeDtypeStruct((length, heads), f32),
        ]
        + [jax.ShapeDtypeStruct((rows, width), bf16)] * blocks,
        in_specs=[pl.BlockSpec(memory_space=pltpu.SMEM)] + [vmem] * (6 + blocks + count),
        out_specs=[vmem] * (6 + blocks),
        compiler_params=ATTENTION_PARAMS,
        cost_estimate=SMALL_COST,
        name="attention_forward",
    )(own_place(), gain[None], *tables, *token_blocks, *parts, mirrors)


def attention_backward(pieces, token_blocks, tables, full, factors, qkv, spread, query_cols, key_cols):
    blocks = len(pieces)
    rows, width = pieces[0].shape
    length = rows * blocks
    columns = query_cols + 2 * key_cols
    heads = query_cols // HEAD_SIZE
    pairs = key_cols // HEAD_SIZE
    ratio = heads // pairs
    step = 256

    def kernel(cosine_ref, sine_ref, down_ref, along_ref, full_ref, factors_ref, qkv_ref, spread_ref, *refs):
        piece_refs, token_refs = refs[:blocks], refs[blocks : 2 * blocks]
        back, gain_back = refs[2 * blocks : 2 * blocks + 2]
        normed_back = refs[2 * blocks + 2 : 3 * blocks + 2]
        heads_back, turned = refs[3 * blocks + 2 :]
        weights = full_ref[...].reshape(width, full_ref.shape[2])
        for s in range(blocks):
            part = jnp.dot(piece_refs[s][...], weights[:, columns:], preferred_element_type=f32)
            heads_back[s * rows : (s + 1) * rows, :] = part.astype(bf16)
        key_back, value_back = [None] * pairs, [None] * pairs

        def add(total, value):
            return value if total is None else total + value

        for q in range(0, length, step):
            span = slice(q, q + step)
            mask = along_ref[...] <= down_ref[span, :]
            query = qkv_ref[span, :query_cols]
            upper = heads_back[span, :]
            query_back = []
            for h in range(heads):
                g = h // ratio
                key = head(qkv_ref[:, query_cols : query_cols + key_cols], g)
                value = head(qkv_ref[:, query_cols + key_cols :], g)
                query_h, upper_h = head(query, h), head(upper, h)
                scores = jnp.where(mask, contract_cols(query_h, key) * score_factor, masked_value)
                probs = jnp.exp(scores - spread_ref[span, h : h + 1])
                prob_back = contract_cols(upper_h, value)
                inner = jnp.sum(probs * prob_back, axis=1, keepdims=True)
                score_back = (probs * (prob_back - inner)).astype(bf16)
                query_back.append(jnp.dot(score_back, key, preferred_element_type=f32) * score_factor)
                key_back[g] = add(key_back[g], contract_rows(score_back, query_h))
                value_back[g] = add(value_back[g], contract_rows(probs.astype(bf16), upper_h))
            turned[span, :query_cols] = jnp.concatenate(query_back, axis=1)
        turned[:, query_cols:] = jnp.concatenate(
            [k * score_factor for k in key_back] + value_back, axis=1
        )
        for g in range((query_cols + key_cols) // 128):
            span = slice(g * 128, (g + 1) * 128)
            x = turned[:, span]
            back[:, span] = (x * cosine_ref[...] - turned_half(x) * sine_ref[...]).astype(bf16)
        back[:, query_cols + key_cols :] = turned[:, query_cols + key_cols :].astype(bf16)
        total = None
        for s in range(blocks):
            span = slice(s * rows, (s + 1) * rows)
            part = contract_cols(back[span, :], weights[:, :columns])
            normed_back[s][...] = part.astype(bf16)
            scaled = part * (token_refs[s][...].astype(f32) * factors_ref[span, :])
            total = add(total, jnp.sum(scaled, axis=0, keepdims=True))
        gain_back[...] = total

    vmem = pl.BlockSpec(memory_space=pltpu.VMEM)
    return pl.pallas_call(
        kernel,
        out_shape=[
            jax.ShapeDtypeStruct((length, columns), bf16),
            jax.ShapeDtypeStruct((1, width), f32),
        ]
        + [jax.ShapeDtypeStruct((rows, width), bf16)] * blocks,
        in_specs=[vmem] * (8 + 2 * blocks),
        out_specs=[vmem] * (2 + blocks),
        scratch_shapes=[pltpu.VMEM((length, query_cols), bf16), pltpu.VMEM((length, columns), f32)],
        compiler_params=ATTENTION_PARAMS,
        cost_estimate=LARGE_COST,
        name="attention_backward",
    )(*tables, full, factors, qkv, spread, *pieces, *token_blocks)


def attention_gradients(normed, back, pieces, heads):
    blocks = len(pieces)
    rows, width = pieces[0].shape
    columns = back.shape[1]
    both = columns + heads.shape[1]
    places = part_places()
    count = len(places)
    cut = width // count

    def kernel(me_ref, normed_ref, back_ref, heads_ref, *refs):
        keep, give, total = refs[blocks:]
        total[:, :columns] = contract_rows(normed_ref[...], back_ref[...]).astype(bf16)
        piece = jnp.concatenate([ref[...] for ref in refs[:blocks]], axis=0)
        total[:, columns:] = contract_rows(piece, heads_ref[...]).astype(bf16)
        for place in places:
            spot = pl.ds(pl.multiple_of((me_ref[0] ^ place) * cut, cut), cut)
            (give if place % 2 else keep)[place // 2] = total[spot, :]

    vmem = pl.BlockSpec(memory_space=pltpu.VMEM)
    shape = jax.ShapeDtypeStruct((count // 2, cut, both), bf16)
    return pl.pallas_call(
        kernel,
        out_shape=[shape, shape],
        in_specs=[pl.BlockSpec(memory_space=pltpu.SMEM)] + [vmem] * (3 + blocks),
        out_specs=[vmem] * 2,
        scratch_shapes=[pltpu.VMEM((width, both), bf16)],
        compiler_params=ATTENTION_PARAMS,
        cost_estimate=LARGE_COST,
        name="attention_gradients",
    )(own_place(), normed, back, heads, *pieces)


def local(
    tokens,
    first_gain,
    query_weight,
    key_matrix,
    value_matrix,
    out_weight,
    second_gain,
    gate_weight,
    up_weight,
    down_weight,
    routes,
    route_logits,
    cotangent,
):
    groups, many = lax.axis_size("gx"), lax.axis_size("gt")
    me_x, me_w = lax.axis_index("gx"), lax.axis_index("gw")
    own_tokens = tokens[0]
    rows, width = own_tokens.shape
    query_cols = query_weight.shape[1]
    key_cols = key_matrix.shape[1]
    query_heads = query_cols // HEAD_SIZE
    pair_heads = key_cols // HEAD_SIZE
    ratio = query_heads // pair_heads
    experts = gate_weight.shape[0]
    some = experts // 2
    spans = ((0, some), (some, experts - some))

    token_blocks = gather_gx(own_tokens)
    attention = jnp.concatenate(
        [query_weight, key_matrix, value_matrix, out_weight.T], axis=1
    )
    across = swap(attention, "gw", 1)
    along = over_y(attention)
    both = over_y(across)
    down_turned = jnp.swapaxes(down_weight, 1, 2)
    keep, give = halve_weights(gate_weight, up_weight, down_turned)
    attention_parts = [attention, across] + along + both
    attention_mirrors = swap(jnp.stack(attention_parts), "co", 1)
    positions = jnp.concatenate(
        [(me_x ^ s) * rows + jnp.arange(rows, dtype=jnp.int32) for s in range(groups)]
    ).astype(f32)
    half = HEAD_SIZE // 2
    freq = rope_base ** (-(jnp.arange(half, dtype=f32) * 2.0 / HEAD_SIZE))
    angle = positions[:, None] * jnp.tile(freq, 128 // half)[None, :]
    tables = (jnp.cos(angle), jnp.sin(angle), positions[:, None], positions[None, :])
    token_blocks, tables, attention_mirrors, give, keep = tie(
        token_blocks, tables, attention_mirrors, give, keep
    )
    across_w, along_w = swap(give, "gw", 1), over_y(keep)
    mirror_keep = swap(keep, "co", 1)

    logits = route_logits[0].T
    weights = jnp.exp(logits - jnp.max(logits, axis=0, keepdims=True))
    chance = weights / jnp.sum(weights, axis=0, keepdims=True)
    chance_high = lax.reduce_precision(chance, 8, 7)
    routing = jnp.concatenate([routes[0].T.astype(f32), chance_high, chance - chance_high], axis=0)
    routing = jnp.pad(routing.astype(bf16).T, ((0, 0), (0, 128 - 3 * TOPK)))
    payload = jnp.concatenate([cotangent[0], routing], axis=1)
    turned = jnp.stack([w * groups + (me_x ^ s) for w in range(2) for s in range(groups)])
    gathered = lax.all_gather(payload, "gx", axis=0)

    attention_full, normed_one, factor_all, qkv, heads, spread, *branch_parts = attention_forward(
        token_blocks, first_gain, attention_parts, attention_mirrors, tables, query_cols, key_cols
    )

    branch_parts, mirror_keep = tie(branch_parts, mirror_keep)
    branch_got = [swap(branch_parts[s], "gx", s) for s in range(1, groups)]
    across_w, gathered, branch_got[0] = tie(across_w, gathered, branch_got[0])
    gathered_across = swap(gathered, "gw", 1)
    branch = branch_parts[0].astype(f32)
    for value in branch_got:
        branch = branch + value.astype(f32)

    hidden = own_tokens.astype(f32)
    middle = hidden + residual_factor * branch
    factor_two = rms_factor(middle)
    normed_two = (middle * factor_two * second_gain).astype(bf16)

    middle_part = experts * 7 // 10
    normed_two, across_w, along_w = tie(normed_two, across_w, along_w)
    normed_parts = gather_gx(normed_two)
    both_0 = over_y(across_w[:middle_part])
    turned_parts = {s: swap(normed_parts[s], "gw", 1) for s in (0, 1)}

    gathered = jnp.concatenate([gathered, gathered_across])
    routes_of, slots, _, slots_by, chances_by = route_slots(gathered, turned, me_x * experts, experts, width)
    back_in = gather_slots(gathered, (turned, width), slots)
    normed_parts, turned_parts[0], turned_parts[1], both_0, across_w, along_w, back_in = tie(
        normed_parts, turned_parts[0], turned_parts[1], both_0, across_w, along_w, back_in
    )

    rest = [s for s in range(groups) if s not in (0, 1)]
    turned_rest = swap(jnp.stack([normed_parts[s] for s in rest]), "gw", 1)
    both_1 = over_y(across_w[middle_part:])
    mirror_w = [swap(v, "co", 1) for v in [across_w] + along_w]
    mirror_both_0 = [swap(v, "co", 1) for v in both_0]
    normed_rows = normed_parts + [turned_parts[0], turned_parts[1]]
    normed_rows = normed_rows + [turned_rest[i] for i in range(len(rest))]
    normed_rows, both_1 = tie(normed_rows, both_1)
    rows_in = gather_slots(normed_rows, None, slots)
    mirror_both_1 = [swap(v, "co", 1) for v in both_1]
    rows_in, mirror_w, mirror_both_0, mirror_both_1 = tie(rows_in, mirror_w, mirror_both_0, mirror_both_1)

    def halved(boths):
        return [[(first, 0), (second, middle_part)] for first, second in zip(*boths)]

    parts = [[(v, 0)] for v in [keep, across_w] + along_w] + halved((both_0, both_1))
    parts = parts + [[(v, 0)] for v in [mirror_keep] + mirror_w] + halved((mirror_both_0, mirror_both_1))
    rows_back, mixed_parts, chance_parts, gradients, given = [], [], [], [], []
    for i, (start, size) in enumerate(spans):
        if i == 1:
            rows_in, rows_back[0] = tie(rows_in, rows_back[0])
        result = run_experts(rows_in, back_in, parts, start, size, slots_by, chances_by)
        for lot, value in zip((rows_back, mixed_parts, chance_parts, gradients, given), result):
            lot.append(value)

    got = [None, None]

    def joint(i, t, w):
        return gradients[i][2 * t + w].astype(f32) + got[i][2 * t + w].astype(f32)

    others = range(1, many)
    got[0] = swap(given[0], "co", 1)
    got[0], rows_back = tie(got[0], rows_back)
    far = [joint(0, t, 1).astype(bf16) for t in others]
    far, rows_back, given[1] = tie(far, rows_back, given[1])
    got[1] = swap(given[1], "co", 1)
    along_one_0 = spread_y(far)
    plain = jnp.arange(2 * groups, dtype=jnp.int32)
    summed = sum_slots(rows_back, slots, plain)
    pieces = ((2, groups), (0, 2))
    crossed = [swap(summed[groups + a : groups + b], "gw", 1) for a, b in pieces]
    far = [joint(1, t, 1).astype(bf16) for t in others]
    mixed_rows = sum_slots(mixed_parts, slots, plain)
    crossed[0], mixed_rows = tie(crossed[0], mixed_rows)

    def half_sum(s):
        a, b = pieces[0] if s >= 2 else pieces[1]
        value = crossed[0] if s >= 2 else crossed[1]
        return summed[s].astype(f32) + value[s - a].astype(f32)

    normed_got = {s: swap(half_sum(s).astype(bf16), "gx", s) for s in range(2, groups)}
    along_one_0, far, got[1], crossed[1] = tie(along_one_0, far, got[1], crossed[1])
    along_one_1 = spread_y(far)
    crossed[1], normed_got[3] = tie(crossed[1], normed_got[3])
    normed_got[1] = swap(half_sum(1).astype(bf16), "gx", 1)
    chance_part = jnp.swapaxes(jnp.concatenate(chance_parts, axis=0), 0, 1)
    ids = (me_x * experts + jnp.arange(experts, dtype=jnp.int32)).astype(f32)
    same = routes_of[:, None, :, :] == ids[None, :, None, None]
    chance_rows = jnp.sum(jnp.where(same, chance_part[:, :, None, :], 0.0), axis=1)
    normed_two_back = half_sum(0)
    for value in normed_got.values():
        normed_two_back = normed_two_back + value.astype(f32)

    upstream = cotangent[0].astype(f32)
    middle_back = upstream + norm_back(middle, factor_two, second_gain, normed_two_back)
    second_part = jnp.sum(normed_two_back * middle * factor_two, axis=0)
    branch_back = (residual_factor * middle_back).astype(bf16)
    branch_back_blocks = gather_gx(branch_back)
    mixed_rows, crossed[1] = tie(mixed_rows, crossed[1])
    mixed_crossed = swap(mixed_rows[groups:], "gw", 1)
    branch_back_blocks[1], gradients[0], along_one_1, mixed_crossed = tie(
        branch_back_blocks[1], gradients[0], along_one_1, mixed_crossed
    )
    far = [joint(0, t, 0).astype(bf16) for t in others]
    along_zero_0 = spread_y(far)

    def near(i, along):
        total = joint(i, 0, 1)
        for value in along:
            total = total + value.astype(f32)
        return total.astype(bf16)

    near_0, mixed_crossed = tie(near(0, along_one_0), mixed_crossed)
    crossed_0 = swap(near_0, "gw", 1)
    branch_back_blocks[1], got[1] = tie(branch_back_blocks[1], got[1])
    near_1 = near(1, along_one_1)
    far = [joint(1, t, 0).astype(bf16) for t in others]
    mixed_rows = mixed_rows[:groups].astype(f32) + mixed_crossed.astype(f32)
    mixed_send = mixed_rows.astype(bf16)
    branch_back_blocks, near_1, far, mixed_send, chance_rows = tie(
        branch_back_blocks, near_1, far, mixed_send, chance_rows
    )
    mixed_got = [swap(mixed_send[s], "gx", s) for s in range(1, groups)]
    far_last, near_last = far, near_1

    back, first_part, *normed_one_parts = attention_backward(
        branch_back_blocks, token_blocks, tables, attention_full, factor_all, qkv, spread, query_cols, key_cols
    )
    back, along_zero_0, crossed_0, far_last, near_last = tie(back, along_zero_0, crossed_0, far_last, near_last)
    along_zero_1 = spread_y(far_last)
    crossed_1 = swap(near_last, "gw", 1)
    keep_gradient, give_gradient = attention_gradients(normed_one, back, branch_back_blocks, heads)
    normed_one_parts, mixed_got, give_gradient = tie(normed_one_parts, mixed_got, give_gradient)
    got_gradient = swap(give_gradient, "co", 1)
    mixed = mixed_rows[0]
    for value in mixed_got:
        mixed = mixed + value.astype(f32)
    output = (middle + residual_factor * mixed).astype(bf16)
    normed_got = [swap(normed_one_parts[s], "gx", s) for s in range(1, groups)]
    gains = jnp.stack([first_part[0], second_part])
    gains = gains + swap(gains, "co", 1)
    normed_got, got_gradient, along_zero_1, gains, chance_rows = tie(
        normed_got, got_gradient, along_zero_1, gains, chance_rows
    )
    chance_crossed = swap(chance_rows[groups:], "gw", 1)
    gains_got = others_of(gains, ("gt", "gw"))
    total = keep_gradient.astype(f32) + got_gradient.astype(f32)
    far_attention = spread_y([total[2 * t : 2 * t + 2].astype(bf16) for t in others])
    sums = finish_gradients([gradients[0], got[0]] + along_zero_0, crossed_0, 0, None, experts)
    sums = finish_gradients([gradients[1], got[1]] + along_zero_1, crossed_1, some, sums, experts)
    gate_sum, up_sum, down_sum = sums
    for value in gains_got:
        gains = gains + value
    for value in others_of(gains, ("gx",)):
        gains = gains + value
    attention_sum = total[:2]
    for value in far_attention:
        attention_sum = attention_sum + value.astype(f32)
    attention_sum = attention_sum[0] + swap(attention_sum[1].astype(bf16), "gw", 1).astype(f32)
    normed_one_back = normed_one_parts[0].astype(f32)
    for value in normed_got:
        normed_one_back = normed_one_back + value.astype(f32)
    tokens_back = middle_back + norm_back(hidden, factor_all[:rows], first_gain, normed_one_back)
    chance_rows = chance_rows[:groups] + chance_crossed
    chance_back = chance_rows[0]
    for s in range(1, groups):
        chance_back = chance_back + swap(chance_rows[s], "gx", s)
    logit_back = chance * (chance_back - jnp.sum(chance * chance_back, axis=0, keepdims=True))
    return (
        output[None],
        tokens_back[None],
        gains[0],
        attention_sum[:, :query_cols],
        attention_sum[:, query_cols : query_cols + key_cols],
        attention_sum[:, query_cols + key_cols : query_cols + 2 * key_cols],
        attention_sum[:, query_cols + 2 * key_cols :].T,
        gains[1],
        gate_sum,
        up_sum,
        jnp.swapaxes(down_sum, 1, 2),
        logit_back.T[None],
    )


def solution(mesh):
    groups, others = mesh.shape["gx"], mesh.shape["gy"]
    split = Mesh(mesh.devices.reshape(groups, others // 4, 2, 2), ("gx", "gt", "gw", "co"))
    gy = ("gt", "gw", "co")
    in_specs = (
        P(gy, "gx", None),
        P(),
        P(gy, "gx"),
        P(gy, "gx"),
        P(gy, "gx"),
        P("gx", gy),
        P(),
        P("gx", gy, None),
        P("gx", gy, None),
        P("gx", None, gy),
        P(gy, "gx", None),
        P(gy, "gx", None),
        P(gy, "gx", None),
    )
    out_specs = (
        P(gy, "gx", None),
        P(gy, "gx", None),
        P(),
        P(gy, "gx"),
        P(gy, "gx"),
        P(gy, "gx"),
        P("gx", gy),
        P(),
        P("gx", gy, None),
        P("gx", gy, None),
        P("gx", None, gy),
        P(gy, "gx", None),
    )
    return jax.shard_map(local, mesh=split, in_specs=in_specs, out_specs=out_specs, check_vma=False)
```

```python
import functools

import jax
import jax.numpy as jnp
from jax import lax
from jax.experimental import pallas as pl
from jax.experimental.pallas import tpu as pltpu
from jax.sharding import Mesh, PartitionSpec as P

HEAD_SIZE = 64
EXPERTS = 40
TOPK = 8
CAP = 48

epsilon = 1e-06
rope_base = 10000.0
residual_factor = 0.22
score_factor = 0.015625
masked_value = -1e30

SMALL_COST = pl.CostEstimate(flops=1, bytes_accessed=1, transcendentals=0)
LARGE_COST = pl.CostEstimate(flops=10**10, bytes_accessed=10**8, transcendentals=0)
NORM_COST = pl.CostEstimate(flops=10**7, bytes_accessed=5 * 10**6, transcendentals=0)

f32 = jnp.float32
bf16 = jnp.bfloat16


def swap(value, axis, step):
    count = lax.axis_size(axis)
    return lax.ppermute(value, axis, [(i, i ^ step) for i in range(count)])


def tie(*values):
    return lax.optimization_barrier(values)


def pick(array, index, dim):
    return lax.dynamic_index_in_dim(array, index, dim, keepdims=False)


def rms_factor(rows):
    return lax.rsqrt(jnp.mean(rows * rows, axis=-1, keepdims=True) + epsilon)


def norm_back(rows, factor, gain, upstream):
    scaled = upstream * gain
    inner = jnp.mean(scaled * rows, axis=-1, keepdims=True)
    return factor * scaled - rows * factor * factor * factor * inner


def contract_rows(left, right):
    return lax.dot_general(left, right, (((0,), (0,)), ((), ())), preferred_element_type=f32)


def contract_cols(left, right):
    return lax.dot_general(left, right, (((1,), (1,)), ((), ())), preferred_element_type=f32)


def gather_gx(block):
    return [block] + [swap(block, "gx", s) for s in range(1, lax.axis_size("gx"))]


def over_y(value):
    return [swap(value, "gt", s) for s in range(1, lax.axis_size("gt"))]


def spread_y(values):
    return [swap(value, "gt", s) for s, value in enumerate(values, 1)]


def part_places():
    many = lax.axis_size("gt")
    places = [0, 2] + [4 * s for s in range(1, many)] + [4 * s + 2 for s in range(1, many)]
    return places + [p + 1 for p in places]


def own_place():
    me = (lax.axis_index("gt") * 2 + lax.axis_index("gw")) * 2 + lax.axis_index("co")
    return jnp.full((1,), me, jnp.int32)


def own_side():
    return jnp.full((1,), lax.axis_index("gw"), jnp.int32)


def halve_weights(gate, up, down):
    experts, rows, full = gate.shape
    half = full // 2

    def kernel(side_ref, gate_ref, up_ref, down_ref, keep, give):
        def put(low, out):
            for i, ref in enumerate((gate_ref, up_ref, down_ref)):
                out[0, :, i * half : (i + 1) * half] = ref[0, :, low : low + half]

        @pl.when(side_ref[0] == 0)
        def _():
            put(0, keep)
            put(half, give)

        @pl.when(side_ref[0] != 0)
        def _():
            put(half, keep)
            put(0, give)

    def block(columns):
        return pl.BlockSpec((1, rows, columns), lambda e, *_: (e, 0, 0))

    shape = jax.ShapeDtypeStruct((experts, rows, 3 * half), bf16)
    return pl.pallas_call(
        kernel,
        grid_spec=pltpu.PrefetchScalarGridSpec(
            num_scalar_prefetch=1,
            grid=(experts,),
            in_specs=[block(full)] * 3,
            out_specs=[block(3 * half)] * 2,
        ),
        out_shape=[shape, shape],
        cost_estimate=LARGE_COST,
        name="halve_weights",
    )(own_side(), gate, up, down)


def finish_gradients(summed, crossed, start, before, total_experts):
    experts, rows, columns = crossed.shape
    half = columns // 3
    count = len(summed)
    aliased = 0 if before is None else 3

    def kernel(side_ref, *refs):
        total = 0.0
        for ref in refs[:count]:
            total = total + (ref[0, 0] if len(ref.shape) == 4 else ref[0]).astype(f32)
        other = refs[count][0].astype(f32)

        def put(low, value):
            for i, out in enumerate(refs[count + 1 + aliased :]):
                out[0, :, low : low + half] = value[:, i * half : (i + 1) * half]

        @pl.when(side_ref[0] == 0)
        def _():
            put(0, total)
            put(half, other)

        @pl.when(side_ref[0] != 0)
        def _():
            put(half, total)
            put(0, other)

    def block(columns, first):
        return pl.BlockSpec((1, rows, columns), lambda e, *_: (e + first, 0, 0))

    shape = jax.ShapeDtypeStruct((total_experts, rows, 2 * half), f32)
    return pl.pallas_call(
        kernel,
        grid_spec=pltpu.PrefetchScalarGridSpec(
            num_scalar_prefetch=1,
            grid=(experts,),
            in_specs=[
                pl.BlockSpec((1, 1, rows, columns), lambda e, *_: (0, e, 0, 0)) if v.ndim == 4 else block(columns, 0)
                for v in summed
            ]
            + [block(columns, 0)]
            + [pl.BlockSpec(memory_space=pl.ANY)] * aliased,
            out_specs=[block(2 * half, start)] * 3,
        ),
        out_shape=[shape] * 3,
        input_output_aliases={count + 2 + i: i for i in range(aliased)},
        cost_estimate=LARGE_COST,
        name="finish_gradients",
    )(own_side(), *summed, crossed, *(before or ()))


def others_of(value, axes):
    count = lax.axis_size(axes)
    return [lax.ppermute(value, axes, [(i, i ^ s) for i in range(count)]) for s in range(1, count)]


def norm_forward(branch, tokens, gain):
    rows, width = tokens.shape

    def kernel(gain_ref, tokens_ref, *refs):
        middle_out, factor_out, normed_out = refs[len(branch) :]
        total = refs[0][...].astype(f32)
        for ref in refs[1 : len(branch)]:
            total = total + ref[...].astype(f32)
        middle = tokens_ref[...].astype(f32) + residual_factor * total
        factor = rms_factor(middle)
        middle_out[...] = middle
        factor_out[...] = factor
        normed_out[...] = (middle * factor * gain_ref[...]).astype(bf16)

    vmem = pl.BlockSpec(memory_space=pltpu.VMEM)
    return pl.pallas_call(
        kernel,
        out_shape=[
            jax.ShapeDtypeStruct((rows, width), f32),
            jax.ShapeDtypeStruct((rows, 1), f32),
            jax.ShapeDtypeStruct((rows, width), bf16),
        ],
        in_specs=[vmem] * (2 + len(branch)),
        out_specs=[vmem] * 3,
        cost_estimate=NORM_COST,
        name="norm_forward",
    )(gain[None], tokens, *branch)


def norm_backward(upstreams, rows_of, factor, gain, added):
    rows, width = rows_of.shape

    def kernel(gain_ref, rows_ref, factor_ref, added_ref, *refs):
        rows_back, branch_back, gain_back = refs[len(upstreams) :]
        total = 0.0
        for ref in refs[: len(upstreams)]:
            total = total + (ref[0] if len(ref.shape) == 3 else ref[...]).astype(f32)
        values, factor = rows_ref[...].astype(f32), factor_ref[...]
        back = added_ref[...].astype(f32) + norm_back(values, factor, gain_ref[...], total)
        rows_back[...] = back
        branch_back[...] = (residual_factor * back).astype(bf16)
        gain_back[...] = jnp.sum(total * values * factor, axis=0, keepdims=True)

    def whole(x):
        block = (1,) + x.shape[1:] if len(x.shape) == 3 else x.shape
        zeros = (0,) * len(block)
        return pl.BlockSpec(block, lambda i: zeros)

    operands = [gain[None], rows_of, factor, added] + upstreams
    shapes = [((rows, width), f32), ((rows, width), bf16), ((1, width), f32)]
    shapes = [jax.ShapeDtypeStruct(*shape) for shape in shapes]
    return pl.pallas_call(
        kernel,
        grid=(1,),
        out_shape=shapes,
        in_specs=[whole(x) for x in operands],
        out_specs=[whole(x) for x in shapes],
        cost_estimate=NORM_COST,
        name="norm_backward",
    )(*operands)


def slot_mask(slot_row):
    wanted = lax.broadcasted_iota(jnp.int32, (CAP, slot_row.shape[1]), 0).astype(f32)
    return slot_row == wanted


def route_slots(gathered, order, first_expert, experts, width):
    blocks, tokens = gathered.shape[:2]

    def kernel(order_ref, first_ref, routing_ref, routes_out, slots_out, chances_out, slots_by, chances_by):
        earlier = lax.broadcasted_iota(jnp.int32, (tokens, tokens), 0)
        earlier = (earlier < lax.broadcasted_iota(jnp.int32, (tokens, tokens), 1)).astype(f32).astype(bf16)
        for b in range(blocks):
            routing = routing_ref[order_ref[b]].astype(f32).T
            routes = routing[:TOPK]
            chance = routing[TOPK : 2 * TOPK] + routing[2 * TOPK : 3 * TOPK]
            routes_out[b] = routes
            hits, chosen = [], []
            for e in range(experts):
                same = routes == (first_ref[0] + e).astype(f32)
                hits.append(jnp.sum(jnp.where(same, 1.0, 0.0), axis=0, keepdims=True))
                chosen.append(jnp.sum(jnp.where(same, chance, 0.0), axis=0, keepdims=True))
            hits, chosen = jnp.concatenate(hits, axis=0), jnp.concatenate(chosen, axis=0)
            rank = jnp.dot(hits.astype(bf16), earlier, preferred_element_type=f32)
            slots = jnp.where(hits > 0.0, rank, -1.0)
            slots_out[b] = slots
            chances_out[b] = chosen
            for e in range(experts):
                slots_by[e, b : b + 1, :] = slots[e : e + 1]
                chances_by[e, b : b + 1, :] = chosen[e : e + 1]

    def whole(*shape):
        zeros = (0,) * len(shape)
        return pl.BlockSpec(shape, lambda i, *_: zeros)

    shapes = [(blocks, TOPK, tokens)] + [(blocks, experts, tokens)] * 2 + [(experts, blocks, tokens)] * 2
    return pl.pallas_call(
        kernel,
        grid_spec=pltpu.PrefetchScalarGridSpec(
            num_scalar_prefetch=2,
            grid=(1,),
            in_specs=[pl.BlockSpec((blocks, tokens, 128), lambda i, *_: (0, 0, width // 128))],
            out_specs=[whole(*shape) for shape in shapes],
        ),
        out_shape=[jax.ShapeDtypeStruct(shape, f32) for shape in shapes],
        cost_estimate=SMALL_COST,
        name="route_slots",
    )(order, jnp.full((1,), first_expert, jnp.int32), gathered)


def gather_slots(sources, slots, width, order=None, first=0, before=None):
    blocks, experts, tokens = slots.shape
    listed = order is None
    steps = len(sources) if listed else blocks
    aliased = 0 if before is None else 1

    def find(slots_ref, rows, out_ref):
        mask = jnp.concatenate([slot_mask(slots_ref[0, e : e + 1, :]) for e in range(experts)], axis=0)
        found = jnp.dot(mask.astype(f32).astype(bf16), rows, preferred_element_type=f32)
        out_ref[...] = found.astype(bf16).reshape(experts, 1, CAP, width)

    def kernel_list(order_ref, slots_ref, *refs):
        out_ref, held = refs[steps + aliased :]
        for i in range(steps):

            @pl.when(pl.program_id(0) == i)
            def _(i=i):
                held[...] = refs[i][...]

        find(slots_ref, held[...], out_ref)

    def kernel_array(order_ref, slots_ref, rows_ref, out_ref):
        find(slots_ref, rows_ref[0], out_ref)

    if listed:
        specs = [pl.BlockSpec((tokens, width), lambda b, *_: (0, 0))] * steps
        specs = specs + [pl.BlockSpec(memory_space=pl.ANY)] * aliased
        scratch = [pltpu.VMEM((tokens, width), bf16)]
        order = jnp.zeros((1,), jnp.int32)
        sources = sources + [before] * aliased
    else:
        specs = [pl.BlockSpec((1, tokens, width), lambda b, order_ref: (order_ref[b], 0, 0))]
        scratch = []
        sources = [sources]
    return pl.pallas_call(
        kernel_list if listed else kernel_array,
        grid_spec=pltpu.PrefetchScalarGridSpec(
            num_scalar_prefetch=1,
            grid=(steps,),
            in_specs=[pl.BlockSpec((1, experts, tokens), lambda b, *_: (b + first, 0, 0))] + specs,
            out_specs=pl.BlockSpec((experts, 1, CAP, width), lambda b, *_: (0, b + first, 0, 0)),
            scratch_shapes=scratch,
        ),
        out_shape=jax.ShapeDtypeStruct((experts, blocks, CAP, width), bf16),
        input_output_aliases={2 + steps: 0} if aliased else {},
        compiler_params=pltpu.CompilerParams(vmem_limit_bytes=60 * 2**20),
        cost_estimate=LARGE_COST,
        name="gather_slots",
    )(order, slots, *sources)


def sum_slots(slot_rows, slots, ends):
    blocks, experts, tokens = slots.shape
    width = slot_rows[0].shape[3]
    starts = [0] + list(ends[:-1])

    def kernel(slots_ref, *refs):
        total, first = None, 0
        for ref in refs[: len(slot_rows)]:
            mine = ref.shape[0]
            mask = jnp.concatenate(
                [slot_mask(slots_ref[0, e : e + 1, :]) for e in range(first, first + mine)], axis=0
            )
            first = first + mine
            part = contract_rows(mask.astype(f32).astype(bf16), ref[...].reshape(mine * CAP, width))
            total = part if total is None else total + part
        total = total.astype(bf16)
        step = pl.program_id(0)
        for start, end, out in zip(starts, ends, refs[len(slot_rows) :]):

            @pl.when((step >= start) & (step < end))
            def _(out=out):
                out[0] = total

    def held(start, end):
        return pl.BlockSpec((1, tokens, width), lambda b: (jnp.clip(b - start, 0, end - start - 1), 0, 0))

    return pl.pallas_call(
        kernel,
        grid=(blocks,),
        in_specs=[pl.BlockSpec((1, experts, tokens), lambda b: (b, 0, 0))]
        + [pl.BlockSpec((r.shape[0], 1, CAP, width), lambda b: (0, b, 0, 0)) for r in slot_rows],
        out_specs=[held(start, end) for start, end in zip(starts, ends)],
        out_shape=[
            jax.ShapeDtypeStruct((end - start, tokens, width), bf16) for start, end in zip(starts, ends)
        ],
        compiler_params=pltpu.CompilerParams(vmem_limit_bytes=60 * 2**20),
        cost_estimate=LARGE_COST,
        name="sum_slots",
    )(slots, *slot_rows)


def run_experts(rows_in, back_in, weights, start, experts, slots, chances):
    blocks, _, width = rows_in.shape[1:]
    places = part_places()
    tokens = slots.shape[2]
    weights = [
        [(w, first) for w, first in part if first < start + experts and first + w.shape[0] > start]
        for part in weights
    ]
    flat = [piece for part in weights for piece in part]
    cut, half = flat[0][0].shape[1], flat[0][0].shape[2] // 3
    count = len(places)
    total_slots = blocks * CAP

    def kernel(me_ref, rows_ref, back_ref, slots_ref, chances_ref, *refs):
        rows_out, mixed_out, chance_out = refs[len(flat) : len(flat) + 3]
        grads = refs[len(flat) + 3 : len(flat) + 5]
        gu_full, d_full, gu_total, d_total = refs[len(flat) + 5 :]
        spots = [pl.ds(pl.multiple_of((me_ref[0] ^ place) * cut, cut), cut) for place in places]
        expert = start + pl.program_id(0)
        part_refs = iter(refs[: len(flat)])
        for spot, part in zip(spots, weights):
            for w, first in part:
                ref = next(part_refs)

                def put(spot=spot, ref=ref):
                    gu_full[spot, :] = ref[0, :, : 2 * half]
                    d_full[spot, :] = ref[0, :, 2 * half :]

                if len(part) == 1:
                    put()
                else:
                    pl.when((expert >= first) & (expert < first + w.shape[0]))(put)
        rows = rows_ref[0].reshape(total_slots, width)
        back = back_ref[0].reshape(total_slots, width)
        masks = [slot_mask(slots_ref[0, b : b + 1, :]) for b in range(blocks)]
        chance = jnp.concatenate(
            [
                jnp.sum(jnp.where(masks[b], chances_ref[0, b : b + 1, :], 0.0), axis=1, keepdims=True)
                for b in range(blocks)
            ],
            axis=0,
        )
        both = jnp.dot(rows, gu_full[...], preferred_element_type=f32)
        active_back = jnp.dot(back, d_full[...], preferred_element_type=f32) * residual_factor
        gate, upper = both[:, :half], both[:, half:]
        sigma = jax.nn.sigmoid(gate)
        silu = gate * sigma
        active = silu * upper
        chance_back = jnp.sum(active * active_back, axis=1, keepdims=True)
        for b in range(blocks):
            column = chance_back[b * CAP : (b + 1) * CAP]
            chance_out[0, b : b + 1, :] = jnp.sum(jnp.where(masks[b], column, 0.0), axis=0, keepdims=True)
        scaled = (active * chance).astype(bf16)
        active_back = active_back * chance
        gate_back = active_back * upper * (sigma * (1.0 + gate * (1.0 - sigma)))
        upper_back = active_back * silu
        both_back = jnp.concatenate([gate_back.astype(bf16), upper_back.astype(bf16)], axis=1)
        rows_out[0] = contract_cols(both_back, gu_full[...]).astype(bf16).reshape(blocks, CAP, width)
        mixed_out[0] = contract_cols(scaled, d_full[...]).astype(bf16).reshape(blocks, CAP, width)
        gu_total[...] = contract_rows(rows, both_back).astype(bf16)
        d_total[...] = (contract_rows(back, scaled) * residual_factor).astype(bf16)
        for spot, place in zip(spots, places):
            grads[place % 2][place // 2, 0, :, : 2 * half] = gu_total[spot, :]
            grads[place % 2][place // 2, 0, :, 2 * half :] = d_total[spot, :]

    def block(shape, first=0):
        zeros = (0,) * len(shape)
        return pl.BlockSpec((1,) + shape, lambda e, *_: (e + first,) + zeros)

    grad_shape = jax.ShapeDtypeStruct((count // 2, experts, cut, 3 * half), bf16)
    def held(size, first):
        return pl.BlockSpec(
            (1, cut, 3 * half), lambda e, *_: (jnp.clip(e + start - first, 0, size - 1), 0, 0)
        )

    slot_shape = jax.ShapeDtypeStruct((experts, blocks, CAP, width), bf16)
    out = pl.pallas_call(
        kernel,
        grid_spec=pltpu.PrefetchScalarGridSpec(
            num_scalar_prefetch=1,
            grid=(experts,),
            in_specs=[
                block((blocks, CAP, width), start),
                block((blocks, CAP, width), start),
                block((blocks, tokens), start),
                block((blocks, tokens), start),
            ]
            + [held(w.shape[0], first) for w, first in flat],
            out_specs=[block((blocks, CAP, width)), block((blocks, CAP, width)), block((blocks, tokens))]
            + [pl.BlockSpec((count // 2, 1, cut, 3 * half), lambda e, *_: (0, e, 0, 0))] * 2,
            scratch_shapes=[
                pltpu.VMEM((width, 2 * half), bf16),
                pltpu.VMEM((width, half), bf16),
                pltpu.VMEM((width, 2 * half), bf16),
                pltpu.VMEM((width, half), bf16),
            ],
        ),
        out_shape=[slot_shape, slot_shape, jax.ShapeDtypeStruct((experts, blocks, tokens), f32)]
        + [grad_shape] * 2,
        compiler_params=pltpu.CompilerParams(vmem_limit_bytes=60 * 2**20),
        cost_estimate=LARGE_COST,
        name="run_experts",
    )(own_place(), rows_in, back_in, slots, chances, *[w for w, _ in flat])
    return out


ATTENTION_PARAMS = pltpu.CompilerParams(vmem_limit_bytes=60 * 2**20)


def turned_half(x):
    lanes = lax.broadcasted_iota(jnp.int32, x.shape, 1) % HEAD_SIZE
    half = HEAD_SIZE // 2
    return jnp.where(lanes < half, -pltpu.roll(x, 128 - half, 1), pltpu.roll(x, half, 1))


def head(x, h):
    return x[:, h * HEAD_SIZE : (h + 1) * HEAD_SIZE]


def attention_forward(token_blocks, gain, parts, mirrors, tables, query_cols, key_cols):
    blocks = len(token_blocks)
    rows, width = token_blocks[0].shape
    length = rows * blocks
    count = len(parts)
    places = part_places()
    columns = query_cols + 2 * key_cols
    heads = query_cols // HEAD_SIZE
    ratio = query_cols // key_cols
    step = 256

    def kernel(me_ref, gain_ref, cosine_ref, sine_ref, down_ref, along_ref, *refs):
        token_refs, part_refs = refs[:blocks], refs[blocks : blocks + count + 1]
        full, normed, factors, qkv, heads_out, spread = refs[blocks + count + 1 : blocks + count + 7]
        branch = refs[blocks + count + 7 :]
        for i, ref in enumerate(part_refs[:count]):
            full[me_ref[0] ^ places[i]] = ref[...]
            full[me_ref[0] ^ places[count + i]] = part_refs[count][i]
        for s in range(blocks):
            x = token_refs[s][...].astype(f32)
            factor = rms_factor(x)
            span = slice(s * rows, (s + 1) * rows)
            factors[span, :] = factor
            normed[span, :] = (x * factor * gain_ref[...]).astype(bf16)
        weights = full[...].reshape(width, full.shape[2])
        projected = jnp.dot(normed[...], weights[:, :columns], preferred_element_type=f32)
        for g in range((query_cols + key_cols) // 128):
            span = slice(g * 128, (g + 1) * 128)
            x = projected[:, span]
            qkv[:, span] = (x * cosine_ref[...] + turned_half(x) * sine_ref[...]).astype(bf16)
        qkv[:, query_cols + key_cols :] = projected[:, query_cols + key_cols :].astype(bf16)
        for q in range(0, length, step):
            span = slice(q, q + step)
            mixed = []
            mask = along_ref[...] <= down_ref[span, :]
            query = qkv[span, :query_cols]
            for h in range(heads):
                key = head(qkv[:, query_cols : query_cols + key_cols], h // ratio)
                value = head(qkv[:, query_cols + key_cols :], h // ratio)
                scores = jnp.where(mask, contract_cols(head(query, h), key) * score_factor, masked_value)
                top = jnp.max(scores, axis=1, keepdims=True)
                exps = jnp.exp(scores - top)
                total = jnp.sum(exps, axis=1, keepdims=True)
                probs = (exps * (1.0 / total)).astype(bf16)
                mixed.append(jnp.dot(probs, value, preferred_element_type=f32).astype(bf16))
                spread[span, h : h + 1] = top + jnp.log(total)
            heads_out[span, :] = jnp.concatenate(mixed, axis=1)
        for s in range(blocks):
            part = contract_cols(heads_out[s * rows : (s + 1) * rows, :], weights[:, columns:])
            branch[s][...] = part.astype(bf16)

    vmem = pl.BlockSpec(memory_space=pltpu.VMEM)
    return pl.pallas_call(
        kernel,
        out_shape=[
            jax.ShapeDtypeStruct((2 * count,) + parts[0].shape, bf16),
            jax.ShapeDtypeStruct((length, width), bf16),
            jax.ShapeDtypeStruct((length, 1), f32),
            jax.ShapeDtypeStruct((length, columns), bf16),
            jax.ShapeDtypeStruct((length, query_cols), bf16),
            jax.ShapeDtypeStruct((length, heads), f32),
        ]
        + [jax.ShapeDtypeStruct((rows, width), bf16)] * blocks,
        in_specs=[pl.BlockSpec(memory_space=pltpu.SMEM)] + [vmem] * (6 + blocks + count),
        out_specs=[vmem] * (6 + blocks),
        compiler_params=ATTENTION_PARAMS,
        cost_estimate=SMALL_COST,
        name="attention_forward",
    )(own_place(), gain[None], *tables, *token_blocks, *parts, mirrors)


def attention_backward(pieces, token_blocks, tables, full, factors, qkv, spread, query_cols, key_cols):
    blocks = len(pieces)
    rows, width = pieces[0].shape
    length = rows * blocks
    columns = query_cols + 2 * key_cols
    heads = query_cols // HEAD_SIZE
    pairs = key_cols // HEAD_SIZE
    ratio = heads // pairs
    step = 256

    def kernel(cosine_ref, sine_ref, down_ref, along_ref, full_ref, factors_ref, qkv_ref, spread_ref, *refs):
        piece_refs, token_refs = refs[:blocks], refs[blocks : 2 * blocks]
        back, gain_back = refs[2 * blocks : 2 * blocks + 2]
        normed_back = refs[2 * blocks + 2 : 3 * blocks + 2]
        heads_back, turned = refs[3 * blocks + 2 :]
        weights = full_ref[...].reshape(width, full_ref.shape[2])
        for s in range(blocks):
            part = jnp.dot(piece_refs[s][...], weights[:, columns:], preferred_element_type=f32)
            heads_back[s * rows : (s + 1) * rows, :] = part.astype(bf16)
        key_back, value_back = [None] * pairs, [None] * pairs

        def add(total, value):
            return value if total is None else total + value

        for q in range(0, length, step):
            span = slice(q, q + step)
            mask = along_ref[...] <= down_ref[span, :]
            query = qkv_ref[span, :query_cols]
            upper = heads_back[span, :]
            query_back = []
            for h in range(heads):
                g = h // ratio
                key = head(qkv_ref[:, query_cols : query_cols + key_cols], g)
                value = head(qkv_ref[:, query_cols + key_cols :], g)
                query_h, upper_h = head(query, h), head(upper, h)
                scores = jnp.where(mask, contract_cols(query_h, key) * score_factor, masked_value)
                probs = jnp.exp(scores - spread_ref[span, h : h + 1])
                prob_back = contract_cols(upper_h, value)
                inner = jnp.sum(probs * prob_back, axis=1, keepdims=True)
                score_back = (probs * (prob_back - inner)).astype(bf16)
                query_back.append(jnp.dot(score_back, key, preferred_element_type=f32) * score_factor)
                key_back[g] = add(key_back[g], contract_rows(score_back, query_h))
                value_back[g] = add(value_back[g], contract_rows(probs.astype(bf16), upper_h))
            turned[span, :query_cols] = jnp.concatenate(query_back, axis=1)
        turned[:, query_cols:] = jnp.concatenate(
            [k * score_factor for k in key_back] + value_back, axis=1
        )
        for g in range((query_cols + key_cols) // 128):
            span = slice(g * 128, (g + 1) * 128)
            x = turned[:, span]
            back[:, span] = (x * cosine_ref[...] - turned_half(x) * sine_ref[...]).astype(bf16)
        back[:, query_cols + key_cols :] = turned[:, query_cols + key_cols :].astype(bf16)
        total = None
        for s in range(blocks):
            span = slice(s * rows, (s + 1) * rows)
            part = contract_cols(back[span, :], weights[:, :columns])
            normed_back[s][...] = part.astype(bf16)
            scaled = part * (token_refs[s][...].astype(f32) * factors_ref[span, :])
            total = add(total, jnp.sum(scaled, axis=0, keepdims=True))
        gain_back[...] = total

    vmem = pl.BlockSpec(memory_space=pltpu.VMEM)
    return pl.pallas_call(
        kernel,
        out_shape=[
            jax.ShapeDtypeStruct((length, columns), bf16),
            jax.ShapeDtypeStruct((1, width), f32),
        ]
        + [jax.ShapeDtypeStruct((rows, width), bf16)] * blocks,
        in_specs=[vmem] * (8 + 2 * blocks),
        out_specs=[vmem] * (2 + blocks),
        scratch_shapes=[pltpu.VMEM((length, query_cols), bf16), pltpu.VMEM((length, columns), f32)],
        compiler_params=ATTENTION_PARAMS,
        cost_estimate=LARGE_COST,
        name="attention_backward",
    )(*tables, full, factors, qkv, spread, *pieces, *token_blocks)


def attention_gradients(normed, back, pieces, heads):
    blocks = len(pieces)
    rows, width = pieces[0].shape
    columns = back.shape[1]
    both = columns + heads.shape[1]
    places = part_places()
    count = len(places)
    cut = width // count

    def kernel(me_ref, normed_ref, back_ref, heads_ref, *refs):
        keep, give, total = refs[blocks:]
        total[:, :columns] = contract_rows(normed_ref[...], back_ref[...]).astype(bf16)
        piece = jnp.concatenate([ref[...] for ref in refs[:blocks]], axis=0)
        total[:, columns:] = contract_rows(piece, heads_ref[...]).astype(bf16)
        for place in places:
            spot = pl.ds(pl.multiple_of((me_ref[0] ^ place) * cut, cut), cut)
            (give if place % 2 else keep)[place // 2] = total[spot, :]

    vmem = pl.BlockSpec(memory_space=pltpu.VMEM)
    shape = jax.ShapeDtypeStruct((count // 2, cut, both), bf16)
    return pl.pallas_call(
        kernel,
        out_shape=[shape, shape],
        in_specs=[pl.BlockSpec(memory_space=pltpu.SMEM)] + [vmem] * (3 + blocks),
        out_specs=[vmem] * 2,
        scratch_shapes=[pltpu.VMEM((width, both), bf16)],
        compiler_params=ATTENTION_PARAMS,
        cost_estimate=LARGE_COST,
        name="attention_gradients",
    )(own_place(), normed, back, heads, *pieces)


def local(
    tokens,
    first_gain,
    query_weight,
    key_matrix,
    value_matrix,
    out_weight,
    second_gain,
    gate_weight,
    up_weight,
    down_weight,
    routes,
    route_logits,
    cotangent,
):
    groups, many = lax.axis_size("gx"), lax.axis_size("gt")
    me_x, me_w = lax.axis_index("gx"), lax.axis_index("gw")
    own_tokens = tokens[0]
    rows, width = own_tokens.shape
    query_cols = query_weight.shape[1]
    key_cols = key_matrix.shape[1]
    query_heads = query_cols // HEAD_SIZE
    pair_heads = key_cols // HEAD_SIZE
    ratio = query_heads // pair_heads
    experts = gate_weight.shape[0]
    some = experts // 2
    spans = ((0, some), (some, experts - some))

    token_blocks = gather_gx(own_tokens)
    attention = jnp.concatenate(
        [query_weight, key_matrix, value_matrix, out_weight.T], axis=1
    )
    across = swap(attention, "gw", 1)
    along = over_y(attention)
    both = over_y(across)
    down_turned = jnp.swapaxes(down_weight, 1, 2)
    keep, give = halve_weights(gate_weight, up_weight, down_turned)
    attention_parts = [attention, across] + along + both
    attention_mirrors = swap(jnp.stack(attention_parts), "co", 1)
    positions = jnp.concatenate(
        [(me_x ^ s) * rows + jnp.arange(rows, dtype=jnp.int32) for s in range(groups)]
    ).astype(f32)
    half = HEAD_SIZE // 2
    freq = rope_base ** (-(jnp.arange(half, dtype=f32) * 2.0 / HEAD_SIZE))
    angle = positions[:, None] * jnp.tile(freq, 128 // half)[None, :]
    tables = (jnp.cos(angle), jnp.sin(angle), positions[:, None], positions[None, :])
    token_blocks, tables, attention_mirrors, give, keep = tie(
        token_blocks, tables, attention_mirrors, give, keep
    )
    across_w, along_w = swap(give, "gw", 1), over_y(keep)
    mirror_keep = swap(keep, "co", 1)

    logits = route_logits[0].T
    weights = jnp.exp(logits - jnp.max(logits, axis=0, keepdims=True))
    chance = weights / jnp.sum(weights, axis=0, keepdims=True)
    chance_high = lax.reduce_precision(chance, 8, 7)
    routing = jnp.concatenate([routes[0].T.astype(f32), chance_high, chance - chance_high], axis=0)
    routing = jnp.pad(routing.astype(bf16).T, ((0, 0), (0, 128 - 3 * TOPK)))
    payload = jnp.concatenate([cotangent[0], routing], axis=1)
    turned = jnp.stack([w * groups + (me_x ^ s) for w in range(2) for s in range(groups)])
    gathered = lax.all_gather(payload, "gx", axis=0)

    attention_full, normed_one, factor_all, qkv, heads, spread, *branch_parts = attention_forward(
        token_blocks, first_gain, attention_parts, attention_mirrors, tables, query_cols, key_cols
    )

    branch_parts, mirror_keep = tie(branch_parts, mirror_keep)
    branch_got = [swap(branch_parts[s], "gx", s) for s in range(1, groups)]
    across_w, gathered, branch_got = tie(across_w, gathered, branch_got)
    gathered_across = swap(gathered, "gw", 1)
    middle, factor_two, normed_two = norm_forward([branch_parts[0]] + branch_got, own_tokens, second_gain)

    middle_part = experts * 7 // 10
    normed_two, across_w, along_w = tie(normed_two, across_w, along_w)
    normed_parts = gather_gx(normed_two)
    both_0 = over_y(across_w[:middle_part])
    turned_parts = {s: swap(normed_parts[s], "gw", 1) for s in (0, 1)}

    gathered = jnp.concatenate([gathered, gathered_across])
    routes_of, slots, _, slots_by, chances_by = route_slots(gathered, turned, me_x * experts, experts, width)
    back_in = gather_slots(gathered, slots, width, order=turned)
    normed_parts, turned_parts[0], turned_parts[1], both_0, across_w, along_w, back_in = tie(
        normed_parts, turned_parts[0], turned_parts[1], both_0, across_w, along_w, back_in
    )

    rest = [s for s in range(groups) if s not in (0, 1)]
    turned_rest = swap(jnp.stack([normed_parts[s] for s in rest]), "gw", 1)
    both_1 = over_y(across_w[middle_part:])
    mirror_w = [swap(v, "co", 1) for v in [across_w] + along_w]
    mirror_both_0 = [swap(v, "co", 1) for v in both_0]
    normed_rows = normed_parts + [turned_parts[0], turned_parts[1]]
    rows_in = gather_slots(normed_rows, slots, width)
    turned_rest, both_1, rows_in = tie(turned_rest, both_1, rows_in)
    rest_rows = [turned_rest[i] for i in range(len(rest))]
    rows_in = gather_slots(rest_rows, slots, width, first=len(normed_rows), before=rows_in)
    mirror_both_1 = [swap(v, "co", 1) for v in both_1]
    rows_in, mirror_w, mirror_both_0, mirror_both_1 = tie(rows_in, mirror_w, mirror_both_0, mirror_both_1)

    def halved(boths):
        return [[(first, 0), (second, middle_part)] for first, second in zip(*boths)]

    parts = [[(v, 0)] for v in [keep, across_w] + along_w] + halved((both_0, both_1))
    parts = parts + [[(v, 0)] for v in [mirror_keep] + mirror_w] + halved((mirror_both_0, mirror_both_1))
    rows_back, mixed_parts, chance_parts, gradients, given = [], [], [], [], []
    for i, (start, size) in enumerate(spans):
        if i == 1:
            rows_in, rows_back[0] = tie(rows_in, rows_back[0])
        result = run_experts(rows_in, back_in, parts, start, size, slots_by, chances_by)
        for lot, value in zip((rows_back, mixed_parts, chance_parts, gradients, given), result):
            lot.append(value)

    got = [None, None]

    def joint(i, t, w):
        return gradients[i][2 * t + w].astype(f32) + got[i][2 * t + w].astype(f32)

    others = range(1, many)
    got[0] = swap(given[0], "co", 1)
    got[0], rows_back = tie(got[0], rows_back)
    far = [joint(0, t, 1).astype(bf16) for t in others]
    far, given[1] = tie(far, given[1])
    got[1] = swap(given[1], "co", 1)
    along_one_0 = spread_y(far)
    summed, *turned_sums = sum_slots(rows_back, slots, (groups, groups + 2, 2 * groups))
    pieces = ((2, groups), (0, 2))
    crossed = [swap(turned_sums[1], "gw", 1), swap(turned_sums[0], "gw", 1)]
    far = [joint(1, t, 1).astype(bf16) for t in others]
    mixed_rows, mixed_turned = sum_slots(mixed_parts, slots, (groups, 2 * groups))
    crossed[0], mixed_rows, mixed_turned = tie(crossed[0], mixed_rows, mixed_turned)

    def half_sum(s):
        a, b = pieces[0] if s >= 2 else pieces[1]
        value = crossed[0] if s >= 2 else crossed[1]
        return summed[s].astype(f32) + value[s - a].astype(f32)

    normed_got = {s: swap(half_sum(s).astype(bf16), "gx", s) for s in range(2, groups)}
    along_one_0, far, got[1], crossed[1] = tie(along_one_0, far, got[1], crossed[1])
    along_one_1 = spread_y(far)
    crossed[1], normed_got[3] = tie(crossed[1], normed_got[3])
    normed_got[1] = swap(half_sum(1).astype(bf16), "gx", 1)
    chance_part = jnp.swapaxes(jnp.concatenate(chance_parts, axis=0), 0, 1)
    ids = (me_x * experts + jnp.arange(experts, dtype=jnp.int32)).astype(f32)
    same = routes_of[:, None, :, :] == ids[None, :, None, None]
    chance_rows = jnp.sum(jnp.where(same, chance_part[:, :, None, :], 0.0), axis=1)
    middle_back, branch_back, second_part = norm_backward(
        [summed, crossed[1]] + list(normed_got.values()), middle, factor_two, second_gain, cotangent[0]
    )
    branch_back_blocks = gather_gx(branch_back)
    mixed_turned, crossed[1] = tie(mixed_turned, crossed[1])
    mixed_crossed = swap(mixed_turned, "gw", 1)
    branch_back_blocks[1], gradients[0], along_one_1, mixed_crossed = tie(
        branch_back_blocks[1], gradients[0], along_one_1, mixed_crossed
    )
    far = [joint(0, t, 0).astype(bf16) for t in others]
    along_zero_0 = spread_y(far)

    def near(i, along):
        total = joint(i, 0, 1)
        for value in along:
            total = total + value.astype(f32)
        return total.astype(bf16)

    near_0, mixed_crossed = tie(near(0, along_one_0), mixed_crossed)
    crossed_0 = swap(near_0, "gw", 1)
    branch_back_blocks[1], got[1] = tie(branch_back_blocks[1], got[1])
    near_1 = near(1, along_one_1)
    far = [joint(1, t, 0).astype(bf16) for t in others]
    mixed_rows = mixed_rows.astype(f32) + mixed_crossed.astype(f32)
    mixed_send = mixed_rows.astype(bf16)
    branch_back_blocks, near_1, far, mixed_send, chance_rows = tie(
        branch_back_blocks, near_1, far, mixed_send, chance_rows
    )
    mixed_got = [swap(mixed_send[s], "gx", s) for s in range(1, groups)]
    far_last, near_last = far, near_1

    back, first_part, *normed_one_parts = attention_backward(
        branch_back_blocks, token_blocks, tables, attention_full, factor_all, qkv, spread, query_cols, key_cols
    )
    back, along_zero_0, crossed_0, far_last, near_last = tie(back, along_zero_0, crossed_0, far_last, near_last)
    along_zero_1 = spread_y(far_last)
    crossed_1 = swap(near_last, "gw", 1)
    keep_gradient, give_gradient = attention_gradients(normed_one, back, branch_back_blocks, heads)
    normed_one_parts, mixed_got, give_gradient = tie(normed_one_parts, mixed_got, give_gradient)
    got_gradient = swap(give_gradient, "co", 1)
    mixed = mixed_rows[0]
    for value in mixed_got:
        mixed = mixed + value.astype(f32)
    output = (middle + residual_factor * mixed).astype(bf16)
    normed_got = [swap(normed_one_parts[s], "gx", s) for s in range(1, groups)]
    gains = jnp.concatenate([first_part, second_part])
    gains = gains + swap(gains, "co", 1)
    total = keep_gradient.astype(f32) + got_gradient.astype(f32)
    far_attention = [total[2 * t : 2 * t + 2].astype(bf16) for t in others]
    sums = finish_gradients([gradients[0], got[0]] + along_zero_0, crossed_0, 0, None, experts)
    normed_got, far_attention, along_zero_1, gains, chance_rows, sums = tie(
        normed_got, far_attention, along_zero_1, gains, chance_rows, sums
    )
    far_attention = spread_y(far_attention)
    gains_got = others_of(gains, ("gt", "gw"))
    chance_crossed = swap(chance_rows[groups:], "gw", 1)
    sums = finish_gradients([gradients[1], got[1]] + along_zero_1, crossed_1, some, sums, experts)
    gate_sum, up_sum, down_sum = sums
    for value in gains_got:
        gains = gains + value
    for value in others_of(gains, ("gx",)):
        gains = gains + value
    attention_sum = total[:2]
    for value in far_attention:
        attention_sum = attention_sum + value.astype(f32)
    attention_sum = attention_sum[0] + swap(attention_sum[1].astype(bf16), "gw", 1).astype(f32)
    tokens_back, _, _ = norm_backward(
        [normed_one_parts[0]] + normed_got, own_tokens, factor_all[:rows], first_gain, middle_back
    )
    chance_rows = chance_rows[:groups] + chance_crossed
    chance_back = chance_rows[0]
    for s in range(1, groups):
        chance_back = chance_back + swap(chance_rows[s], "gx", s)
    logit_back = chance * (chance_back - jnp.sum(chance * chance_back, axis=0, keepdims=True))
    return (
        output[None],
        tokens_back[None],
        gains[0],
        attention_sum[:, :query_cols],
        attention_sum[:, query_cols : query_cols + key_cols],
        attention_sum[:, query_cols + key_cols : query_cols + 2 * key_cols],
        attention_sum[:, query_cols + 2 * key_cols :].T,
        gains[1],
        gate_sum,
        up_sum,
        jnp.swapaxes(down_sum, 1, 2),
        logit_back.T[None],
    )


def solution(mesh):
    groups, others = mesh.shape["gx"], mesh.shape["gy"]
    split = Mesh(mesh.devices.reshape(groups, others // 4, 2, 2), ("gx", "gt", "gw", "co"))
    gy = ("gt", "gw", "co")
    in_specs = (
        P(gy, "gx", None),
        P(),
        P(gy, "gx"),
        P(gy, "gx"),
        P(gy, "gx"),
        P("gx", gy),
        P(),
        P("gx", gy, None),
        P("gx", gy, None),
        P("gx", None, gy),
        P(gy, "gx", None),
        P(gy, "gx", None),
        P(gy, "gx", None),
    )
    out_specs = (
        P(gy, "gx", None),
        P(gy, "gx", None),
        P(),
        P(gy, "gx"),
        P(gy, "gx"),
        P(gy, "gx"),
        P("gx", gy),
        P(),
        P("gx", gy, None),
        P("gx", gy, None),
        P("gx", None, gy),
        P(gy, "gx", None),
    )
    return jax.shard_map(local, mesh=split, in_specs=in_specs, out_specs=out_specs, check_vma=False)
```

```python
import functools

import jax
import jax.numpy as jnp
from jax import lax
from jax.experimental import pallas as pl
from jax.experimental.pallas import tpu as pltpu
from jax.sharding import Mesh, PartitionSpec as P

HEAD_SIZE = 64
EXPERTS = 40
TOPK = 8
CAP = 48

epsilon = 1e-06
rope_base = 10000.0
residual_factor = 0.22
score_factor = 0.015625
masked_value = -1e30

SMALL_COST = pl.CostEstimate(flops=1, bytes_accessed=1, transcendentals=0)
LARGE_COST = pl.CostEstimate(flops=10**10, bytes_accessed=10**8, transcendentals=0)
NORM_COST = pl.CostEstimate(flops=10**7, bytes_accessed=5 * 10**6, transcendentals=0)

f32 = jnp.float32
bf16 = jnp.bfloat16


def swap(value, axis, step):
    count = lax.axis_size(axis)
    return lax.ppermute(value, axis, [(i, i ^ step) for i in range(count)])


def tie(*values):
    return lax.optimization_barrier(values)


def pick(array, index, dim):
    return lax.dynamic_index_in_dim(array, index, dim, keepdims=False)


def rms_factor(rows):
    return lax.rsqrt(jnp.mean(rows * rows, axis=-1, keepdims=True) + epsilon)


def norm_back(rows, factor, gain, upstream):
    scaled = upstream * gain
    inner = jnp.mean(scaled * rows, axis=-1, keepdims=True)
    return factor * scaled - rows * factor * factor * factor * inner


def contract_rows(left, right):
    return lax.dot_general(left, right, (((0,), (0,)), ((), ())), preferred_element_type=f32)


def contract_cols(left, right):
    return lax.dot_general(left, right, (((1,), (1,)), ((), ())), preferred_element_type=f32)


def gather_gx(block):
    return [block] + [swap(block, "gx", s) for s in range(1, lax.axis_size("gx"))]


def over_y(value):
    return [swap(value, "gt", s) for s in range(1, lax.axis_size("gt"))]


def spread_y(values):
    return [swap(value, "gt", s) for s, value in enumerate(values, 1)]


def part_places():
    many = lax.axis_size("gt")
    places = [0, 2] + [4 * s for s in range(1, many)] + [4 * s + 2 for s in range(1, many)]
    return places + [p + 1 for p in places]


def own_place():
    me = (lax.axis_index("gt") * 2 + lax.axis_index("gw")) * 2 + lax.axis_index("co")
    return jnp.full((1,), me, jnp.int32)


def own_side():
    return jnp.full((1,), lax.axis_index("gw"), jnp.int32)


def halve_weights(gate, up, down):
    experts, rows, full = gate.shape
    half = full // 2

    def kernel(side_ref, gate_ref, up_ref, down_ref, keep, give):
        def put(low, out):
            for i, ref in enumerate((gate_ref, up_ref, down_ref)):
                out[0, :, i * half : (i + 1) * half] = ref[0, :, low : low + half]

        @pl.when(side_ref[0] == 0)
        def _():
            put(0, keep)
            put(half, give)

        @pl.when(side_ref[0] != 0)
        def _():
            put(half, keep)
            put(0, give)

    def block(columns):
        return pl.BlockSpec((1, rows, columns), lambda e, *_: (e, 0, 0))

    shape = jax.ShapeDtypeStruct((experts, rows, 3 * half), bf16)
    return pl.pallas_call(
        kernel,
        grid_spec=pltpu.PrefetchScalarGridSpec(
            num_scalar_prefetch=1,
            grid=(experts,),
            in_specs=[block(full)] * 3,
            out_specs=[block(3 * half)] * 2,
        ),
        out_shape=[shape, shape],
        cost_estimate=LARGE_COST,
        name="halve_weights",
    )(own_side(), gate, up, down)


def finish_gradients(summed, crossed, start, before, total_experts):
    experts, rows, columns = crossed.shape
    half = columns // 3
    count = len(summed)
    aliased = 0 if before is None else 3

    def kernel(side_ref, *refs):
        total = 0.0
        for ref in refs[:count]:
            total = total + (ref[0, 0] if len(ref.shape) == 4 else ref[0]).astype(f32)
        other = refs[count][0].astype(f32)

        def put(low, value):
            for i, out in enumerate(refs[count + 1 + aliased :]):
                out[0, :, low : low + half] = value[:, i * half : (i + 1) * half]

        @pl.when(side_ref[0] == 0)
        def _():
            put(0, total)
            put(half, other)

        @pl.when(side_ref[0] != 0)
        def _():
            put(half, total)
            put(0, other)

    def block(columns, first):
        return pl.BlockSpec((1, rows, columns), lambda e, *_: (e + first, 0, 0))

    shape = jax.ShapeDtypeStruct((total_experts, rows, 2 * half), f32)
    return pl.pallas_call(
        kernel,
        grid_spec=pltpu.PrefetchScalarGridSpec(
            num_scalar_prefetch=1,
            grid=(experts,),
            in_specs=[
                pl.BlockSpec((1, 1, rows, columns), lambda e, *_: (0, e, 0, 0)) if v.ndim == 4 else block(columns, 0)
                for v in summed
            ]
            + [block(columns, 0)]
            + [pl.BlockSpec(memory_space=pl.ANY)] * aliased,
            out_specs=[block(2 * half, start)] * 3,
        ),
        out_shape=[shape] * 3,
        input_output_aliases={count + 2 + i: i for i in range(aliased)},
        cost_estimate=LARGE_COST,
        name="finish_gradients",
    )(own_side(), *summed, crossed, *(before or ()))


def others_of(value, axes):
    count = lax.axis_size(axes)
    return [lax.ppermute(value, axes, [(i, i ^ s) for i in range(count)]) for s in range(1, count)]


def norm_forward(branch, tokens, gain):
    rows, width = tokens.shape

    def kernel(gain_ref, tokens_ref, *refs):
        middle_out, factor_out, normed_out = refs[len(branch) :]
        total = refs[0][...].astype(f32)
        for ref in refs[1 : len(branch)]:
            total = total + ref[...].astype(f32)
        middle = tokens_ref[...].astype(f32) + residual_factor * total
        factor = rms_factor(middle)
        middle_out[...] = middle
        factor_out[...] = factor
        normed_out[...] = (middle * factor * gain_ref[...]).astype(bf16)

    vmem = pl.BlockSpec(memory_space=pltpu.VMEM)
    return pl.pallas_call(
        kernel,
        out_shape=[
            jax.ShapeDtypeStruct((rows, width), f32),
            jax.ShapeDtypeStruct((rows, 1), f32),
            jax.ShapeDtypeStruct((rows, width), bf16),
        ],
        in_specs=[vmem] * (2 + len(branch)),
        out_specs=[vmem] * 3,
        cost_estimate=NORM_COST,
        name="norm_forward",
    )(gain[None], tokens, *branch)


def norm_backward(upstreams, rows_of, factor, gain, added):
    rows, width = rows_of.shape

    def kernel(gain_ref, rows_ref, factor_ref, added_ref, *refs):
        rows_back, branch_back, gain_back = refs[len(upstreams) :]
        total = 0.0
        for ref in refs[: len(upstreams)]:
            total = total + (ref[0] if len(ref.shape) == 3 else ref[...]).astype(f32)
        values, factor = rows_ref[...].astype(f32), factor_ref[...]
        back = added_ref[...].astype(f32) + norm_back(values, factor, gain_ref[...], total)
        rows_back[...] = back
        branch_back[...] = (residual_factor * back).astype(bf16)
        gain_back[...] = jnp.sum(total * values * factor, axis=0, keepdims=True)

    def whole(x):
        block = (1,) + x.shape[1:] if len(x.shape) == 3 else x.shape
        zeros = (0,) * len(block)
        return pl.BlockSpec(block, lambda i: zeros)

    operands = [gain[None], rows_of, factor, added] + upstreams
    shapes = [((rows, width), f32), ((rows, width), bf16), ((1, width), f32)]
    shapes = [jax.ShapeDtypeStruct(*shape) for shape in shapes]
    return pl.pallas_call(
        kernel,
        grid=(1,),
        out_shape=shapes,
        in_specs=[whole(x) for x in operands],
        out_specs=[whole(x) for x in shapes],
        cost_estimate=NORM_COST,
        name="norm_backward",
    )(*operands)


def slot_mask(slot_row):
    wanted = lax.broadcasted_iota(jnp.int32, (CAP, slot_row.shape[1]), 0).astype(f32)
    return slot_row == wanted


def route_slots(gathered, order, first_expert, experts, width):
    blocks, tokens = gathered.shape[:2]

    def kernel(order_ref, first_ref, routing_ref, routes_out, slots_out, chances_out, slots_by, chances_by):
        earlier = lax.broadcasted_iota(jnp.int32, (tokens, tokens), 0)
        earlier = (earlier < lax.broadcasted_iota(jnp.int32, (tokens, tokens), 1)).astype(f32).astype(bf16)
        for b in range(blocks):
            routing = routing_ref[order_ref[b]].astype(f32).T
            routes = routing[:TOPK]
            chance = routing[TOPK : 2 * TOPK] + routing[2 * TOPK : 3 * TOPK]
            routes_out[b] = routes
            hits, chosen = [], []
            for e in range(experts):
                same = routes == (first_ref[0] + e).astype(f32)
                hits.append(jnp.sum(jnp.where(same, 1.0, 0.0), axis=0, keepdims=True))
                chosen.append(jnp.sum(jnp.where(same, chance, 0.0), axis=0, keepdims=True))
            hits, chosen = jnp.concatenate(hits, axis=0), jnp.concatenate(chosen, axis=0)
            rank = jnp.dot(hits.astype(bf16), earlier, preferred_element_type=f32)
            slots = jnp.where(hits > 0.0, rank, -1.0)
            slots_out[b] = slots
            chances_out[b] = chosen
            for e in range(experts):
                slots_by[e, b : b + 1, :] = slots[e : e + 1]
                chances_by[e, b : b + 1, :] = chosen[e : e + 1]

    def whole(*shape):
        zeros = (0,) * len(shape)
        return pl.BlockSpec(shape, lambda i, *_: zeros)

    shapes = [(blocks, TOPK, tokens)] + [(blocks, experts, tokens)] * 2 + [(experts, blocks, tokens)] * 2
    return pl.pallas_call(
        kernel,
        grid_spec=pltpu.PrefetchScalarGridSpec(
            num_scalar_prefetch=2,
            grid=(1,),
            in_specs=[pl.BlockSpec((blocks, tokens, 128), lambda i, *_: (0, 0, width // 128))],
            out_specs=[whole(*shape) for shape in shapes],
        ),
        out_shape=[jax.ShapeDtypeStruct(shape, f32) for shape in shapes],
        cost_estimate=SMALL_COST,
        name="route_slots",
    )(order, jnp.full((1,), first_expert, jnp.int32), gathered)


def gather_slots(sources, slots, width, order=None, first=0, before=None):
    blocks, experts, tokens = slots.shape
    listed = order is None
    steps = len(sources) if listed else blocks
    aliased = 0 if before is None else 1

    def find(slots_ref, rows, out_ref):
        mask = jnp.concatenate([slot_mask(slots_ref[0, e : e + 1, :]) for e in range(experts)], axis=0)
        found = jnp.dot(mask.astype(f32).astype(bf16), rows, preferred_element_type=f32)
        out_ref[...] = found.astype(bf16).reshape(experts, 1, CAP, width)

    def kernel_list(order_ref, slots_ref, *refs):
        out_ref, held = refs[steps + aliased :]
        for i in range(steps):

            @pl.when(pl.program_id(0) == i)
            def _(i=i):
                held[...] = refs[i][...]

        find(slots_ref, held[...], out_ref)

    def kernel_array(order_ref, slots_ref, rows_ref, out_ref):
        find(slots_ref, rows_ref[0], out_ref)

    if listed:
        specs = [pl.BlockSpec((tokens, width), lambda b, *_: (0, 0))] * steps
        specs = specs + [pl.BlockSpec(memory_space=pl.ANY)] * aliased
        scratch = [pltpu.VMEM((tokens, width), bf16)]
        order = jnp.zeros((1,), jnp.int32)
        sources = sources + [before] * aliased
    else:
        specs = [pl.BlockSpec((1, tokens, width), lambda b, order_ref: (order_ref[b], 0, 0))]
        scratch = []
        sources = [sources]
    return pl.pallas_call(
        kernel_list if listed else kernel_array,
        grid_spec=pltpu.PrefetchScalarGridSpec(
            num_scalar_prefetch=1,
            grid=(steps,),
            in_specs=[pl.BlockSpec((1, experts, tokens), lambda b, *_: (b + first, 0, 0))] + specs,
            out_specs=pl.BlockSpec((experts, 1, CAP, width), lambda b, *_: (0, b + first, 0, 0)),
            scratch_shapes=scratch,
        ),
        out_shape=jax.ShapeDtypeStruct((experts, blocks, CAP, width), bf16),
        input_output_aliases={2 + steps: 0} if aliased else {},
        compiler_params=pltpu.CompilerParams(vmem_limit_bytes=60 * 2**20),
        cost_estimate=LARGE_COST,
        name="gather_slots",
    )(order, slots, *sources)


def sum_slots(slot_rows, slots, ends):
    blocks, experts, tokens = slots.shape
    width = slot_rows[0].shape[3]
    starts = [0] + list(ends[:-1])

    def kernel(slots_ref, *refs):
        total, first = None, 0
        for ref in refs[: len(slot_rows)]:
            mine = ref.shape[0]
            mask = jnp.concatenate(
                [slot_mask(slots_ref[0, e : e + 1, :]) for e in range(first, first + mine)], axis=0
            )
            first = first + mine
            part = contract_rows(mask.astype(f32).astype(bf16), ref[...].reshape(mine * CAP, width))
            total = part if total is None else total + part
        total = total.astype(bf16)
        step = pl.program_id(0)
        for start, end, out in zip(starts, ends, refs[len(slot_rows) :]):

            @pl.when((step >= start) & (step < end))
            def _(out=out):
                out[0] = total

    def held(start, end):
        return pl.BlockSpec((1, tokens, width), lambda b: (jnp.clip(b - start, 0, end - start - 1), 0, 0))

    return pl.pallas_call(
        kernel,
        grid=(blocks,),
        in_specs=[pl.BlockSpec((1, experts, tokens), lambda b: (b, 0, 0))]
        + [pl.BlockSpec((r.shape[0], 1, CAP, width), lambda b: (0, b, 0, 0)) for r in slot_rows],
        out_specs=[held(start, end) for start, end in zip(starts, ends)],
        out_shape=[
            jax.ShapeDtypeStruct((end - start, tokens, width), bf16) for start, end in zip(starts, ends)
        ],
        compiler_params=pltpu.CompilerParams(vmem_limit_bytes=60 * 2**20),
        cost_estimate=LARGE_COST,
        name="sum_slots",
    )(slots, *slot_rows)


def run_experts(rows_in, back_in, weights, start, experts, slots, chances):
    blocks, _, width = rows_in.shape[1:]
    places = part_places()
    tokens = slots.shape[2]
    weights = [
        [(w, first) for w, first in part if first < start + experts and first + w.shape[0] > start]
        for part in weights
    ]
    flat = [piece for part in weights for piece in part]
    cut, half = flat[0][0].shape[1], flat[0][0].shape[2] // 3
    count = len(places)
    total_slots = blocks * CAP

    def kernel(me_ref, rows_ref, back_ref, slots_ref, chances_ref, *refs):
        rows_out, mixed_out, chance_out = refs[len(flat) : len(flat) + 3]
        grads = refs[len(flat) + 3 : len(flat) + 5]
        gu_full, d_full, gu_total, d_total = refs[len(flat) + 5 :]
        spots = [pl.ds(pl.multiple_of((me_ref[0] ^ place) * cut, cut), cut) for place in places]
        expert = start + pl.program_id(0)
        part_refs = iter(refs[: len(flat)])
        for spot, part in zip(spots, weights):
            for w, first in part:
                ref = next(part_refs)

                def put(spot=spot, ref=ref):
                    gu_full[spot, :] = ref[0, :, : 2 * half]
                    d_full[spot, :] = ref[0, :, 2 * half :]

                if len(part) == 1:
                    put()
                else:
                    pl.when((expert >= first) & (expert < first + w.shape[0]))(put)
        rows = rows_ref[0].reshape(total_slots, width)
        back = back_ref[0].reshape(total_slots, width)
        masks = [slot_mask(slots_ref[0, b : b + 1, :]) for b in range(blocks)]
        chance = jnp.concatenate(
            [
                jnp.sum(jnp.where(masks[b], chances_ref[0, b : b + 1, :], 0.0), axis=1, keepdims=True)
                for b in range(blocks)
            ],
            axis=0,
        )
        both = jnp.dot(rows, gu_full[...], preferred_element_type=f32)
        active_back = jnp.dot(back, d_full[...], preferred_element_type=f32) * residual_factor
        gate, upper = both[:, :half], both[:, half:]
        sigma = jax.nn.sigmoid(gate)
        silu = gate * sigma
        active = silu * upper
        chance_back = jnp.sum(active * active_back, axis=1, keepdims=True)
        for b in range(blocks):
            column = chance_back[b * CAP : (b + 1) * CAP]
            chance_out[0, b : b + 1, :] = jnp.sum(jnp.where(masks[b], column, 0.0), axis=0, keepdims=True)
        scaled = (active * chance).astype(bf16)
        active_back = active_back * chance
        gate_back = active_back * upper * (sigma * (1.0 + gate * (1.0 - sigma)))
        upper_back = active_back * silu
        both_back = jnp.concatenate([gate_back.astype(bf16), upper_back.astype(bf16)], axis=1)
        rows_out[0] = contract_cols(both_back, gu_full[...]).astype(bf16).reshape(blocks, CAP, width)
        mixed_out[0] = contract_cols(scaled, d_full[...]).astype(bf16).reshape(blocks, CAP, width)
        gu_total[...] = contract_rows(rows, both_back).astype(bf16)
        d_total[...] = (contract_rows(back, scaled) * residual_factor).astype(bf16)
        for spot, place in zip(spots, places):
            grads[place % 2][place // 2, 0, :, : 2 * half] = gu_total[spot, :]
            grads[place % 2][place // 2, 0, :, 2 * half :] = d_total[spot, :]

    def block(shape, first=0):
        zeros = (0,) * len(shape)
        return pl.BlockSpec((1,) + shape, lambda e, *_: (e + first,) + zeros)

    grad_shape = jax.ShapeDtypeStruct((count // 2, experts, cut, 3 * half), bf16)
    def held(size, first):
        return pl.BlockSpec(
            (1, cut, 3 * half), lambda e, *_: (jnp.clip(e + start - first, 0, size - 1), 0, 0)
        )

    slot_shape = jax.ShapeDtypeStruct((experts, blocks, CAP, width), bf16)
    out = pl.pallas_call(
        kernel,
        grid_spec=pltpu.PrefetchScalarGridSpec(
            num_scalar_prefetch=1,
            grid=(experts,),
            in_specs=[
                block((blocks, CAP, width), start),
                block((blocks, CAP, width), start),
                block((blocks, tokens), start),
                block((blocks, tokens), start),
            ]
            + [held(w.shape[0], first) for w, first in flat],
            out_specs=[block((blocks, CAP, width)), block((blocks, CAP, width)), block((blocks, tokens))]
            + [pl.BlockSpec((count // 2, 1, cut, 3 * half), lambda e, *_: (0, e, 0, 0))] * 2,
            scratch_shapes=[
                pltpu.VMEM((width, 2 * half), bf16),
                pltpu.VMEM((width, half), bf16),
                pltpu.VMEM((width, 2 * half), bf16),
                pltpu.VMEM((width, half), bf16),
            ],
        ),
        out_shape=[slot_shape, slot_shape, jax.ShapeDtypeStruct((experts, blocks, tokens), f32)]
        + [grad_shape] * 2,
        compiler_params=pltpu.CompilerParams(vmem_limit_bytes=60 * 2**20),
        cost_estimate=LARGE_COST,
        name="run_experts",
    )(own_place(), rows_in, back_in, slots, chances, *[w for w, _ in flat])
    return out


ATTENTION_PARAMS = pltpu.CompilerParams(vmem_limit_bytes=60 * 2**20)


def turned_half(x):
    lanes = lax.broadcasted_iota(jnp.int32, x.shape, 1) % HEAD_SIZE
    half = HEAD_SIZE // 2
    return jnp.where(lanes < half, -pltpu.roll(x, 128 - half, 1), pltpu.roll(x, half, 1))


def head(x, h):
    return x[:, h * HEAD_SIZE : (h + 1) * HEAD_SIZE]


def attention_forward(token_blocks, gain, parts, mirrors, tables, query_cols, key_cols):
    blocks = len(token_blocks)
    rows, width = token_blocks[0].shape
    length = rows * blocks
    count = len(parts)
    places = part_places()
    columns = query_cols + 2 * key_cols
    heads = query_cols // HEAD_SIZE
    ratio = query_cols // key_cols
    step = 256

    def kernel(me_ref, gain_ref, cosine_ref, sine_ref, down_ref, along_ref, *refs):
        token_refs, part_refs = refs[:blocks], refs[blocks : blocks + count + 1]
        full, normed, factors, qkv, heads_out, spread = refs[blocks + count + 1 : blocks + count + 7]
        branch = refs[blocks + count + 7 :]
        for i, ref in enumerate(part_refs[:count]):
            full[me_ref[0] ^ places[i]] = ref[...]
            full[me_ref[0] ^ places[count + i]] = part_refs[count][i]
        for s in range(blocks):
            x = token_refs[s][...].astype(f32)
            factor = rms_factor(x)
            span = slice(s * rows, (s + 1) * rows)
            factors[span, :] = factor
            normed[span, :] = (x * factor * gain_ref[...]).astype(bf16)
        weights = full[...].reshape(width, full.shape[2])
        projected = jnp.dot(normed[...], weights[:, :columns], preferred_element_type=f32)
        for g in range((query_cols + key_cols) // 128):
            span = slice(g * 128, (g + 1) * 128)
            x = projected[:, span]
            qkv[:, span] = (x * cosine_ref[...] + turned_half(x) * sine_ref[...]).astype(bf16)
        qkv[:, query_cols + key_cols :] = projected[:, query_cols + key_cols :].astype(bf16)
        for q in range(0, length, step):
            span = slice(q, q + step)
            mixed = []
            mask = along_ref[...] <= down_ref[span, :]
            query = qkv[span, :query_cols]
            for h in range(heads):
                key = head(qkv[:, query_cols : query_cols + key_cols], h // ratio)
                value = head(qkv[:, query_cols + key_cols :], h // ratio)
                scores = jnp.where(mask, contract_cols(head(query, h), key) * score_factor, masked_value)
                top = jnp.max(scores, axis=1, keepdims=True)
                exps = jnp.exp(scores - top)
                total = jnp.sum(exps, axis=1, keepdims=True)
                probs = (exps * (1.0 / total)).astype(bf16)
                mixed.append(jnp.dot(probs, value, preferred_element_type=f32).astype(bf16))
                spread[span, h : h + 1] = top + jnp.log(total)
            heads_out[span, :] = jnp.concatenate(mixed, axis=1)
        for s in range(blocks):
            part = contract_cols(heads_out[s * rows : (s + 1) * rows, :], weights[:, columns:])
            branch[s][...] = part.astype(bf16)

    vmem = pl.BlockSpec(memory_space=pltpu.VMEM)
    return pl.pallas_call(
        kernel,
        out_shape=[
            jax.ShapeDtypeStruct((2 * count,) + parts[0].shape, bf16),
            jax.ShapeDtypeStruct((length, width), bf16),
            jax.ShapeDtypeStruct((length, 1), f32),
            jax.ShapeDtypeStruct((length, columns), bf16),
            jax.ShapeDtypeStruct((length, query_cols), bf16),
            jax.ShapeDtypeStruct((length, heads), f32),
        ]
        + [jax.ShapeDtypeStruct((rows, width), bf16)] * blocks,
        in_specs=[pl.BlockSpec(memory_space=pltpu.SMEM)] + [vmem] * (6 + blocks + count),
        out_specs=[vmem] * (6 + blocks),
        compiler_params=ATTENTION_PARAMS,
        cost_estimate=SMALL_COST,
        name="attention_forward",
    )(own_place(), gain[None], *tables, *token_blocks, *parts, mirrors)


def attention_backward(pieces, token_blocks, tables, full, factors, qkv, spread, query_cols, key_cols):
    blocks = len(pieces)
    rows, width = pieces[0].shape
    length = rows * blocks
    columns = query_cols + 2 * key_cols
    heads = query_cols // HEAD_SIZE
    pairs = key_cols // HEAD_SIZE
    ratio = heads // pairs
    step = 256

    def kernel(cosine_ref, sine_ref, down_ref, along_ref, full_ref, factors_ref, qkv_ref, spread_ref, *refs):
        piece_refs, token_refs = refs[:blocks], refs[blocks : 2 * blocks]
        back, gain_back = refs[2 * blocks : 2 * blocks + 2]
        normed_back = refs[2 * blocks + 2 : 3 * blocks + 2]
        heads_back, turned = refs[3 * blocks + 2 :]
        weights = full_ref[...].reshape(width, full_ref.shape[2])
        for s in range(blocks):
            part = jnp.dot(piece_refs[s][...], weights[:, columns:], preferred_element_type=f32)
            heads_back[s * rows : (s + 1) * rows, :] = part.astype(bf16)
        key_back, value_back = [None] * pairs, [None] * pairs

        def add(total, value):
            return value if total is None else total + value

        for q in range(0, length, step):
            span = slice(q, q + step)
            mask = along_ref[...] <= down_ref[span, :]
            query = qkv_ref[span, :query_cols]
            upper = heads_back[span, :]
            query_back = []
            for h in range(heads):
                g = h // ratio
                key = head(qkv_ref[:, query_cols : query_cols + key_cols], g)
                value = head(qkv_ref[:, query_cols + key_cols :], g)
                query_h, upper_h = head(query, h), head(upper, h)
                scores = jnp.where(mask, contract_cols(query_h, key) * score_factor, masked_value)
                probs = jnp.exp(scores - spread_ref[span, h : h + 1])
                prob_back = contract_cols(upper_h, value)
                inner = jnp.sum(probs * prob_back, axis=1, keepdims=True)
                score_back = (probs * (prob_back - inner)).astype(bf16)
                query_back.append(jnp.dot(score_back, key, preferred_element_type=f32) * score_factor)
                key_back[g] = add(key_back[g], contract_rows(score_back, query_h))
                value_back[g] = add(value_back[g], contract_rows(probs.astype(bf16), upper_h))
            turned[span, :query_cols] = jnp.concatenate(query_back, axis=1)
        turned[:, query_cols:] = jnp.concatenate(
            [k * score_factor for k in key_back] + value_back, axis=1
        )
        for g in range((query_cols + key_cols) // 128):
            span = slice(g * 128, (g + 1) * 128)
            x = turned[:, span]
            back[:, span] = (x * cosine_ref[...] - turned_half(x) * sine_ref[...]).astype(bf16)
        back[:, query_cols + key_cols :] = turned[:, query_cols + key_cols :].astype(bf16)
        total = None
        for s in range(blocks):
            span = slice(s * rows, (s + 1) * rows)
            part = contract_cols(back[span, :], weights[:, :columns])
            normed_back[s][...] = part.astype(bf16)
            scaled = part * (token_refs[s][...].astype(f32) * factors_ref[span, :])
            total = add(total, jnp.sum(scaled, axis=0, keepdims=True))
        gain_back[...] = total

    vmem = pl.BlockSpec(memory_space=pltpu.VMEM)
    return pl.pallas_call(
        kernel,
        out_shape=[
            jax.ShapeDtypeStruct((length, columns), bf16),
            jax.ShapeDtypeStruct((1, width), f32),
        ]
        + [jax.ShapeDtypeStruct((rows, width), bf16)] * blocks,
        in_specs=[vmem] * (8 + 2 * blocks),
        out_specs=[vmem] * (2 + blocks),
        scratch_shapes=[pltpu.VMEM((length, query_cols), bf16), pltpu.VMEM((length, columns), f32)],
        compiler_params=ATTENTION_PARAMS,
        cost_estimate=LARGE_COST,
        name="attention_backward",
    )(*tables, full, factors, qkv, spread, *pieces, *token_blocks)


def attention_gradients(normed, back, pieces, heads):
    blocks = len(pieces)
    rows, width = pieces[0].shape
    columns = back.shape[1]
    both = columns + heads.shape[1]
    places = part_places()
    count = len(places)
    cut = width // count

    def kernel(me_ref, normed_ref, back_ref, heads_ref, *refs):
        keep, give, total = refs[blocks:]
        total[:, :columns] = contract_rows(normed_ref[...], back_ref[...]).astype(bf16)
        piece = jnp.concatenate([ref[...] for ref in refs[:blocks]], axis=0)
        total[:, columns:] = contract_rows(piece, heads_ref[...]).astype(bf16)
        for place in places:
            spot = pl.ds(pl.multiple_of((me_ref[0] ^ place) * cut, cut), cut)
            (give if place % 2 else keep)[place // 2] = total[spot, :]

    vmem = pl.BlockSpec(memory_space=pltpu.VMEM)
    shape = jax.ShapeDtypeStruct((count // 2, cut, both), bf16)
    return pl.pallas_call(
        kernel,
        out_shape=[shape, shape],
        in_specs=[pl.BlockSpec(memory_space=pltpu.SMEM)] + [vmem] * (3 + blocks),
        out_specs=[vmem] * 2,
        scratch_shapes=[pltpu.VMEM((width, both), bf16)],
        compiler_params=ATTENTION_PARAMS,
        cost_estimate=LARGE_COST,
        name="attention_gradients",
    )(own_place(), normed, back, heads, *pieces)


def local(
    tokens,
    first_gain,
    query_weight,
    key_matrix,
    value_matrix,
    out_weight,
    second_gain,
    gate_weight,
    up_weight,
    down_weight,
    routes,
    route_logits,
    cotangent,
):
    groups, many = lax.axis_size("gx"), lax.axis_size("gt")
    me_x, me_w = lax.axis_index("gx"), lax.axis_index("gw")
    own_tokens = tokens[0]
    rows, width = own_tokens.shape
    query_cols = query_weight.shape[1]
    key_cols = key_matrix.shape[1]
    query_heads = query_cols // HEAD_SIZE
    pair_heads = key_cols // HEAD_SIZE
    ratio = query_heads // pair_heads
    experts = gate_weight.shape[0]
    some = experts // 2
    spans = ((0, some), (some, experts - some))

    token_blocks = gather_gx(own_tokens)
    attention = jnp.concatenate(
        [query_weight, key_matrix, value_matrix, out_weight.T], axis=1
    )
    across = swap(attention, "gw", 1)
    along = over_y(attention)
    both = over_y(across)
    down_turned = jnp.swapaxes(down_weight, 1, 2)
    keep, give = halve_weights(gate_weight, up_weight, down_turned)
    attention_parts = [attention, across] + along + both
    attention_mirrors = swap(jnp.stack(attention_parts), "co", 1)
    positions = jnp.concatenate(
        [(me_x ^ s) * rows + jnp.arange(rows, dtype=jnp.int32) for s in range(groups)]
    ).astype(f32)
    half = HEAD_SIZE // 2
    freq = rope_base ** (-(jnp.arange(half, dtype=f32) * 2.0 / HEAD_SIZE))
    angle = positions[:, None] * jnp.tile(freq, 128 // half)[None, :]
    tables = (jnp.cos(angle), jnp.sin(angle), positions[:, None], positions[None, :])
    token_blocks, tables, attention_mirrors, give, keep = tie(
        token_blocks, tables, attention_mirrors, give, keep
    )
    across_w, along_w = swap(give, "gw", 1), over_y(keep)
    mirror_keep = swap(keep, "co", 1)

    logits = route_logits[0].T
    weights = jnp.exp(logits - jnp.max(logits, axis=0, keepdims=True))
    chance = weights / jnp.sum(weights, axis=0, keepdims=True)
    chance_high = lax.reduce_precision(chance, 8, 7)
    routing = jnp.concatenate([routes[0].T.astype(f32), chance_high, chance - chance_high], axis=0)
    routing = jnp.pad(routing.astype(bf16).T, ((0, 0), (0, 128 - 3 * TOPK)))
    payload = jnp.concatenate([cotangent[0], routing], axis=1)
    turned = jnp.stack([w * groups + (me_x ^ s) for w in range(2) for s in range(groups)])
    gathered = lax.all_gather(payload, "gx", axis=0)

    attention_full, normed_one, factor_all, qkv, heads, spread, *branch_parts = attention_forward(
        token_blocks, first_gain, attention_parts, attention_mirrors, tables, query_cols, key_cols
    )

    branch_parts, mirror_keep = tie(branch_parts, mirror_keep)
    branch_got = [swap(branch_parts[s], "gx", s) for s in range(1, groups)]
    across_w, gathered, branch_got = tie(across_w, gathered, branch_got)
    gathered_across = swap(gathered, "gw", 1)
    middle, factor_two, normed_two = norm_forward([branch_parts[0]] + branch_got, own_tokens, second_gain)

    middle_part = experts * 7 // 10
    normed_two, across_w, along_w = tie(normed_two, across_w, along_w)
    normed_parts = gather_gx(normed_two)
    across_rest = across_w[middle_part:]
    both_0 = over_y(across_w[:middle_part])
    turned_parts = {s: swap(normed_parts[s], "gw", 1) for s in (0, 1)}

    gathered = jnp.concatenate([gathered, gathered_across])
    routes_of, slots, _, slots_by, chances_by = route_slots(gathered, turned, me_x * experts, experts, width)
    back_in = gather_slots(gathered, slots, width, order=turned)
    normed_parts, turned_parts[0], turned_parts[1], both_0, across_w, across_rest, along_w, back_in = tie(
        normed_parts, turned_parts[0], turned_parts[1], both_0, across_w, across_rest, along_w, back_in
    )

    rest = [s for s in range(groups) if s not in (0, 1)]
    turned_rest = swap(jnp.concatenate([normed_parts[s] for s in rest]), "gw", 1)
    both_1 = over_y(across_rest)
    mirror_w = [swap(v, "co", 1) for v in [across_w] + along_w]
    mirror_both_0 = [swap(v, "co", 1) for v in both_0]
    normed_rows = normed_parts + [turned_parts[0], turned_parts[1]]
    rows_in = gather_slots(normed_rows, slots, width)
    turned_rest, both_1, rows_in = tie(turned_rest, both_1, rows_in)
    rest_rows = [turned_rest[i * rows : (i + 1) * rows] for i in range(len(rest))]
    rows_in = gather_slots(rest_rows, slots, width, first=len(normed_rows), before=rows_in)
    mirror_both_1 = [swap(v, "co", 1) for v in both_1]
    rows_in, mirror_w, mirror_both_0, mirror_both_1 = tie(rows_in, mirror_w, mirror_both_0, mirror_both_1)

    def halved(boths):
        return [[(first, 0), (second, middle_part)] for first, second in zip(*boths)]

    parts = [[(v, 0)] for v in [keep, across_w] + along_w] + halved((both_0, both_1))
    parts = parts + [[(v, 0)] for v in [mirror_keep] + mirror_w] + halved((mirror_both_0, mirror_both_1))
    rows_back, mixed_parts, chance_parts, gradients, given = [], [], [], [], []
    for i, (start, size) in enumerate(spans):
        if i == 1:
            rows_in, rows_back[0] = tie(rows_in, rows_back[0])
        result = run_experts(rows_in, back_in, parts, start, size, slots_by, chances_by)
        for lot, value in zip((rows_back, mixed_parts, chance_parts, gradients, given), result):
            lot.append(value)

    got = [None, None]

    def joint(i, t, w):
        return gradients[i][2 * t + w].astype(f32) + got[i][2 * t + w].astype(f32)

    others = range(1, many)
    got[0] = swap(given[0], "co", 1)
    got[0], rows_back = tie(got[0], rows_back)
    far = [joint(0, t, 1).astype(bf16) for t in others]
    far, given[1] = tie(far, given[1])
    got[1] = swap(given[1], "co", 1)
    along_one_0 = spread_y(far)
    summed, *turned_sums = sum_slots(rows_back, slots, (groups, groups + 2, 2 * groups))
    pieces = ((2, groups), (0, 2))
    crossed = [swap(turned_sums[1], "gw", 1), swap(turned_sums[0], "gw", 1)]
    far = [joint(1, t, 1).astype(bf16) for t in others]
    mixed_rows, mixed_turned = sum_slots(mixed_parts, slots, (groups, 2 * groups))
    crossed[0], mixed_rows, mixed_turned = tie(crossed[0], mixed_rows, mixed_turned)

    def half_sum(s):
        a, b = pieces[0] if s >= 2 else pieces[1]
        value = crossed[0] if s >= 2 else crossed[1]
        return summed[s].astype(f32) + value[s - a].astype(f32)

    normed_got = {s: swap(half_sum(s).astype(bf16), "gx", s) for s in range(2, groups)}
    along_one_0, far, got[1], crossed[1] = tie(along_one_0, far, got[1], crossed[1])
    along_one_1 = spread_y(far)
    crossed[1], normed_got[3] = tie(crossed[1], normed_got[3])
    normed_got[1] = swap(half_sum(1).astype(bf16), "gx", 1)
    chance_part = jnp.swapaxes(jnp.concatenate(chance_parts, axis=0), 0, 1)
    ids = (me_x * experts + jnp.arange(experts, dtype=jnp.int32)).astype(f32)
    same = routes_of[:, None, :, :] == ids[None, :, None, None]
    chance_rows = jnp.sum(jnp.where(same, chance_part[:, :, None, :], 0.0), axis=1)
    middle_back, branch_back, second_part = norm_backward(
        [summed, crossed[1]] + list(normed_got.values()), middle, factor_two, second_gain, cotangent[0]
    )
    branch_back_blocks = gather_gx(branch_back)
    chance_crossed = swap(chance_rows[groups:], "gw", 1)
    mixed_turned, crossed[1], chance_crossed = tie(mixed_turned, crossed[1], chance_crossed)
    chance_rows = chance_rows[:groups] + chance_crossed
    mixed_crossed = swap(mixed_turned, "gw", 1)
    branch_back_blocks[1], gradients[0], along_one_1, mixed_crossed = tie(
        branch_back_blocks[1], gradients[0], along_one_1, mixed_crossed
    )
    far = [joint(0, t, 0).astype(bf16) for t in others]
    along_zero_0 = spread_y(far)

    def near(i, along):
        total = joint(i, 0, 1)
        for value in along:
            total = total + value.astype(f32)
        return total.astype(bf16)

    near_0, mixed_crossed = tie(near(0, along_one_0), mixed_crossed)
    crossed_0 = swap(near_0, "gw", 1)
    branch_back_blocks[1], got[1] = tie(branch_back_blocks[1], got[1])
    near_1 = near(1, along_one_1)
    far = [joint(1, t, 0).astype(bf16) for t in others]
    mixed_rows = mixed_rows.astype(f32) + mixed_crossed.astype(f32)
    mixed_send = mixed_rows.astype(bf16)
    branch_back_blocks, near_1, far, mixed_send, chance_rows = tie(
        branch_back_blocks, near_1, far, mixed_send, chance_rows
    )
    mixed_got = [swap(mixed_send[s], "gx", s) for s in range(1, groups)]
    far_last, near_last = far, near_1

    back, first_part, *normed_one_parts = attention_backward(
        branch_back_blocks, token_blocks, tables, attention_full, factor_all, qkv, spread, query_cols, key_cols
    )
    back, along_zero_0, crossed_0, far_last, near_last = tie(back, along_zero_0, crossed_0, far_last, near_last)
    along_zero_1 = spread_y(far_last)
    crossed_1 = swap(near_last, "gw", 1)
    keep_gradient, give_gradient = attention_gradients(normed_one, back, branch_back_blocks, heads)
    normed_one_parts, mixed_got, give_gradient = tie(normed_one_parts, mixed_got, give_gradient)
    got_gradient = swap(give_gradient, "co", 1)
    mixed = mixed_rows[0]
    for value in mixed_got:
        mixed = mixed + value.astype(f32)
    output = (middle + residual_factor * mixed).astype(bf16)
    normed_got = [swap(normed_one_parts[s], "gx", s) for s in range(1, groups)]
    gains = jnp.concatenate([first_part, second_part])
    gains = gains + swap(gains, "co", 1)
    total = keep_gradient.astype(f32) + got_gradient.astype(f32)
    cut_at = total.shape[2] // 2
    far_attention = [total[2 * t : 2 * t + 2, :, :cut_at].astype(bf16) for t in others]
    side_attention = total[1::2, :, cut_at:].astype(bf16)
    sums = finish_gradients([gradients[0], got[0]] + along_zero_0, crossed_0, 0, None, experts)
    normed_got, far_attention, side_attention, along_zero_1, gains, sums = tie(
        normed_got, far_attention, side_attention, along_zero_1, gains, sums
    )
    far_attention = spread_y(far_attention)
    side_attention = swap(side_attention, "gw", 1)
    gains_got = others_of(gains, ("gt", "gw"))
    far_attention, side_attention, gains_got, chance_rows = tie(
        far_attention, side_attention, gains_got, chance_rows
    )
    sums = finish_gradients([gradients[1], got[1]] + along_zero_1, crossed_1, some, sums, experts)
    gate_sum, up_sum, down_sum = sums
    for value in gains_got:
        gains = gains + value
    step = groups // 2
    while step:
        gains = gains + swap(gains, "gx", step)
        step = step // 2
    first_half = total[:2, :, :cut_at]
    for value in far_attention:
        first_half = first_half + value.astype(f32)
    second_half = total[0::2, :, cut_at:] + side_attention.astype(f32)
    far_attention = spread_y([second_half[t].astype(bf16) for t in others])
    first_half = first_half[0] + swap(first_half[1].astype(bf16), "gw", 1).astype(f32)
    second_half = second_half[0]
    for value in far_attention:
        second_half = second_half + value.astype(f32)
    attention_sum = jnp.concatenate([first_half, second_half], axis=1)
    tokens_back, _, _ = norm_backward(
        [normed_one_parts[0]] + normed_got, own_tokens, factor_all[:rows], first_gain, middle_back
    )
    while chance_rows.shape[0] > 1:
        step = chance_rows.shape[0] // 2
        chance_rows = chance_rows[:step] + swap(chance_rows[step:], "gx", step)
    chance_back = chance_rows[0]
    logit_back = chance * (chance_back - jnp.sum(chance * chance_back, axis=0, keepdims=True))
    return (
        output[None],
        tokens_back[None],
        gains[0],
        attention_sum[:, :query_cols],
        attention_sum[:, query_cols : query_cols + key_cols],
        attention_sum[:, query_cols + key_cols : query_cols + 2 * key_cols],
        attention_sum[:, query_cols + 2 * key_cols :].T,
        gains[1],
        gate_sum,
        up_sum,
        jnp.swapaxes(down_sum, 1, 2),
        logit_back.T[None],
    )


def solution(mesh):
    groups, others = mesh.shape["gx"], mesh.shape["gy"]
    split = Mesh(mesh.devices.reshape(groups, others // 4, 2, 2), ("gx", "gt", "gw", "co"))
    gy = ("gt", "gw", "co")
    in_specs = (
        P(gy, "gx", None),
        P(),
        P(gy, "gx"),
        P(gy, "gx"),
        P(gy, "gx"),
        P("gx", gy),
        P(),
        P("gx", gy, None),
        P("gx", gy, None),
        P("gx", None, gy),
        P(gy, "gx", None),
        P(gy, "gx", None),
        P(gy, "gx", None),
    )
    out_specs = (
        P(gy, "gx", None),
        P(gy, "gx", None),
        P(),
        P(gy, "gx"),
        P(gy, "gx"),
        P(gy, "gx"),
        P("gx", gy),
        P(),
        P("gx", gy, None),
        P("gx", gy, None),
        P("gx", None, gy),
        P(gy, "gx", None),
    )
    return jax.shard_map(local, mesh=split, in_specs=in_specs, out_specs=out_specs, check_vma=False)
```

```python
import functools

import jax
import jax.numpy as jnp
from jax import lax
from jax.experimental import pallas as pl
from jax.experimental.pallas import tpu as pltpu
from jax.sharding import Mesh, PartitionSpec as P

HEAD_SIZE = 64
EXPERTS = 40
TOPK = 8
CAP = 48

epsilon = 1e-06
rope_base = 10000.0
residual_factor = 0.22
score_factor = 0.015625
masked_value = -1e30

SMALL_COST = pl.CostEstimate(flops=1, bytes_accessed=1, transcendentals=0)
LARGE_COST = pl.CostEstimate(flops=10**10, bytes_accessed=10**8, transcendentals=0)
NORM_COST = pl.CostEstimate(flops=10**7, bytes_accessed=5 * 10**6, transcendentals=0)

f32 = jnp.float32
bf16 = jnp.bfloat16


def swap(value, axis, step):
    count = lax.axis_size(axis)
    return lax.ppermute(value, axis, [(i, i ^ step) for i in range(count)])


def tie(*values):
    return lax.optimization_barrier(values)


def pick(array, index, dim):
    return lax.dynamic_index_in_dim(array, index, dim, keepdims=False)


def rms_factor(rows):
    return lax.rsqrt(jnp.mean(rows * rows, axis=-1, keepdims=True) + epsilon)


def norm_back(rows, factor, gain, upstream):
    scaled = upstream * gain
    inner = jnp.mean(scaled * rows, axis=-1, keepdims=True)
    return factor * scaled - rows * factor * factor * factor * inner


def contract_rows(left, right):
    return lax.dot_general(left, right, (((0,), (0,)), ((), ())), preferred_element_type=f32)


def contract_cols(left, right):
    return lax.dot_general(left, right, (((1,), (1,)), ((), ())), preferred_element_type=f32)


def gather_gx(block):
    return [block] + [swap(block, "gx", s) for s in range(1, lax.axis_size("gx"))]


def over_y(value):
    return [swap(value, "gt", s) for s in range(1, lax.axis_size("gt"))]


def spread_y(values):
    return [swap(value, "gt", s) for s, value in enumerate(values, 1)]


def part_places():
    many = lax.axis_size("gt")
    places = [0, 2] + [4 * s for s in range(1, many)] + [4 * s + 2 for s in range(1, many)]
    return places + [p + 1 for p in places]


def own_place():
    me = (lax.axis_index("gt") * 2 + lax.axis_index("gw")) * 2 + lax.axis_index("co")
    return jnp.full((1,), me, jnp.int32)


def own_side():
    return jnp.full((1,), lax.axis_index("gw"), jnp.int32)


def halve_weights(gate, up, down):
    experts, rows, full = gate.shape
    half = full // 2

    def kernel(side_ref, gate_ref, up_ref, down_ref, keep, give):
        def put(low, out):
            for i, ref in enumerate((gate_ref, up_ref, down_ref)):
                out[0, :, i * half : (i + 1) * half] = ref[0, :, low : low + half]

        @pl.when(side_ref[0] == 0)
        def _():
            put(0, keep)
            put(half, give)

        @pl.when(side_ref[0] != 0)
        def _():
            put(half, keep)
            put(0, give)

    def block(columns):
        return pl.BlockSpec((1, rows, columns), lambda e, *_: (e, 0, 0))

    shape = jax.ShapeDtypeStruct((experts, rows, 3 * half), bf16)
    return pl.pallas_call(
        kernel,
        grid_spec=pltpu.PrefetchScalarGridSpec(
            num_scalar_prefetch=1,
            grid=(experts,),
            in_specs=[block(full)] * 3,
            out_specs=[block(3 * half)] * 2,
        ),
        out_shape=[shape, shape],
        cost_estimate=LARGE_COST,
        name="halve_weights",
    )(own_side(), gate, up, down)


def finish_gradients(summed, crossed, start, before, total_experts):
    experts, rows, columns = crossed.shape
    half = columns // 3
    count = len(summed)
    aliased = 0 if before is None else 3

    def kernel(side_ref, *refs):
        total = 0.0
        for ref in refs[:count]:
            total = total + (ref[0, 0] if len(ref.shape) == 4 else ref[0]).astype(f32)
        other = refs[count][0].astype(f32)

        def put(low, value):
            for i, out in enumerate(refs[count + 1 + aliased :]):
                out[0, :, low : low + half] = value[:, i * half : (i + 1) * half]

        @pl.when(side_ref[0] == 0)
        def _():
            put(0, total)
            put(half, other)

        @pl.when(side_ref[0] != 0)
        def _():
            put(half, total)
            put(0, other)

    def block(columns, first):
        return pl.BlockSpec((1, rows, columns), lambda e, *_: (e + first, 0, 0))

    shape = jax.ShapeDtypeStruct((total_experts, rows, 2 * half), f32)
    return pl.pallas_call(
        kernel,
        grid_spec=pltpu.PrefetchScalarGridSpec(
            num_scalar_prefetch=1,
            grid=(experts,),
            in_specs=[
                pl.BlockSpec((1, 1, rows, columns), lambda e, *_: (0, e, 0, 0)) if v.ndim == 4 else block(columns, 0)
                for v in summed
            ]
            + [block(columns, 0)]
            + [pl.BlockSpec(memory_space=pl.ANY)] * aliased,
            out_specs=[block(2 * half, start)] * 3,
        ),
        out_shape=[shape] * 3,
        input_output_aliases={count + 2 + i: i for i in range(aliased)},
        cost_estimate=LARGE_COST,
        name="finish_gradients",
    )(own_side(), *summed, crossed, *(before or ()))


def others_of(value, axes):
    count = lax.axis_size(axes)
    return [lax.ppermute(value, axes, [(i, i ^ s) for i in range(count)]) for s in range(1, count)]


def norm_forward(branch, tokens, gain):
    rows, width = tokens.shape

    def kernel(gain_ref, tokens_ref, *refs):
        middle_out, factor_out, normed_out = refs[len(branch) :]
        total = refs[0][...].astype(f32)
        for ref in refs[1 : len(branch)]:
            total = total + ref[...].astype(f32)
        middle = tokens_ref[...].astype(f32) + residual_factor * total
        factor = rms_factor(middle)
        middle_out[...] = middle
        factor_out[...] = factor
        normed_out[...] = (middle * factor * gain_ref[...]).astype(bf16)

    vmem = pl.BlockSpec(memory_space=pltpu.VMEM)
    return pl.pallas_call(
        kernel,
        out_shape=[
            jax.ShapeDtypeStruct((rows, width), f32),
            jax.ShapeDtypeStruct((rows, 1), f32),
            jax.ShapeDtypeStruct((rows, width), bf16),
        ],
        in_specs=[vmem] * (2 + len(branch)),
        out_specs=[vmem] * 3,
        cost_estimate=NORM_COST,
        name="norm_forward",
    )(gain[None], tokens, *branch)


def norm_backward(upstreams, rows_of, factor, gain, added):
    rows, width = rows_of.shape

    def kernel(gain_ref, rows_ref, factor_ref, added_ref, *refs):
        rows_back, branch_back, gain_back = refs[len(upstreams) :]
        total = 0.0
        for ref in refs[: len(upstreams)]:
            total = total + (ref[0] if len(ref.shape) == 3 else ref[...]).astype(f32)
        values, factor = rows_ref[...].astype(f32), factor_ref[...]
        back = added_ref[...].astype(f32) + norm_back(values, factor, gain_ref[...], total)
        rows_back[...] = back
        branch_back[...] = (residual_factor * back).astype(bf16)
        gain_back[...] = jnp.sum(total * values * factor, axis=0, keepdims=True)

    def whole(x):
        block = (1,) + x.shape[1:] if len(x.shape) == 3 else x.shape
        zeros = (0,) * len(block)
        return pl.BlockSpec(block, lambda i: zeros)

    operands = [gain[None], rows_of, factor, added] + upstreams
    shapes = [((rows, width), f32), ((rows, width), bf16), ((1, width), f32)]
    shapes = [jax.ShapeDtypeStruct(*shape) for shape in shapes]
    return pl.pallas_call(
        kernel,
        grid=(1,),
        out_shape=shapes,
        in_specs=[whole(x) for x in operands],
        out_specs=[whole(x) for x in shapes],
        cost_estimate=NORM_COST,
        name="norm_backward",
    )(*operands)


def slot_mask(slot_row):
    wanted = lax.broadcasted_iota(jnp.int32, (CAP, slot_row.shape[1]), 0).astype(f32)
    return slot_row == wanted


def route_slots(gathered, order, first_expert, experts, width):
    blocks, tokens = gathered.shape[:2]

    def kernel(order_ref, first_ref, routing_ref, routes_out, slots_out, chances_out, slots_by, chances_by):
        earlier = lax.broadcasted_iota(jnp.int32, (tokens, tokens), 0)
        earlier = (earlier < lax.broadcasted_iota(jnp.int32, (tokens, tokens), 1)).astype(f32).astype(bf16)
        for b in range(blocks):
            routing = routing_ref[order_ref[b]].astype(f32).T
            routes = routing[:TOPK]
            chance = routing[TOPK : 2 * TOPK] + routing[2 * TOPK : 3 * TOPK]
            routes_out[b] = routes
            hits, chosen = [], []
            for e in range(experts):
                same = routes == (first_ref[0] + e).astype(f32)
                hits.append(jnp.sum(jnp.where(same, 1.0, 0.0), axis=0, keepdims=True))
                chosen.append(jnp.sum(jnp.where(same, chance, 0.0), axis=0, keepdims=True))
            hits, chosen = jnp.concatenate(hits, axis=0), jnp.concatenate(chosen, axis=0)
            rank = jnp.dot(hits.astype(bf16), earlier, preferred_element_type=f32)
            slots = jnp.where(hits > 0.0, rank, -1.0)
            slots_out[b] = slots
            chances_out[b] = chosen
            for e in range(experts):
                slots_by[e, b : b + 1, :] = slots[e : e + 1]
                chances_by[e, b : b + 1, :] = chosen[e : e + 1]

    def whole(*shape):
        zeros = (0,) * len(shape)
        return pl.BlockSpec(shape, lambda i, *_: zeros)

    shapes = [(blocks, TOPK, tokens)] + [(blocks, experts, tokens)] * 2 + [(experts, blocks, tokens)] * 2
    return pl.pallas_call(
        kernel,
        grid_spec=pltpu.PrefetchScalarGridSpec(
            num_scalar_prefetch=2,
            grid=(1,),
            in_specs=[pl.BlockSpec((blocks, tokens, 128), lambda i, *_: (0, 0, width // 128))],
            out_specs=[whole(*shape) for shape in shapes],
        ),
        out_shape=[jax.ShapeDtypeStruct(shape, f32) for shape in shapes],
        cost_estimate=SMALL_COST,
        name="route_slots",
    )(order, jnp.full((1,), first_expert, jnp.int32), gathered)


def gather_slots(sources, slots, width, order=None, first=0, before=None):
    blocks, experts, tokens = slots.shape
    listed = order is None
    steps = len(sources) if listed else blocks
    aliased = 0 if before is None else 1

    def find(slots_ref, rows, out_ref):
        mask = jnp.concatenate([slot_mask(slots_ref[0, e : e + 1, :]) for e in range(experts)], axis=0)
        found = jnp.dot(mask.astype(f32).astype(bf16), rows, preferred_element_type=f32)
        out_ref[...] = found.astype(bf16).reshape(experts, 1, CAP, width)

    def kernel_list(order_ref, slots_ref, *refs):
        out_ref, held = refs[steps + aliased :]
        for i in range(steps):

            @pl.when(pl.program_id(0) == i)
            def _(i=i):
                held[...] = refs[i][...]

        find(slots_ref, held[...], out_ref)

    def kernel_array(order_ref, slots_ref, rows_ref, out_ref):
        find(slots_ref, rows_ref[0], out_ref)

    if listed:
        specs = [pl.BlockSpec((tokens, width), lambda b, *_, i=i: (i, 0)) for _, i in sources]
        sources = [source for source, _ in sources]
        specs = specs + [pl.BlockSpec(memory_space=pl.ANY)] * aliased
        scratch = [pltpu.VMEM((tokens, width), bf16)]
        order = jnp.zeros((1,), jnp.int32)
        sources = sources + [before] * aliased
    else:
        specs = [pl.BlockSpec((1, tokens, width), lambda b, order_ref: (order_ref[b], 0, 0))]
        scratch = []
        sources = [sources]
    return pl.pallas_call(
        kernel_list if listed else kernel_array,
        grid_spec=pltpu.PrefetchScalarGridSpec(
            num_scalar_prefetch=1,
            grid=(steps,),
            in_specs=[pl.BlockSpec((1, experts, tokens), lambda b, *_: (b + first, 0, 0))] + specs,
            out_specs=pl.BlockSpec((experts, 1, CAP, width), lambda b, *_: (0, b + first, 0, 0)),
            scratch_shapes=scratch,
        ),
        out_shape=jax.ShapeDtypeStruct((experts, blocks, CAP, width), bf16),
        input_output_aliases={2 + steps: 0} if aliased else {},
        compiler_params=pltpu.CompilerParams(vmem_limit_bytes=60 * 2**20),
        cost_estimate=LARGE_COST,
        name="gather_slots",
    )(order, slots, *sources)


def sum_slots(slot_rows, slots, ends, cost):
    blocks, experts, tokens = slots.shape
    width = slot_rows[0].shape[3]
    starts = [0] + list(ends[:-1])

    def kernel(slots_ref, *refs):
        total, first = None, 0
        for ref in refs[: len(slot_rows)]:
            mine = ref.shape[0]
            mask = jnp.concatenate(
                [slot_mask(slots_ref[0, e : e + 1, :]) for e in range(first, first + mine)], axis=0
            )
            first = first + mine
            part = contract_rows(mask.astype(f32).astype(bf16), ref[...].reshape(mine * CAP, width))
            total = part if total is None else total + part
        total = total.astype(bf16)
        step = pl.program_id(0)
        for start, end, out in zip(starts, ends, refs[len(slot_rows) :]):

            @pl.when((step >= start) & (step < end))
            def _(out=out):
                out[0] = total

    def held(start, end):
        return pl.BlockSpec((1, tokens, width), lambda b: (jnp.clip(b - start, 0, end - start - 1), 0, 0))

    return pl.pallas_call(
        kernel,
        grid=(blocks,),
        in_specs=[pl.BlockSpec((1, experts, tokens), lambda b: (b, 0, 0))]
        + [pl.BlockSpec((r.shape[0], 1, CAP, width), lambda b: (0, b, 0, 0)) for r in slot_rows],
        out_specs=[held(start, end) for start, end in zip(starts, ends)],
        out_shape=[
            jax.ShapeDtypeStruct((end - start, tokens, width), bf16) for start, end in zip(starts, ends)
        ],
        compiler_params=pltpu.CompilerParams(vmem_limit_bytes=60 * 2**20),
        cost_estimate=cost,
        name="sum_slots",
    )(slots, *slot_rows)


def run_experts(rows_in, back_in, weights, start, experts, slots, chances):
    blocks, _, width = rows_in.shape[1:]
    places = part_places()
    tokens = slots.shape[2]
    weights = [
        [(w, first) for w, first in part if first < start + experts and first + w.shape[0] > start]
        for part in weights
    ]
    flat = [piece for part in weights for piece in part]
    cut, half = flat[0][0].shape[1], flat[0][0].shape[2] // 3
    count = len(places)
    total_slots = blocks * CAP

    def kernel(me_ref, rows_ref, back_ref, slots_ref, chances_ref, *refs):
        rows_out, mixed_out, chance_out = refs[len(flat) : len(flat) + 3]
        grads = refs[len(flat) + 3 : len(flat) + 5]
        gu_full, d_full, gu_total, d_total = refs[len(flat) + 5 :]
        spots = [pl.ds(pl.multiple_of((me_ref[0] ^ place) * cut, cut), cut) for place in places]
        expert = start + pl.program_id(0)
        part_refs = iter(refs[: len(flat)])
        for spot, part in zip(spots, weights):
            for w, first in part:
                ref = next(part_refs)

                def put(spot=spot, ref=ref):
                    gu_full[spot, :] = ref[0, :, : 2 * half]
                    d_full[spot, :] = ref[0, :, 2 * half :]

                if len(part) == 1:
                    put()
                else:
                    pl.when((expert >= first) & (expert < first + w.shape[0]))(put)
        rows = rows_ref[0].reshape(total_slots, width)
        back = back_ref[0].reshape(total_slots, width)
        masks = [slot_mask(slots_ref[0, b : b + 1, :]) for b in range(blocks)]
        chance = jnp.concatenate(
            [
                jnp.sum(jnp.where(masks[b], chances_ref[0, b : b + 1, :], 0.0), axis=1, keepdims=True)
                for b in range(blocks)
            ],
            axis=0,
        )
        both = jnp.dot(rows, gu_full[...], preferred_element_type=f32)
        active_back = jnp.dot(back, d_full[...], preferred_element_type=f32) * residual_factor
        gate, upper = both[:, :half], both[:, half:]
        sigma = jax.nn.sigmoid(gate)
        silu = gate * sigma
        active = silu * upper
        chance_back = jnp.sum(active * active_back, axis=1, keepdims=True)
        for b in range(blocks):
            column = chance_back[b * CAP : (b + 1) * CAP]
            chance_out[0, b : b + 1, :] = jnp.sum(jnp.where(masks[b], column, 0.0), axis=0, keepdims=True)
        scaled = (active * chance).astype(bf16)
        active_back = active_back * chance
        gate_back = active_back * upper * (sigma * (1.0 + gate * (1.0 - sigma)))
        upper_back = active_back * silu
        both_back = jnp.concatenate([gate_back.astype(bf16), upper_back.astype(bf16)], axis=1)
        rows_out[0] = contract_cols(both_back, gu_full[...]).astype(bf16).reshape(blocks, CAP, width)
        mixed_out[0] = contract_cols(scaled, d_full[...]).astype(bf16).reshape(blocks, CAP, width)
        gu_total[...] = contract_rows(rows, both_back).astype(bf16)
        d_total[...] = (contract_rows(back, scaled) * residual_factor).astype(bf16)
        for spot, place in zip(spots, places):
            grads[place % 2][place // 2, 0, :, : 2 * half] = gu_total[spot, :]
            grads[place % 2][place // 2, 0, :, 2 * half :] = d_total[spot, :]

    def block(shape, first=0):
        zeros = (0,) * len(shape)
        return pl.BlockSpec((1,) + shape, lambda e, *_: (e + first,) + zeros)

    grad_shape = jax.ShapeDtypeStruct((count // 2, experts, cut, 3 * half), bf16)
    def held(size, first):
        return pl.BlockSpec(
            (1, cut, 3 * half), lambda e, *_: (jnp.clip(e + start - first, 0, size - 1), 0, 0)
        )

    slot_shape = jax.ShapeDtypeStruct((experts, blocks, CAP, width), bf16)
    out = pl.pallas_call(
        kernel,
        grid_spec=pltpu.PrefetchScalarGridSpec(
            num_scalar_prefetch=1,
            grid=(experts,),
            in_specs=[
                block((blocks, CAP, width), start),
                block((blocks, CAP, width), start),
                block((blocks, tokens), start),
                block((blocks, tokens), start),
            ]
            + [held(w.shape[0], first) for w, first in flat],
            out_specs=[block((blocks, CAP, width)), block((blocks, CAP, width)), block((blocks, tokens))]
            + [pl.BlockSpec((count // 2, 1, cut, 3 * half), lambda e, *_: (0, e, 0, 0))] * 2,
            scratch_shapes=[
                pltpu.VMEM((width, 2 * half), bf16),
                pltpu.VMEM((width, half), bf16),
                pltpu.VMEM((width, 2 * half), bf16),
                pltpu.VMEM((width, half), bf16),
            ],
        ),
        out_shape=[slot_shape, slot_shape, jax.ShapeDtypeStruct((experts, blocks, tokens), f32)]
        + [grad_shape] * 2,
        compiler_params=pltpu.CompilerParams(vmem_limit_bytes=60 * 2**20),
        cost_estimate=LARGE_COST,
        name="run_experts",
    )(own_place(), rows_in, back_in, slots, chances, *[w for w, _ in flat])
    return out


ATTENTION_PARAMS = pltpu.CompilerParams(vmem_limit_bytes=60 * 2**20)


def turned_half(x):
    lanes = lax.broadcasted_iota(jnp.int32, x.shape, 1) % HEAD_SIZE
    half = HEAD_SIZE // 2
    return jnp.where(lanes < half, -pltpu.roll(x, 128 - half, 1), pltpu.roll(x, half, 1))


def head(x, h):
    return x[:, h * HEAD_SIZE : (h + 1) * HEAD_SIZE]


def attention_forward(token_blocks, gain, parts, mirrors, tables, query_cols, key_cols):
    blocks = len(token_blocks)
    rows, width = token_blocks[0].shape
    length = rows * blocks
    count = len(parts)
    places = part_places()
    columns = query_cols + 2 * key_cols
    heads = query_cols // HEAD_SIZE
    ratio = query_cols // key_cols
    step = 256

    def kernel(me_ref, gain_ref, cosine_ref, sine_ref, down_ref, along_ref, *refs):
        token_refs, part_refs = refs[:blocks], refs[blocks : blocks + count + 1]
        full, normed, factors, qkv, heads_out, spread = refs[blocks + count + 1 : blocks + count + 7]
        branch = refs[blocks + count + 7 :]
        for i, ref in enumerate(part_refs[:count]):
            full[me_ref[0] ^ places[i]] = ref[...]
            full[me_ref[0] ^ places[count + i]] = part_refs[count][i]
        for s in range(blocks):
            x = token_refs[s][...].astype(f32)
            factor = rms_factor(x)
            span = slice(s * rows, (s + 1) * rows)
            factors[span, :] = factor
            normed[span, :] = (x * factor * gain_ref[...]).astype(bf16)
        weights = full[...].reshape(width, full.shape[2])
        projected = jnp.dot(normed[...], weights[:, :columns], preferred_element_type=f32)
        for g in range((query_cols + key_cols) // 128):
            span = slice(g * 128, (g + 1) * 128)
            x = projected[:, span]
            qkv[:, span] = (x * cosine_ref[...] + turned_half(x) * sine_ref[...]).astype(bf16)
        qkv[:, query_cols + key_cols :] = projected[:, query_cols + key_cols :].astype(bf16)
        for q in range(0, length, step):
            span = slice(q, q + step)
            mixed = []
            mask = along_ref[...] <= down_ref[span, :]
            query = qkv[span, :query_cols]
            for h in range(heads):
                key = head(qkv[:, query_cols : query_cols + key_cols], h // ratio)
                value = head(qkv[:, query_cols + key_cols :], h // ratio)
                scores = jnp.where(mask, contract_cols(head(query, h), key) * score_factor, masked_value)
                top = jnp.max(scores, axis=1, keepdims=True)
                exps = jnp.exp(scores - top)
                total = jnp.sum(exps, axis=1, keepdims=True)
                probs = (exps * (1.0 / total)).astype(bf16)
                mixed.append(jnp.dot(probs, value, preferred_element_type=f32).astype(bf16))
                spread[span, h : h + 1] = top + jnp.log(total)
            heads_out[span, :] = jnp.concatenate(mixed, axis=1)
        for s in range(blocks):
            part = contract_cols(heads_out[s * rows : (s + 1) * rows, :], weights[:, columns:])
            branch[s][...] = part.astype(bf16)

    vmem = pl.BlockSpec(memory_space=pltpu.VMEM)
    return pl.pallas_call(
        kernel,
        out_shape=[
            jax.ShapeDtypeStruct((2 * count,) + parts[0].shape, bf16),
            jax.ShapeDtypeStruct((length, width), bf16),
            jax.ShapeDtypeStruct((length, 1), f32),
            jax.ShapeDtypeStruct((length, columns), bf16),
            jax.ShapeDtypeStruct((length, query_cols), bf16),
            jax.ShapeDtypeStruct((length, heads), f32),
        ]
        + [jax.ShapeDtypeStruct((rows, width), bf16)] * blocks,
        in_specs=[pl.BlockSpec(memory_space=pltpu.SMEM)] + [vmem] * (6 + blocks + count),
        out_specs=[vmem] * (6 + blocks),
        compiler_params=ATTENTION_PARAMS,
        cost_estimate=SMALL_COST,
        name="attention_forward",
    )(own_place(), gain[None], *tables, *token_blocks, *parts, mirrors)


def attention_backward(pieces, token_blocks, tables, full, factors, qkv, spread, query_cols, key_cols):
    blocks = len(pieces)
    rows, width = pieces[0].shape
    length = rows * blocks
    columns = query_cols + 2 * key_cols
    heads = query_cols // HEAD_SIZE
    pairs = key_cols // HEAD_SIZE
    ratio = heads // pairs
    step = 256

    def kernel(cosine_ref, sine_ref, down_ref, along_ref, full_ref, factors_ref, qkv_ref, spread_ref, *refs):
        piece_refs, token_refs = refs[:blocks], refs[blocks : 2 * blocks]
        back, gain_back = refs[2 * blocks : 2 * blocks + 2]
        normed_back = refs[2 * blocks + 2 : 3 * blocks + 2]
        heads_back, turned = refs[3 * blocks + 2 :]
        weights = full_ref[...].reshape(width, full_ref.shape[2])
        for s in range(blocks):
            part = jnp.dot(piece_refs[s][...], weights[:, columns:], preferred_element_type=f32)
            heads_back[s * rows : (s + 1) * rows, :] = part.astype(bf16)
        key_back, value_back = [None] * pairs, [None] * pairs

        def add(total, value):
            return value if total is None else total + value

        for q in range(0, length, step):
            span = slice(q, q + step)
            mask = along_ref[...] <= down_ref[span, :]
            query = qkv_ref[span, :query_cols]
            upper = heads_back[span, :]
            query_back = []
            for h in range(heads):
                g = h // ratio
                key = head(qkv_ref[:, query_cols : query_cols + key_cols], g)
                value = head(qkv_ref[:, query_cols + key_cols :], g)
                query_h, upper_h = head(query, h), head(upper, h)
                scores = jnp.where(mask, contract_cols(query_h, key) * score_factor, masked_value)
                probs = jnp.exp(scores - spread_ref[span, h : h + 1])
                prob_back = contract_cols(upper_h, value)
                inner = jnp.sum(probs * prob_back, axis=1, keepdims=True)
                score_back = (probs * (prob_back - inner)).astype(bf16)
                query_back.append(jnp.dot(score_back, key, preferred_element_type=f32) * score_factor)
                key_back[g] = add(key_back[g], contract_rows(score_back, query_h))
                value_back[g] = add(value_back[g], contract_rows(probs.astype(bf16), upper_h))
            turned[span, :query_cols] = jnp.concatenate(query_back, axis=1)
        turned[:, query_cols:] = jnp.concatenate(
            [k * score_factor for k in key_back] + value_back, axis=1
        )
        for g in range((query_cols + key_cols) // 128):
            span = slice(g * 128, (g + 1) * 128)
            x = turned[:, span]
            back[:, span] = (x * cosine_ref[...] - turned_half(x) * sine_ref[...]).astype(bf16)
        back[:, query_cols + key_cols :] = turned[:, query_cols + key_cols :].astype(bf16)
        total = None
        for s in range(blocks):
            span = slice(s * rows, (s + 1) * rows)
            part = contract_cols(back[span, :], weights[:, :columns])
            normed_back[s][...] = part.astype(bf16)
            scaled = part * (token_refs[s][...].astype(f32) * factors_ref[span, :])
            total = add(total, jnp.sum(scaled, axis=0, keepdims=True))
        gain_back[...] = total

    vmem = pl.BlockSpec(memory_space=pltpu.VMEM)
    return pl.pallas_call(
        kernel,
        out_shape=[
            jax.ShapeDtypeStruct((length, columns), bf16),
            jax.ShapeDtypeStruct((1, width), f32),
        ]
        + [jax.ShapeDtypeStruct((rows, width), bf16)] * blocks,
        in_specs=[vmem] * (8 + 2 * blocks),
        out_specs=[vmem] * (2 + blocks),
        scratch_shapes=[pltpu.VMEM((length, query_cols), bf16), pltpu.VMEM((length, columns), f32)],
        compiler_params=ATTENTION_PARAMS,
        cost_estimate=LARGE_COST,
        name="attention_backward",
    )(*tables, full, factors, qkv, spread, *pieces, *token_blocks)


def attention_gradients(normed, back, pieces, heads):
    blocks = len(pieces)
    rows, width = pieces[0].shape
    columns = back.shape[1]
    both = columns + heads.shape[1]
    places = part_places()
    count = len(places)
    cut = width // count

    def kernel(me_ref, normed_ref, back_ref, heads_ref, *refs):
        keep, give, total = refs[blocks:]
        total[:, :columns] = contract_rows(normed_ref[...], back_ref[...]).astype(bf16)
        piece = jnp.concatenate([ref[...] for ref in refs[:blocks]], axis=0)
        total[:, columns:] = contract_rows(piece, heads_ref[...]).astype(bf16)
        for place in places:
            spot = pl.ds(pl.multiple_of((me_ref[0] ^ place) * cut, cut), cut)
            (give if place % 2 else keep)[place // 2] = total[spot, :]

    vmem = pl.BlockSpec(memory_space=pltpu.VMEM)
    shape = jax.ShapeDtypeStruct((count // 2, cut, both), bf16)
    return pl.pallas_call(
        kernel,
        out_shape=[shape, shape],
        in_specs=[pl.BlockSpec(memory_space=pltpu.SMEM)] + [vmem] * (3 + blocks),
        out_specs=[vmem] * 2,
        scratch_shapes=[pltpu.VMEM((width, both), bf16)],
        compiler_params=ATTENTION_PARAMS,
        cost_estimate=LARGE_COST,
        name="attention_gradients",
    )(own_place(), normed, back, heads, *pieces)


def local(
    tokens,
    first_gain,
    query_weight,
    key_matrix,
    value_matrix,
    out_weight,
    second_gain,
    gate_weight,
    up_weight,
    down_weight,
    routes,
    route_logits,
    cotangent,
):
    groups, many = lax.axis_size("gx"), lax.axis_size("gt")
    me_x, me_w = lax.axis_index("gx"), lax.axis_index("gw")
    own_tokens = tokens[0]
    rows, width = own_tokens.shape
    query_cols = query_weight.shape[1]
    key_cols = key_matrix.shape[1]
    query_heads = query_cols // HEAD_SIZE
    pair_heads = key_cols // HEAD_SIZE
    ratio = query_heads // pair_heads
    experts = gate_weight.shape[0]
    some = experts // 2
    spans = ((0, some), (some, experts - some))

    token_blocks = gather_gx(own_tokens)
    attention = jnp.concatenate(
        [query_weight, key_matrix, value_matrix, out_weight.T], axis=1
    )
    across = swap(attention, "gw", 1)
    along = over_y(attention)
    both = over_y(across)
    down_turned = jnp.swapaxes(down_weight, 1, 2)
    keep, give = halve_weights(gate_weight, up_weight, down_turned)
    attention_parts = [attention, across] + along + both
    attention_mirrors = swap(jnp.stack(attention_parts), "co", 1)
    positions = jnp.concatenate(
        [(me_x ^ s) * rows + jnp.arange(rows, dtype=jnp.int32) for s in range(groups)]
    ).astype(f32)
    half = HEAD_SIZE // 2
    freq = rope_base ** (-(jnp.arange(half, dtype=f32) * 2.0 / HEAD_SIZE))
    angle = positions[:, None] * jnp.tile(freq, 128 // half)[None, :]
    tables = (jnp.cos(angle), jnp.sin(angle), positions[:, None], positions[None, :])
    token_blocks, tables, attention_mirrors, give, keep = tie(
        token_blocks, tables, attention_mirrors, give, keep
    )
    across_w, along_w = swap(give, "gw", 1), over_y(keep)
    mirror_keep = swap(keep, "co", 1)

    logits = route_logits[0].T
    weights = jnp.exp(logits - jnp.max(logits, axis=0, keepdims=True))
    chance = weights / jnp.sum(weights, axis=0, keepdims=True)
    chance_high = lax.reduce_precision(chance, 8, 7)
    routing = jnp.concatenate([routes[0].T.astype(f32), chance_high, chance - chance_high], axis=0)
    routing = jnp.pad(routing.astype(bf16).T, ((0, 0), (0, 128 - 3 * TOPK)))
    payload = jnp.concatenate([cotangent[0], routing], axis=1)
    turned = jnp.stack([w * groups + (me_x ^ s) for w in range(2) for s in range(groups)])
    gathered = lax.all_gather(payload, "gx", axis=0)

    attention_full, normed_one, factor_all, qkv, heads, spread, *branch_parts = attention_forward(
        token_blocks, first_gain, attention_parts, attention_mirrors, tables, query_cols, key_cols
    )

    branch_parts, mirror_keep = tie(branch_parts, mirror_keep)
    branch_got = [swap(branch_parts[s], "gx", s) for s in range(1, groups)]
    across_w, gathered, branch_got = tie(across_w, gathered, branch_got)
    gathered_across = swap(gathered, "gw", 1)
    middle, factor_two, normed_two = norm_forward([branch_parts[0]] + branch_got, own_tokens, second_gain)

    middle_part = experts * 7 // 10
    normed_two, across_w, along_w = tie(normed_two, across_w, along_w)
    normed_parts = gather_gx(normed_two)
    across_rest = across_w[middle_part:]
    both_0 = over_y(across_w[:middle_part])
    turned_parts = {s: swap(normed_parts[s], "gw", 1) for s in (0, 1)}

    gathered = jnp.concatenate([gathered, gathered_across])
    routes_of, slots, _, slots_by, chances_by = route_slots(gathered, turned, me_x * experts, experts, width)
    back_in = gather_slots(gathered, slots, width, order=turned)
    normed_parts, turned_parts[0], turned_parts[1], both_0, across_w, across_rest, along_w, back_in = tie(
        normed_parts, turned_parts[0], turned_parts[1], both_0, across_w, across_rest, along_w, back_in
    )

    rest = [s for s in range(groups) if s not in (0, 1)]
    turned_rest = swap(jnp.concatenate([normed_parts[s] for s in rest]), "gw", 1)
    both_1 = over_y(across_rest)
    mirror_w = [swap(v, "co", 1) for v in [across_w] + along_w]
    mirror_both_0 = [swap(v, "co", 1) for v in both_0]
    normed_rows = normed_parts + [turned_parts[0], turned_parts[1]]
    rows_in = gather_slots([(v, 0) for v in normed_rows], slots, width)
    turned_rest, both_1, rows_in = tie(turned_rest, both_1, rows_in)
    rest_rows = [(turned_rest, i) for i in range(len(rest))]
    rows_in = gather_slots(rest_rows, slots, width, first=len(normed_rows), before=rows_in)
    mirror_both_1 = [swap(v, "co", 1) for v in both_1]
    rows_in, mirror_w, mirror_both_0, mirror_both_1 = tie(rows_in, mirror_w, mirror_both_0, mirror_both_1)

    def halved(boths):
        return [[(first, 0), (second, middle_part)] for first, second in zip(*boths)]

    parts = [[(v, 0)] for v in [keep, across_w] + along_w] + halved((both_0, both_1))
    parts = parts + [[(v, 0)] for v in [mirror_keep] + mirror_w] + halved((mirror_both_0, mirror_both_1))
    rows_back, mixed_parts, chance_parts, gradients, given = [], [], [], [], []
    for i, (start, size) in enumerate(spans):
        if i == 1:
            rows_in, rows_back[0] = tie(rows_in, rows_back[0])
        result = run_experts(rows_in, back_in, parts, start, size, slots_by, chances_by)
        for lot, value in zip((rows_back, mixed_parts, chance_parts, gradients, given), result):
            lot.append(value)

    got = [None, None]

    def joint(i, t, w):
        return gradients[i][2 * t + w].astype(f32) + got[i][2 * t + w].astype(f32)

    others = range(1, many)
    got[0] = swap(given[0], "co", 1)
    got[0], rows_back = tie(got[0], rows_back)
    far = [joint(0, t, 1).astype(bf16) for t in others]
    far, given[1] = tie(far, given[1])
    got[1] = swap(given[1], "co", 1)
    along_one_0 = spread_y(far)
    summed, *turned_sums = sum_slots(rows_back, slots, (groups, groups + 2, 2 * groups), LARGE_COST)
    pieces = ((2, groups), (0, 2))
    crossed = [swap(turned_sums[1], "gw", 1), swap(turned_sums[0], "gw", 1)]
    far = [joint(1, t, 1).astype(bf16) for t in others]
    mixed_rows, mixed_turned = sum_slots(mixed_parts, slots, (groups, 2 * groups), SMALL_COST)
    crossed[0], mixed_rows, mixed_turned = tie(crossed[0], mixed_rows, mixed_turned)

    def half_sum(s):
        a, b = pieces[0] if s >= 2 else pieces[1]
        value = crossed[0] if s >= 2 else crossed[1]
        return summed[s].astype(f32) + value[s - a].astype(f32)

    normed_got = {s: swap(half_sum(s).astype(bf16), "gx", s) for s in range(2, groups)}
    along_one_0, far, got[1], crossed[1] = tie(along_one_0, far, got[1], crossed[1])
    along_one_1 = spread_y(far)
    crossed[1], normed_got[3] = tie(crossed[1], normed_got[3])
    normed_got[1] = swap(half_sum(1).astype(bf16), "gx", 1)
    chance_part = jnp.swapaxes(jnp.concatenate(chance_parts, axis=0), 0, 1)
    ids = (me_x * experts + jnp.arange(experts, dtype=jnp.int32)).astype(f32)
    same = routes_of[:, None, :, :] == ids[None, :, None, None]
    chance_rows = jnp.sum(jnp.where(same, chance_part[:, :, None, :], 0.0), axis=1)
    middle_back, branch_back, second_part = norm_backward(
        [summed, crossed[1]] + list(normed_got.values()), middle, factor_two, second_gain, cotangent[0]
    )
    branch_back_blocks = gather_gx(branch_back)
    chance_crossed = swap(chance_rows[groups:], "gw", 1)
    mixed_turned, crossed[1], chance_crossed = tie(mixed_turned, crossed[1], chance_crossed)
    chance_rows = chance_rows[:groups] + chance_crossed
    mixed_crossed = swap(mixed_turned, "gw", 1)
    branch_back_blocks[1], gradients[0], along_one_1, mixed_crossed = tie(
        branch_back_blocks[1], gradients[0], along_one_1, mixed_crossed
    )
    far = [joint(0, t, 0).astype(bf16) for t in others]
    along_zero_0 = spread_y(far)

    def near(i, along):
        total = joint(i, 0, 1)
        for value in along:
            total = total + value.astype(f32)
        return total.astype(bf16)

    near_0, mixed_crossed = tie(near(0, along_one_0), mixed_crossed)
    crossed_0 = swap(near_0, "gw", 1)
    branch_back_blocks[1], got[1] = tie(branch_back_blocks[1], got[1])
    near_1 = near(1, along_one_1)
    far = [joint(1, t, 0).astype(bf16) for t in others]
    mixed_rows = mixed_rows.astype(f32) + mixed_crossed.astype(f32)
    mixed_send = mixed_rows.astype(bf16)
    branch_back_blocks, near_1, far, mixed_send, chance_rows = tie(
        branch_back_blocks, near_1, far, mixed_send, chance_rows
    )
    mixed_got = [swap(mixed_send[s], "gx", s) for s in range(1, groups)]
    far_last, near_last = far, near_1

    back, first_part, *normed_one_parts = attention_backward(
        branch_back_blocks, token_blocks, tables, attention_full, factor_all, qkv, spread, query_cols, key_cols
    )
    back, along_zero_0, crossed_0, far_last, near_last = tie(back, along_zero_0, crossed_0, far_last, near_last)
    along_zero_1 = spread_y(far_last)
    crossed_1 = swap(near_last, "gw", 1)
    keep_gradient, give_gradient = attention_gradients(normed_one, back, branch_back_blocks, heads)
    normed_one_parts, mixed_got, give_gradient = tie(normed_one_parts, mixed_got, give_gradient)
    got_gradient = swap(give_gradient, "co", 1)
    mixed = mixed_rows[0]
    for value in mixed_got:
        mixed = mixed + value.astype(f32)
    output = (middle + residual_factor * mixed).astype(bf16)
    normed_got = [swap(normed_one_parts[s], "gx", s) for s in range(1, groups)]
    gains = jnp.concatenate([first_part, second_part])
    gains = gains + swap(gains, "co", 1)
    total = keep_gradient.astype(f32) + got_gradient.astype(f32)
    cut_at = total.shape[2] // 2
    far_attention = [total[2 * t : 2 * t + 2, :, :cut_at].astype(bf16) for t in others]
    side_attention = total[1::2, :, cut_at:].astype(bf16)
    sums = finish_gradients([gradients[0], got[0]] + along_zero_0, crossed_0, 0, None, experts)
    normed_got, far_attention, side_attention, along_zero_1, gains, sums = tie(
        normed_got, far_attention, side_attention, along_zero_1, gains, sums
    )
    far_attention = spread_y(far_attention)
    side_attention = swap(side_attention, "gw", 1)
    gains_got = others_of(gains, ("gt", "gw"))
    far_attention, side_attention, gains_got, chance_rows = tie(
        far_attention, side_attention, gains_got, chance_rows
    )
    sums = finish_gradients([gradients[1], got[1]] + along_zero_1, crossed_1, some, sums, experts)
    gate_sum, up_sum, down_sum = sums
    for value in gains_got:
        gains = gains + value
    step = groups // 2
    while step:
        gains = gains + swap(gains, "gx", step)
        step = step // 2
    first_half = total[:2, :, :cut_at]
    for value in far_attention:
        first_half = first_half + value.astype(f32)
    second_half = total[0::2, :, cut_at:] + side_attention.astype(f32)
    far_attention = spread_y([second_half[t].astype(bf16) for t in others])
    first_half = first_half[0] + swap(first_half[1].astype(bf16), "gw", 1).astype(f32)
    second_half = second_half[0]
    for value in far_attention:
        second_half = second_half + value.astype(f32)
    attention_sum = jnp.concatenate([first_half, second_half], axis=1)
    tokens_back, _, _ = norm_backward(
        [normed_one_parts[0]] + normed_got, own_tokens, factor_all[:rows], first_gain, middle_back
    )
    while chance_rows.shape[0] > 1:
        step = chance_rows.shape[0] // 2
        chance_rows = chance_rows[:step] + swap(chance_rows[step:], "gx", step)
    chance_back = chance_rows[0]
    logit_back = chance * (chance_back - jnp.sum(chance * chance_back, axis=0, keepdims=True))
    return (
        output[None],
        tokens_back[None],
        gains[0],
        attention_sum[:, :query_cols],
        attention_sum[:, query_cols : query_cols + key_cols],
        attention_sum[:, query_cols + key_cols : query_cols + 2 * key_cols],
        attention_sum[:, query_cols + 2 * key_cols :].T,
        gains[1],
        gate_sum,
        up_sum,
        jnp.swapaxes(down_sum, 1, 2),
        logit_back.T[None],
    )


def solution(mesh):
    groups, others = mesh.shape["gx"], mesh.shape["gy"]
    split = Mesh(mesh.devices.reshape(groups, others // 4, 2, 2), ("gx", "gt", "gw", "co"))
    gy = ("gt", "gw", "co")
    in_specs = (
        P(gy, "gx", None),
        P(),
        P(gy, "gx"),
        P(gy, "gx"),
        P(gy, "gx"),
        P("gx", gy),
        P(),
        P("gx", gy, None),
        P("gx", gy, None),
        P("gx", None, gy),
        P(gy, "gx", None),
        P(gy, "gx", None),
        P(gy, "gx", None),
    )
    out_specs = (
        P(gy, "gx", None),
        P(gy, "gx", None),
        P(),
        P(gy, "gx"),
        P(gy, "gx"),
        P(gy, "gx"),
        P("gx", gy),
        P(),
        P("gx", gy, None),
        P("gx", gy, None),
        P("gx", None, gy),
        P(gy, "gx", None),
    )
    return jax.shard_map(local, mesh=split, in_specs=in_specs, out_specs=out_specs, check_vma=False)
```

```python
import functools

import jax
import jax.numpy as jnp
from jax import lax
from jax.experimental import pallas as pl
from jax.experimental.pallas import tpu as pltpu
from jax.sharding import Mesh, PartitionSpec as P

HEAD_SIZE = 64
EXPERTS = 40
TOPK = 8
CAP = 48

epsilon = 1e-06
rope_base = 10000.0
residual_factor = 0.22
score_factor = 0.015625
masked_value = -1e30

SMALL_COST = pl.CostEstimate(flops=1, bytes_accessed=1, transcendentals=0)
LARGE_COST = pl.CostEstimate(flops=10**10, bytes_accessed=10**8, transcendentals=0)
NORM_COST = pl.CostEstimate(flops=10**7, bytes_accessed=5 * 10**6, transcendentals=0)

f32 = jnp.float32
bf16 = jnp.bfloat16


def swap(value, axis, step):
    count = lax.axis_size(axis)
    return lax.ppermute(value, axis, [(i, i ^ step) for i in range(count)])


def tie(*values):
    return lax.optimization_barrier(values)


def pick(array, index, dim):
    return lax.dynamic_index_in_dim(array, index, dim, keepdims=False)


def rms_factor(rows):
    return lax.rsqrt(jnp.mean(rows * rows, axis=-1, keepdims=True) + epsilon)


def norm_back(rows, factor, gain, upstream):
    scaled = upstream * gain
    inner = jnp.mean(scaled * rows, axis=-1, keepdims=True)
    return factor * scaled - rows * factor * factor * factor * inner


def contract_rows(left, right):
    return lax.dot_general(left, right, (((0,), (0,)), ((), ())), preferred_element_type=f32)


def contract_cols(left, right):
    return lax.dot_general(left, right, (((1,), (1,)), ((), ())), preferred_element_type=f32)


def gather_gx(block):
    return [block] + [swap(block, "gx", s) for s in range(1, lax.axis_size("gx"))]


def over_y(value):
    return [swap(value, "gt", s) for s in range(1, lax.axis_size("gt"))]


def spread_y(values):
    return [swap(value, "gt", s) for s, value in enumerate(values, 1)]


def part_places():
    many = lax.axis_size("gt")
    places = [0, 2] + [4 * s for s in range(1, many)] + [4 * s + 2 for s in range(1, many)]
    return places + [p + 1 for p in places]


def own_place():
    me = (lax.axis_index("gt") * 2 + lax.axis_index("gw")) * 2 + lax.axis_index("co")
    return jnp.full((1,), me, jnp.int32)


def own_side():
    return jnp.full((1,), lax.axis_index("gw"), jnp.int32)


def halve_weights(gate, up, down):
    experts, rows, full = gate.shape
    half = full // 2

    def kernel(side_ref, gate_ref, up_ref, down_ref, keep, give):
        def put(low, out):
            for i, ref in enumerate((gate_ref, up_ref, down_ref)):
                out[0, :, i * half : (i + 1) * half] = ref[0, :, low : low + half]

        @pl.when(side_ref[0] == 0)
        def _():
            put(0, keep)
            put(half, give)

        @pl.when(side_ref[0] != 0)
        def _():
            put(half, keep)
            put(0, give)

    def block(columns):
        return pl.BlockSpec((1, rows, columns), lambda e, *_: (e, 0, 0))

    shape = jax.ShapeDtypeStruct((experts, rows, 3 * half), bf16)
    return pl.pallas_call(
        kernel,
        grid_spec=pltpu.PrefetchScalarGridSpec(
            num_scalar_prefetch=1,
            grid=(experts,),
            in_specs=[block(full)] * 3,
            out_specs=[block(3 * half)] * 2,
        ),
        out_shape=[shape, shape],
        cost_estimate=LARGE_COST,
        name="halve_weights",
    )(own_side(), gate, up, down)


def finish_gradients(summed, crossed, start, before, total_experts):
    experts, rows, columns = crossed.shape
    half = columns // 3
    count = len(summed)
    aliased = 0 if before is None else 3

    def kernel(side_ref, *refs):
        total = 0.0
        for ref in refs[:count]:
            total = total + (ref[0, 0] if len(ref.shape) == 4 else ref[0]).astype(f32)
        other = refs[count][0].astype(f32)

        def put(low, value):
            for i, out in enumerate(refs[count + 1 + aliased :]):
                out[0, :, low : low + half] = value[:, i * half : (i + 1) * half]

        @pl.when(side_ref[0] == 0)
        def _():
            put(0, total)
            put(half, other)

        @pl.when(side_ref[0] != 0)
        def _():
            put(half, total)
            put(0, other)

    def block(columns, first):
        return pl.BlockSpec((1, rows, columns), lambda e, *_: (e + first, 0, 0))

    shape = jax.ShapeDtypeStruct((total_experts, rows, 2 * half), f32)
    return pl.pallas_call(
        kernel,
        grid_spec=pltpu.PrefetchScalarGridSpec(
            num_scalar_prefetch=1,
            grid=(experts,),
            in_specs=[
                pl.BlockSpec((1, 1, rows, columns), lambda e, *_: (0, e, 0, 0)) if v.ndim == 4 else block(columns, 0)
                for v in summed
            ]
            + [block(columns, 0)]
            + [pl.BlockSpec(memory_space=pl.ANY)] * aliased,
            out_specs=[block(2 * half, start)] * 3,
        ),
        out_shape=[shape] * 3,
        input_output_aliases={count + 2 + i: i for i in range(aliased)},
        cost_estimate=LARGE_COST,
        name="finish_gradients",
    )(own_side(), *summed, crossed, *(before or ()))


def others_of(value, axes):
    count = lax.axis_size(axes)
    return [lax.ppermute(value, axes, [(i, i ^ s) for i in range(count)]) for s in range(1, count)]


def norm_forward(branch, tokens, gain):
    rows, width = tokens.shape

    def kernel(gain_ref, tokens_ref, *refs):
        middle_out, factor_out, normed_out = refs[len(branch) :]
        total = refs[0][...].astype(f32)
        for ref in refs[1 : len(branch)]:
            total = total + ref[...].astype(f32)
        middle = tokens_ref[...].astype(f32) + residual_factor * total
        factor = rms_factor(middle)
        middle_out[...] = middle
        factor_out[...] = factor
        normed_out[...] = (middle * factor * gain_ref[...]).astype(bf16)

    vmem = pl.BlockSpec(memory_space=pltpu.VMEM)
    return pl.pallas_call(
        kernel,
        out_shape=[
            jax.ShapeDtypeStruct((rows, width), f32),
            jax.ShapeDtypeStruct((rows, 1), f32),
            jax.ShapeDtypeStruct((rows, width), bf16),
        ],
        in_specs=[vmem] * (2 + len(branch)),
        out_specs=[vmem] * 3,
        cost_estimate=NORM_COST,
        name="norm_forward",
    )(gain[None], tokens, *branch)


def norm_backward(upstreams, rows_of, factor, gain, added):
    rows, width = rows_of.shape

    def kernel(gain_ref, rows_ref, factor_ref, added_ref, *refs):
        rows_back, branch_back, gain_back = refs[len(upstreams) :]
        total = 0.0
        for ref in refs[: len(upstreams)]:
            total = total + (ref[0] if len(ref.shape) == 3 else ref[...]).astype(f32)
        values, factor = rows_ref[...].astype(f32), factor_ref[...]
        back = added_ref[...].astype(f32) + norm_back(values, factor, gain_ref[...], total)
        rows_back[...] = back
        branch_back[...] = (residual_factor * back).astype(bf16)
        gain_back[...] = jnp.sum(total * values * factor, axis=0, keepdims=True)

    def whole(x):
        block = (1,) + x.shape[1:] if len(x.shape) == 3 else x.shape
        zeros = (0,) * len(block)
        return pl.BlockSpec(block, lambda i: zeros)

    operands = [gain[None], rows_of, factor, added] + upstreams
    shapes = [((rows, width), f32), ((rows, width), bf16), ((1, width), f32)]
    shapes = [jax.ShapeDtypeStruct(*shape) for shape in shapes]
    return pl.pallas_call(
        kernel,
        grid=(1,),
        out_shape=shapes,
        in_specs=[whole(x) for x in operands],
        out_specs=[whole(x) for x in shapes],
        cost_estimate=NORM_COST,
        name="norm_backward",
    )(*operands)


def slot_mask(slot_row):
    wanted = lax.broadcasted_iota(jnp.int32, (CAP, slot_row.shape[1]), 0).astype(f32)
    return slot_row == wanted


def route_slots(gathered, order, first_expert, experts, width):
    blocks, tokens = gathered.shape[:2]

    def kernel(order_ref, first_ref, routing_ref, routes_out, slots_out, chances_out, slots_by, chances_by):
        earlier = lax.broadcasted_iota(jnp.int32, (tokens, tokens), 0)
        earlier = (earlier < lax.broadcasted_iota(jnp.int32, (tokens, tokens), 1)).astype(f32).astype(bf16)
        for b in range(blocks):
            routing = routing_ref[order_ref[b]].astype(f32).T
            routes = routing[:TOPK]
            chance = routing[TOPK : 2 * TOPK] + routing[2 * TOPK : 3 * TOPK]
            routes_out[b] = routes
            hits, chosen = [], []
            for e in range(experts):
                same = routes == (first_ref[0] + e).astype(f32)
                hits.append(jnp.sum(jnp.where(same, 1.0, 0.0), axis=0, keepdims=True))
                chosen.append(jnp.sum(jnp.where(same, chance, 0.0), axis=0, keepdims=True))
            hits, chosen = jnp.concatenate(hits, axis=0), jnp.concatenate(chosen, axis=0)
            rank = jnp.dot(hits.astype(bf16), earlier, preferred_element_type=f32)
            slots = jnp.where(hits > 0.0, rank, -1.0)
            slots_out[b] = slots
            chances_out[b] = chosen
            for e in range(experts):
                slots_by[e, b : b + 1, :] = slots[e : e + 1]
                chances_by[e, b : b + 1, :] = chosen[e : e + 1]

    def whole(*shape):
        zeros = (0,) * len(shape)
        return pl.BlockSpec(shape, lambda i, *_: zeros)

    shapes = [(blocks, TOPK, tokens)] + [(blocks, experts, tokens)] * 2 + [(experts, blocks, tokens)] * 2
    return pl.pallas_call(
        kernel,
        grid_spec=pltpu.PrefetchScalarGridSpec(
            num_scalar_prefetch=2,
            grid=(1,),
            in_specs=[pl.BlockSpec((blocks, tokens, 128), lambda i, *_: (0, 0, width // 128))],
            out_specs=[whole(*shape) for shape in shapes],
        ),
        out_shape=[jax.ShapeDtypeStruct(shape, f32) for shape in shapes],
        cost_estimate=SMALL_COST,
        name="route_slots",
    )(order, jnp.full((1,), first_expert, jnp.int32), gathered)


def gather_slots(sources, slots, width, order=None, first=0, before=None):
    blocks, experts, tokens = slots.shape
    listed = order is None
    steps = len(sources) if listed else blocks
    aliased = 0 if before is None else 1

    def find(slots_ref, rows, out_ref):
        mask = jnp.concatenate([slot_mask(slots_ref[0, e : e + 1, :]) for e in range(experts)], axis=0)
        found = jnp.dot(mask.astype(f32).astype(bf16), rows, preferred_element_type=f32)
        out_ref[...] = found.astype(bf16).reshape(experts, 1, CAP, width)

    def kernel_list(order_ref, slots_ref, *refs):
        out_ref, held = refs[steps + aliased :]
        for i in range(steps):

            @pl.when(pl.program_id(0) == i)
            def _(i=i):
                held[...] = refs[i][...]

        find(slots_ref, held[...], out_ref)

    def kernel_array(order_ref, slots_ref, rows_ref, out_ref):
        find(slots_ref, rows_ref[0], out_ref)

    if listed:
        specs = [pl.BlockSpec((tokens, width), lambda b, *_, i=i: (i, 0)) for _, i in sources]
        sources = [source for source, _ in sources]
        specs = specs + [pl.BlockSpec(memory_space=pl.ANY)] * aliased
        scratch = [pltpu.VMEM((tokens, width), bf16)]
        order = jnp.zeros((1,), jnp.int32)
        sources = sources + [before] * aliased
    else:
        specs = [pl.BlockSpec((1, tokens, width), lambda b, order_ref: (order_ref[b], 0, 0))]
        scratch = []
        sources = [sources]
    return pl.pallas_call(
        kernel_list if listed else kernel_array,
        grid_spec=pltpu.PrefetchScalarGridSpec(
            num_scalar_prefetch=1,
            grid=(steps,),
            in_specs=[pl.BlockSpec((1, experts, tokens), lambda b, *_: (b + first, 0, 0))] + specs,
            out_specs=pl.BlockSpec((experts, 1, CAP, width), lambda b, *_: (0, b + first, 0, 0)),
            scratch_shapes=scratch,
        ),
        out_shape=jax.ShapeDtypeStruct((experts, blocks, CAP, width), bf16),
        input_output_aliases={2 + steps: 0} if aliased else {},
        compiler_params=pltpu.CompilerParams(vmem_limit_bytes=60 * 2**20),
        cost_estimate=LARGE_COST,
        name="gather_slots",
    )(order, slots, *sources)


def sum_slots(slot_rows, slots, ends, cost):
    blocks, experts, tokens = slots.shape
    width = slot_rows[0].shape[3]
    starts = [0] + list(ends[:-1])

    def kernel(slots_ref, *refs):
        total, first = None, 0
        for ref in refs[: len(slot_rows)]:
            mine = ref.shape[0]
            mask = jnp.concatenate(
                [slot_mask(slots_ref[0, e : e + 1, :]) for e in range(first, first + mine)], axis=0
            )
            first = first + mine
            part = contract_rows(mask.astype(f32).astype(bf16), ref[...].reshape(mine * CAP, width))
            total = part if total is None else total + part
        total = total.astype(bf16)
        step = pl.program_id(0)
        for start, end, out in zip(starts, ends, refs[len(slot_rows) :]):

            @pl.when((step >= start) & (step < end))
            def _(out=out):
                out[0] = total

    def held(start, end):
        return pl.BlockSpec((1, tokens, width), lambda b: (jnp.clip(b - start, 0, end - start - 1), 0, 0))

    return pl.pallas_call(
        kernel,
        grid=(blocks,),
        in_specs=[pl.BlockSpec((1, experts, tokens), lambda b: (b, 0, 0))]
        + [pl.BlockSpec((r.shape[0], 1, CAP, width), lambda b: (0, b, 0, 0)) for r in slot_rows],
        out_specs=[held(start, end) for start, end in zip(starts, ends)],
        out_shape=[
            jax.ShapeDtypeStruct((end - start, tokens, width), bf16) for start, end in zip(starts, ends)
        ],
        compiler_params=pltpu.CompilerParams(vmem_limit_bytes=60 * 2**20),
        cost_estimate=cost,
        name="sum_slots",
    )(slots, *slot_rows)


def run_experts(rows_in, back_in, weights, start, experts, slots, chances):
    blocks, _, width = rows_in.shape[1:]
    places = part_places()
    tokens = slots.shape[2]
    weights = [
        [(w, first) for w, first in part if first < start + experts and first + w.shape[0] > start]
        for part in weights
    ]
    flat = [piece for part in weights for piece in part]
    cut, half = flat[0][0].shape[1], flat[0][0].shape[2] // 3
    count = len(places)
    total_slots = blocks * CAP

    def kernel(me_ref, rows_ref, back_ref, slots_ref, chances_ref, *refs):
        rows_out, mixed_out, chance_out = refs[len(flat) : len(flat) + 3]
        grads = refs[len(flat) + 3 : len(flat) + 5]
        gu_full, d_full, gu_total, d_total = refs[len(flat) + 5 :]
        spots = [pl.ds(pl.multiple_of((me_ref[0] ^ place) * cut, cut), cut) for place in places]
        expert = start + pl.program_id(0)
        part_refs = iter(refs[: len(flat)])
        for spot, part in zip(spots, weights):
            for w, first in part:
                ref = next(part_refs)

                def put(spot=spot, ref=ref):
                    gu_full[spot, :] = ref[0, :, : 2 * half]
                    d_full[spot, :] = ref[0, :, 2 * half :]

                if len(part) == 1:
                    put()
                else:
                    pl.when((expert >= first) & (expert < first + w.shape[0]))(put)
        rows = rows_ref[0].reshape(total_slots, width)
        back = back_ref[0].reshape(total_slots, width)
        masks = [slot_mask(slots_ref[0, b : b + 1, :]) for b in range(blocks)]
        chance = jnp.concatenate(
            [
                jnp.sum(jnp.where(masks[b], chances_ref[0, b : b + 1, :], 0.0), axis=1, keepdims=True)
                for b in range(blocks)
            ],
            axis=0,
        )
        both = jnp.dot(rows, gu_full[...], preferred_element_type=f32)
        active_back = jnp.dot(back, d_full[...], preferred_element_type=f32) * residual_factor
        gate, upper = both[:, :half], both[:, half:]
        sigma = jax.nn.sigmoid(gate)
        silu = gate * sigma
        active = silu * upper
        chance_back = jnp.sum(active * active_back, axis=1, keepdims=True)
        for b in range(blocks):
            column = chance_back[b * CAP : (b + 1) * CAP]
            chance_out[0, b : b + 1, :] = jnp.sum(jnp.where(masks[b], column, 0.0), axis=0, keepdims=True)
        scaled = (active * chance).astype(bf16)
        active_back = active_back * chance
        gate_back = active_back * upper * (sigma * (1.0 + gate * (1.0 - sigma)))
        upper_back = active_back * silu
        both_back = jnp.concatenate([gate_back.astype(bf16), upper_back.astype(bf16)], axis=1)
        rows_out[0] = contract_cols(both_back, gu_full[...]).astype(bf16).reshape(blocks, CAP, width)
        mixed_out[0] = contract_cols(scaled, d_full[...]).astype(bf16).reshape(blocks, CAP, width)
        gu_total[...] = contract_rows(rows, both_back).astype(bf16)
        d_total[...] = (contract_rows(back, scaled) * residual_factor).astype(bf16)
        for spot, place in zip(spots, places):
            grads[place % 2][place // 2, 0, :, : 2 * half] = gu_total[spot, :]
            grads[place % 2][place // 2, 0, :, 2 * half :] = d_total[spot, :]

    def block(shape, first=0):
        zeros = (0,) * len(shape)
        return pl.BlockSpec((1,) + shape, lambda e, *_: (e + first,) + zeros)

    grad_shape = jax.ShapeDtypeStruct((count // 2, experts, cut, 3 * half), bf16)
    def held(size, first):
        return pl.BlockSpec(
            (1, cut, 3 * half), lambda e, *_: (jnp.clip(e + start - first, 0, size - 1), 0, 0)
        )

    slot_shape = jax.ShapeDtypeStruct((experts, blocks, CAP, width), bf16)
    out = pl.pallas_call(
        kernel,
        grid_spec=pltpu.PrefetchScalarGridSpec(
            num_scalar_prefetch=1,
            grid=(experts,),
            in_specs=[
                block((blocks, CAP, width), start),
                block((blocks, CAP, width), start),
                block((blocks, tokens), start),
                block((blocks, tokens), start),
            ]
            + [held(w.shape[0], first) for w, first in flat],
            out_specs=[block((blocks, CAP, width)), block((blocks, CAP, width)), block((blocks, tokens))]
            + [pl.BlockSpec((count // 2, 1, cut, 3 * half), lambda e, *_: (0, e, 0, 0))] * 2,
            scratch_shapes=[
                pltpu.VMEM((width, 2 * half), bf16),
                pltpu.VMEM((width, half), bf16),
                pltpu.VMEM((width, 2 * half), bf16),
                pltpu.VMEM((width, half), bf16),
            ],
        ),
        out_shape=[slot_shape, slot_shape, jax.ShapeDtypeStruct((experts, blocks, tokens), f32)]
        + [grad_shape] * 2,
        compiler_params=pltpu.CompilerParams(vmem_limit_bytes=60 * 2**20),
        cost_estimate=LARGE_COST,
        name="run_experts",
    )(own_place(), rows_in, back_in, slots, chances, *[w for w, _ in flat])
    return out


ATTENTION_PARAMS = pltpu.CompilerParams(vmem_limit_bytes=60 * 2**20)


def turned_half(x):
    lanes = lax.broadcasted_iota(jnp.int32, x.shape, 1) % HEAD_SIZE
    half = HEAD_SIZE // 2
    return jnp.where(lanes < half, -pltpu.roll(x, 128 - half, 1), pltpu.roll(x, half, 1))


def head(x, h):
    return x[:, h * HEAD_SIZE : (h + 1) * HEAD_SIZE]


def attention_forward(token_blocks, gain, parts, mirrors, tables, query_cols, key_cols):
    blocks = len(token_blocks)
    rows, width = token_blocks[0].shape
    length = rows * blocks
    count = len(parts)
    places = part_places()
    columns = query_cols + 2 * key_cols
    heads = query_cols // HEAD_SIZE
    ratio = query_cols // key_cols
    step = 256

    def kernel(me_ref, gain_ref, cosine_ref, sine_ref, down_ref, along_ref, *refs):
        token_refs, part_refs = refs[:blocks], refs[blocks : blocks + count + 1]
        full, normed, factors, qkv, heads_out, spread = refs[blocks + count + 1 : blocks + count + 7]
        branch = refs[blocks + count + 7 :]
        for i, ref in enumerate(part_refs[:count]):
            full[me_ref[0] ^ places[i]] = ref[...]
            full[me_ref[0] ^ places[count + i]] = part_refs[count][i]
        for s in range(blocks):
            x = token_refs[s][...].astype(f32)
            factor = rms_factor(x)
            span = slice(s * rows, (s + 1) * rows)
            factors[span, :] = factor
            normed[span, :] = (x * factor * gain_ref[...]).astype(bf16)
        weights = full[...].reshape(width, full.shape[2])
        projected = jnp.dot(normed[...], weights[:, :columns], preferred_element_type=f32)
        for g in range((query_cols + key_cols) // 128):
            span = slice(g * 128, (g + 1) * 128)
            x = projected[:, span]
            qkv[:, span] = (x * cosine_ref[...] + turned_half(x) * sine_ref[...]).astype(bf16)
        qkv[:, query_cols + key_cols :] = projected[:, query_cols + key_cols :].astype(bf16)
        for q in range(0, length, step):
            span = slice(q, q + step)
            mixed = []
            mask = along_ref[...] <= down_ref[span, :]
            query = qkv[span, :query_cols]
            for h in range(heads):
                key = head(qkv[:, query_cols : query_cols + key_cols], h // ratio)
                value = head(qkv[:, query_cols + key_cols :], h // ratio)
                scores = jnp.where(mask, contract_cols(head(query, h), key) * score_factor, masked_value)
                top = jnp.max(scores, axis=1, keepdims=True)
                exps = jnp.exp(scores - top)
                total = jnp.sum(exps, axis=1, keepdims=True)
                probs = (exps * (1.0 / total)).astype(bf16)
                mixed.append(jnp.dot(probs, value, preferred_element_type=f32).astype(bf16))
                spread[span, h : h + 1] = top + jnp.log(total)
            heads_out[span, :] = jnp.concatenate(mixed, axis=1)
        for s in range(blocks):
            part = contract_cols(heads_out[s * rows : (s + 1) * rows, :], weights[:, columns:])
            branch[s][...] = part.astype(bf16)

    vmem = pl.BlockSpec(memory_space=pltpu.VMEM)
    return pl.pallas_call(
        kernel,
        out_shape=[
            jax.ShapeDtypeStruct((2 * count,) + parts[0].shape, bf16),
            jax.ShapeDtypeStruct((length, width), bf16),
            jax.ShapeDtypeStruct((length, 1), f32),
            jax.ShapeDtypeStruct((length, columns), bf16),
            jax.ShapeDtypeStruct((length, query_cols), bf16),
            jax.ShapeDtypeStruct((length, heads), f32),
        ]
        + [jax.ShapeDtypeStruct((rows, width), bf16)] * blocks,
        in_specs=[pl.BlockSpec(memory_space=pltpu.SMEM)] + [vmem] * (6 + blocks + count),
        out_specs=[vmem] * (6 + blocks),
        compiler_params=ATTENTION_PARAMS,
        cost_estimate=SMALL_COST,
        name="attention_forward",
    )(own_place(), gain[None], *tables, *token_blocks, *parts, mirrors)


def attention_backward(pieces, token_blocks, tables, full, factors, qkv, spread, query_cols, key_cols):
    blocks = len(pieces)
    rows, width = pieces[0].shape
    length = rows * blocks
    columns = query_cols + 2 * key_cols
    heads = query_cols // HEAD_SIZE
    pairs = key_cols // HEAD_SIZE
    ratio = heads // pairs
    step = 256

    def kernel(cosine_ref, sine_ref, down_ref, along_ref, full_ref, factors_ref, qkv_ref, spread_ref, *refs):
        piece_refs, token_refs = refs[:blocks], refs[blocks : 2 * blocks]
        back, gain_back = refs[2 * blocks : 2 * blocks + 2]
        normed_back = refs[2 * blocks + 2 : 3 * blocks + 2]
        heads_back, turned = refs[3 * blocks + 2 :]
        weights = full_ref[...].reshape(width, full_ref.shape[2])
        for s in range(blocks):
            part = jnp.dot(piece_refs[s][...], weights[:, columns:], preferred_element_type=f32)
            heads_back[s * rows : (s + 1) * rows, :] = part.astype(bf16)
        key_back, value_back = [None] * pairs, [None] * pairs

        def add(total, value):
            return value if total is None else total + value

        for q in range(0, length, step):
            span = slice(q, q + step)
            mask = along_ref[...] <= down_ref[span, :]
            query = qkv_ref[span, :query_cols]
            upper = heads_back[span, :]
            query_back = []
            for h in range(heads):
                g = h // ratio
                key = head(qkv_ref[:, query_cols : query_cols + key_cols], g)
                value = head(qkv_ref[:, query_cols + key_cols :], g)
                query_h, upper_h = head(query, h), head(upper, h)
                scores = jnp.where(mask, contract_cols(query_h, key) * score_factor, masked_value)
                probs = jnp.exp(scores - spread_ref[span, h : h + 1])
                prob_back = contract_cols(upper_h, value)
                inner = jnp.sum(probs * prob_back, axis=1, keepdims=True)
                score_back = (probs * (prob_back - inner)).astype(bf16)
                query_back.append(jnp.dot(score_back, key, preferred_element_type=f32) * score_factor)
                key_back[g] = add(key_back[g], contract_rows(score_back, query_h))
                value_back[g] = add(value_back[g], contract_rows(probs.astype(bf16), upper_h))
            turned[span, :query_cols] = jnp.concatenate(query_back, axis=1)
        turned[:, query_cols:] = jnp.concatenate(
            [k * score_factor for k in key_back] + value_back, axis=1
        )
        for g in range((query_cols + key_cols) // 128):
            span = slice(g * 128, (g + 1) * 128)
            x = turned[:, span]
            back[:, span] = (x * cosine_ref[...] - turned_half(x) * sine_ref[...]).astype(bf16)
        back[:, query_cols + key_cols :] = turned[:, query_cols + key_cols :].astype(bf16)
        total = None
        for s in range(blocks):
            span = slice(s * rows, (s + 1) * rows)
            part = contract_cols(back[span, :], weights[:, :columns])
            normed_back[s][...] = part.astype(bf16)
            scaled = part * (token_refs[s][...].astype(f32) * factors_ref[span, :])
            total = add(total, jnp.sum(scaled, axis=0, keepdims=True))
        gain_back[...] = total

    vmem = pl.BlockSpec(memory_space=pltpu.VMEM)
    return pl.pallas_call(
        kernel,
        out_shape=[
            jax.ShapeDtypeStruct((length, columns), bf16),
            jax.ShapeDtypeStruct((1, width), f32),
        ]
        + [jax.ShapeDtypeStruct((rows, width), bf16)] * blocks,
        in_specs=[vmem] * (8 + 2 * blocks),
        out_specs=[vmem] * (2 + blocks),
        scratch_shapes=[pltpu.VMEM((length, query_cols), bf16), pltpu.VMEM((length, columns), f32)],
        compiler_params=ATTENTION_PARAMS,
        cost_estimate=LARGE_COST,
        name="attention_backward",
    )(*tables, full, factors, qkv, spread, *pieces, *token_blocks)


def attention_gradients(normed, back, pieces, heads):
    blocks = len(pieces)
    rows, width = pieces[0].shape
    columns = back.shape[1]
    both = columns + heads.shape[1]
    places = part_places()
    count = len(places)
    cut = width // count

    def kernel(me_ref, normed_ref, back_ref, heads_ref, *refs):
        keep, give, total = refs[blocks:]
        total[:, :columns] = contract_rows(normed_ref[...], back_ref[...]).astype(bf16)
        piece = jnp.concatenate([ref[...] for ref in refs[:blocks]], axis=0)
        total[:, columns:] = contract_rows(piece, heads_ref[...]).astype(bf16)
        for place in places:
            spot = pl.ds(pl.multiple_of((me_ref[0] ^ place) * cut, cut), cut)
            (give if place % 2 else keep)[place // 2] = total[spot, :]

    vmem = pl.BlockSpec(memory_space=pltpu.VMEM)
    shape = jax.ShapeDtypeStruct((count // 2, cut, both), bf16)
    return pl.pallas_call(
        kernel,
        out_shape=[shape, shape],
        in_specs=[pl.BlockSpec(memory_space=pltpu.SMEM)] + [vmem] * (3 + blocks),
        out_specs=[vmem] * 2,
        scratch_shapes=[pltpu.VMEM((width, both), bf16)],
        compiler_params=ATTENTION_PARAMS,
        cost_estimate=LARGE_COST,
        name="attention_gradients",
    )(own_place(), normed, back, heads, *pieces)


def local(
    tokens,
    first_gain,
    query_weight,
    key_matrix,
    value_matrix,
    out_weight,
    second_gain,
    gate_weight,
    up_weight,
    down_weight,
    routes,
    route_logits,
    cotangent,
):
    groups, many = lax.axis_size("gx"), lax.axis_size("gt")
    me_x, me_w = lax.axis_index("gx"), lax.axis_index("gw")
    own_tokens = tokens[0]
    rows, width = own_tokens.shape
    query_cols = query_weight.shape[1]
    key_cols = key_matrix.shape[1]
    query_heads = query_cols // HEAD_SIZE
    pair_heads = key_cols // HEAD_SIZE
    ratio = query_heads // pair_heads
    experts = gate_weight.shape[0]
    some = experts // 2
    spans = ((0, some), (some, experts - some))

    token_blocks = gather_gx(own_tokens)
    attention = jnp.concatenate(
        [query_weight, key_matrix, value_matrix, out_weight.T], axis=1
    )
    across = swap(attention, "gw", 1)
    along = over_y(attention)
    both = over_y(across)
    down_turned = jnp.swapaxes(down_weight, 1, 2)
    keep, give = halve_weights(gate_weight, up_weight, down_turned)
    attention_parts = [attention, across] + along + both
    attention_mirrors = swap(jnp.stack(attention_parts), "co", 1)
    positions = jnp.concatenate(
        [(me_x ^ s) * rows + jnp.arange(rows, dtype=jnp.int32) for s in range(groups)]
    ).astype(f32)
    half = HEAD_SIZE // 2
    freq = rope_base ** (-(jnp.arange(half, dtype=f32) * 2.0 / HEAD_SIZE))
    angle = positions[:, None] * jnp.tile(freq, 128 // half)[None, :]
    tables = (jnp.cos(angle), jnp.sin(angle), positions[:, None], positions[None, :])
    token_blocks, tables, attention_mirrors, give, keep = tie(
        token_blocks, tables, attention_mirrors, give, keep
    )
    across_w, along_w = swap(give, "gw", 1), over_y(keep)
    mirror_keep = swap(keep, "co", 1)

    logits = route_logits[0].T
    weights = jnp.exp(logits - jnp.max(logits, axis=0, keepdims=True))
    chance = weights / jnp.sum(weights, axis=0, keepdims=True)
    chance_high = lax.reduce_precision(chance, 8, 7)
    routing = jnp.concatenate([routes[0].T.astype(f32), chance_high, chance - chance_high], axis=0)
    routing = jnp.pad(routing.astype(bf16).T, ((0, 0), (0, 128 - 3 * TOPK)))
    payload = jnp.concatenate([cotangent[0], routing], axis=1)
    turned = jnp.stack([w * groups + (me_x ^ s) for w in range(2) for s in range(groups)])
    gathered = lax.all_gather(payload, "gx", axis=0)

    attention_full, normed_one, factor_all, qkv, heads, spread, *branch_parts = attention_forward(
        token_blocks, first_gain, attention_parts, attention_mirrors, tables, query_cols, key_cols
    )

    branch_parts, mirror_keep = tie(branch_parts, mirror_keep)
    branch_got = [swap(branch_parts[s], "gx", s) for s in range(1, groups)]
    middle_part = experts * 7 // 10
    across_first, across_rest = across_w[:middle_part], across_w[middle_part:]
    across_w, across_first, across_rest, gathered, branch_got = tie(
        across_w, across_first, across_rest, gathered, branch_got
    )
    gathered_across = swap(gathered, "gw", 1)
    middle, factor_two, normed_two = norm_forward([branch_parts[0]] + branch_got, own_tokens, second_gain)

    normed_two, across_w, across_first, along_w = tie(normed_two, across_w, across_first, along_w)
    normed_parts = gather_gx(normed_two)
    both_0 = over_y(across_first)
    turned_parts = {s: swap(normed_parts[s], "gw", 1) for s in (0, 1)}

    gathered = jnp.concatenate([gathered, gathered_across])
    routes_of, slots, _, slots_by, chances_by = route_slots(gathered, turned, me_x * experts, experts, width)
    back_in = gather_slots(gathered, slots, width, order=turned)
    normed_parts, turned_parts[0], turned_parts[1], both_0, across_w, across_rest, along_w, back_in = tie(
        normed_parts, turned_parts[0], turned_parts[1], both_0, across_w, across_rest, along_w, back_in
    )

    rest = [s for s in range(groups) if s not in (0, 1)]
    turned_rest = swap(jnp.concatenate([normed_parts[s] for s in rest]), "gw", 1)
    both_1 = over_y(across_rest)
    mirror_w = [swap(v, "co", 1) for v in [across_w] + along_w]
    mirror_both_0 = [swap(v, "co", 1) for v in both_0]
    normed_rows = normed_parts + [turned_parts[0], turned_parts[1]]
    rows_in = gather_slots([(v, 0) for v in normed_rows], slots, width)
    turned_rest, both_1, rows_in = tie(turned_rest, both_1, rows_in)
    rest_rows = [(turned_rest, i) for i in range(len(rest))]
    rows_in = gather_slots(rest_rows, slots, width, first=len(normed_rows), before=rows_in)
    mirror_both_1 = [swap(v, "co", 1) for v in both_1]
    rows_in, mirror_w, mirror_both_0, mirror_both_1 = tie(rows_in, mirror_w, mirror_both_0, mirror_both_1)

    def halved(boths):
        return [[(first, 0), (second, middle_part)] for first, second in zip(*boths)]

    parts = [[(v, 0)] for v in [keep, across_w] + along_w] + halved((both_0, both_1))
    parts = parts + [[(v, 0)] for v in [mirror_keep] + mirror_w] + halved((mirror_both_0, mirror_both_1))
    rows_back, mixed_parts, chance_parts, gradients, given = [], [], [], [], []
    for i, (start, size) in enumerate(spans):
        if i == 1:
            rows_in, rows_back[0] = tie(rows_in, rows_back[0])
        result = run_experts(rows_in, back_in, parts, start, size, slots_by, chances_by)
        for lot, value in zip((rows_back, mixed_parts, chance_parts, gradients, given), result):
            lot.append(value)

    got = [None, None]

    def joint(i, t, w):
        return gradients[i][2 * t + w].astype(f32) + got[i][2 * t + w].astype(f32)

    others = range(1, many)
    got[0] = swap(given[0], "co", 1)
    got[0], rows_back = tie(got[0], rows_back)
    far = [joint(0, t, 1).astype(bf16) for t in others]
    far, given[1] = tie(far, given[1])
    got[1] = swap(given[1], "co", 1)
    along_one_0 = spread_y(far)
    summed, *turned_sums = sum_slots(rows_back, slots, (groups, groups + 2, 2 * groups), LARGE_COST)
    pieces = ((2, groups), (0, 2))
    crossed = [swap(turned_sums[1], "gw", 1), swap(turned_sums[0], "gw", 1)]
    far = [joint(1, t, 1).astype(bf16) for t in others]
    mixed_rows, mixed_turned = sum_slots(mixed_parts, slots, (groups, 2 * groups), SMALL_COST)
    crossed[0], mixed_rows, mixed_turned = tie(crossed[0], mixed_rows, mixed_turned)

    def half_sum(s):
        a, b = pieces[0] if s >= 2 else pieces[1]
        value = crossed[0] if s >= 2 else crossed[1]
        return summed[s].astype(f32) + value[s - a].astype(f32)

    normed_got = {s: swap(half_sum(s).astype(bf16), "gx", s) for s in range(2, groups)}
    along_one_0, far, got[1], crossed[1] = tie(along_one_0, far, got[1], crossed[1])
    along_one_1 = spread_y(far)
    crossed[1], normed_got[3] = tie(crossed[1], normed_got[3])
    normed_got[1] = swap(half_sum(1).astype(bf16), "gx", 1)
    chance_part = jnp.swapaxes(jnp.concatenate(chance_parts, axis=0), 0, 1)
    ids = (me_x * experts + jnp.arange(experts, dtype=jnp.int32)).astype(f32)
    same = routes_of[:, None, :, :] == ids[None, :, None, None]
    chance_rows = jnp.sum(jnp.where(same, chance_part[:, :, None, :], 0.0), axis=1)
    middle_back, branch_back, second_part = norm_backward(
        [summed, crossed[1]] + list(normed_got.values()), middle, factor_two, second_gain, cotangent[0]
    )
    branch_back_blocks = gather_gx(branch_back)
    chance_crossed = swap(chance_rows[groups:], "gw", 1)
    mixed_turned, crossed[1], chance_crossed = tie(mixed_turned, crossed[1], chance_crossed)
    chance_rows = chance_rows[:groups] + chance_crossed
    mixed_crossed = swap(mixed_turned, "gw", 1)
    branch_back_blocks[1], gradients[0], along_one_1, mixed_crossed = tie(
        branch_back_blocks[1], gradients[0], along_one_1, mixed_crossed
    )
    far = [joint(0, t, 0).astype(bf16) for t in others]
    along_zero_0 = spread_y(far)

    def near(i, along):
        total = joint(i, 0, 1)
        for value in along:
            total = total + value.astype(f32)
        return total.astype(bf16)

    near_0, mixed_crossed = tie(near(0, along_one_0), mixed_crossed)
    crossed_0 = swap(near_0, "gw", 1)
    branch_back_blocks[1], got[1] = tie(branch_back_blocks[1], got[1])
    near_1 = near(1, along_one_1)
    far = [joint(1, t, 0).astype(bf16) for t in others]
    mixed_rows = mixed_rows.astype(f32) + mixed_crossed.astype(f32)
    mixed_send = mixed_rows.astype(bf16)
    branch_back_blocks, near_1, far, mixed_send, chance_rows = tie(
        branch_back_blocks, near_1, far, mixed_send, chance_rows
    )
    mixed_got = [swap(mixed_send[s], "gx", s) for s in range(1, groups)]
    far_last, near_last = far, near_1

    back, first_part, *normed_one_parts = attention_backward(
        branch_back_blocks, token_blocks, tables, attention_full, factor_all, qkv, spread, query_cols, key_cols
    )
    back, along_zero_0, crossed_0, far_last, near_last = tie(back, along_zero_0, crossed_0, far_last, near_last)
    along_zero_1 = spread_y(far_last)
    crossed_1 = swap(near_last, "gw", 1)
    keep_gradient, give_gradient = attention_gradients(normed_one, back, branch_back_blocks, heads)
    normed_one_parts, mixed_got, give_gradient = tie(normed_one_parts, mixed_got, give_gradient)
    got_gradient = swap(give_gradient, "co", 1)
    mixed = mixed_rows[0]
    for value in mixed_got:
        mixed = mixed + value.astype(f32)
    output = (middle + residual_factor * mixed).astype(bf16)
    normed_got = [swap(normed_one_parts[s], "gx", s) for s in range(1, groups)]
    gains = jnp.concatenate([first_part, second_part])
    gains = gains + swap(gains, "co", 1)
    total = keep_gradient.astype(f32) + got_gradient.astype(f32)
    cut_at = total.shape[2] // 2
    far_attention = [total[2 * t : 2 * t + 2, :, :cut_at].astype(bf16) for t in others]
    side_attention = total[1::2, :, cut_at:].astype(bf16)
    sums = finish_gradients([gradients[0], got[0]] + along_zero_0, crossed_0, 0, None, experts)
    normed_got, far_attention, side_attention, along_zero_1, gains, sums = tie(
        normed_got, far_attention, side_attention, along_zero_1, gains, sums
    )
    far_attention = spread_y(far_attention)
    side_attention = swap(side_attention, "gw", 1)
    gains_got = others_of(gains, ("gt", "gw"))
    far_attention, side_attention, gains_got, chance_rows = tie(
        far_attention, side_attention, gains_got, chance_rows
    )
    sums = finish_gradients([gradients[1], got[1]] + along_zero_1, crossed_1, some, sums, experts)
    gate_sum, up_sum, down_sum = sums
    for value in gains_got:
        gains = gains + value
    step = groups // 2
    while step:
        gains = gains + swap(gains, "gx", step)
        step = step // 2
    first_half = total[:2, :, :cut_at]
    for value in far_attention:
        first_half = first_half + value.astype(f32)
    second_half = total[0::2, :, cut_at:] + side_attention.astype(f32)
    far_attention = spread_y([second_half[t].astype(bf16) for t in others])
    first_half = first_half[0] + swap(first_half[1].astype(bf16), "gw", 1).astype(f32)
    second_half = second_half[0]
    for value in far_attention:
        second_half = second_half + value.astype(f32)
    attention_sum = jnp.concatenate([first_half, second_half], axis=1)
    tokens_back, _, _ = norm_backward(
        [normed_one_parts[0]] + normed_got, own_tokens, factor_all[:rows], first_gain, middle_back
    )
    while chance_rows.shape[0] > 1:
        step = chance_rows.shape[0] // 2
        chance_rows = chance_rows[:step] + swap(chance_rows[step:], "gx", step)
    chance_back = chance_rows[0]
    logit_back = chance * (chance_back - jnp.sum(chance * chance_back, axis=0, keepdims=True))
    return (
        output[None],
        tokens_back[None],
        gains[0],
        attention_sum[:, :query_cols],
        attention_sum[:, query_cols : query_cols + key_cols],
        attention_sum[:, query_cols + key_cols : query_cols + 2 * key_cols],
        attention_sum[:, query_cols + 2 * key_cols :].T,
        gains[1],
        gate_sum,
        up_sum,
        jnp.swapaxes(down_sum, 1, 2),
        logit_back.T[None],
    )


def solution(mesh):
    groups, others = mesh.shape["gx"], mesh.shape["gy"]
    split = Mesh(mesh.devices.reshape(groups, others // 4, 2, 2), ("gx", "gt", "gw", "co"))
    gy = ("gt", "gw", "co")
    in_specs = (
        P(gy, "gx", None),
        P(),
        P(gy, "gx"),
        P(gy, "gx"),
        P(gy, "gx"),
        P("gx", gy),
        P(),
        P("gx", gy, None),
        P("gx", gy, None),
        P("gx", None, gy),
        P(gy, "gx", None),
        P(gy, "gx", None),
        P(gy, "gx", None),
    )
    out_specs = (
        P(gy, "gx", None),
        P(gy, "gx", None),
        P(),
        P(gy, "gx"),
        P(gy, "gx"),
        P(gy, "gx"),
        P("gx", gy),
        P(),
        P("gx", gy, None),
        P("gx", gy, None),
        P("gx", None, gy),
        P(gy, "gx", None),
    )
    return jax.shard_map(local, mesh=split, in_specs=in_specs, out_specs=out_specs, check_vma=False)
```
